32 devices in a mesh: dp: 4 (over x, core), seq: 8 (over z, y).
Axes of the slice: x: 2, y: 2, z: 4, core: 2. Of those that a mesh axis runs over, the one named last changes fastest.
Arguments:
- tokens: bfloat16 [6144, 2048], P(('dp', 'seq')), may hold values from -6 to 6
- lengths: int32 [4], P('dp'), may hold values from 768 to 1536, as said below
- cotangent: bfloat16 [6144, 2048], P(('dp', 'seq')), may hold values from -6 to 6
- w_query: bfloat16 [2048, 2048], P('dp', 'seq'), may hold values from -0.125 to 0.125
- w_key: bfloat16 [2048, 2048], P('dp', 'seq'), may hold values from -0.125 to 0.125
- w_value: bfloat16 [2048, 2048], P('dp', 'seq'), may hold values from -0.125 to 0.125
- w_out: bfloat16 [2048, 2048], P('dp', 'seq'), may hold values from -2.5 to 2.5
- w_gate: bfloat16 [2048, 8192], P('dp', 'seq'), may hold values from -0.125 to 0.125
- w_up: bfloat16 [2048, 8192], P('dp', 'seq'), may hold values from -0.125 to 0.125
- w_down: bfloat16 [2048, 8192], P('dp', 'seq'), may hold values from -0.0625 to 0.0625
- gain_attn: bfloat16 [2048], P('dp'), may hold values from 0.099609375 to 1.8984375
- gain_ffn: bfloat16 [2048], P('dp'), may hold values from 0.099609375 to 1.8984375
Outputs:
- output: bfloat16 [6144, 2048], P(('dp', 'seq'))
- grad_tokens: float32 [6144, 2048], P(('dp', 'seq'))
- grad_w_query: float32 [2048, 2048], P('dp', 'seq')
- grad_w_key: float32 [2048, 2048], P('dp', 'seq')
- grad_w_value: float32 [2048, 2048], P('dp', 'seq')
- grad_w_out: float32 [2048, 2048], P('dp', 'seq')
- grad_w_gate: float32 [2048, 8192], P('dp', 'seq')
- grad_w_up: float32 [2048, 8192], P('dp', 'seq')
- grad_w_down: float32 [2048, 8192], P('dp', 'seq')
- grad_gain_attn: float32 [2048], P(('dp', 'seq'))
- grad_gain_ffn: float32 [2048], P(('dp', 'seq'))
The draws below stay inside these ranges and needn't reach their ends.
Inputs may be any that keep to these rules, and one draw needn't show every extreme that they name: `lengths`: each sequence's count of real tokens; at least one sequence is full, 1536.
All inputs are finite; a program needn't handle non-finite values.
Results may differ from the reference program's by a relative error of at most 0.017.
Values may be sent and summed in bfloat16 or wider, within the bound.
A program may use at most 320 MiB of HBM per device.

```python
import math
import jax
import jax.numpy as jnp
from jax import lax

D = 2048
HEADS = 16
HD = 128
FF = 8192
WINDOW = 2048
LEN = 1536
SEQS = 4
TOKENS = 6144


def draw_lengths(key, part):
    drawn_lengths = jax.random.randint(key, (SEQS,), LEN // 2, LEN + 1, dtype=jnp.int32)
    chosen = jax.random.randint(jax.random.fold_in(key, 7), (), 0, SEQS, dtype=jnp.int32)
    return jnp.where(jnp.arange(SEQS, dtype=jnp.int32) == chosen, LEN, drawn_lengths).astype(jnp.int32)


def shard_levels(key, shape, cuts, low, top_value):
    loudness = 1.0
    for dim, shards_of in cuts:
        steps = jax.random.uniform(jax.random.fold_in(jax.random.fold_in(key, 6), dim), (shards_of,), jnp.float32, low / len(cuts), top_value / len(cuts))
        loudness = loudness * jnp.repeat(jnp.exp(steps), shape[dim] // shards_of).reshape((-1,) + (1,) * (len(shape) - 1 - dim))
    return loudness


def noise(rng, shape, width, most, pieces=(), kind=jnp.bfloat16):
    values = jax.random.normal(rng, shape, jnp.float32) * width
    if len(pieces) > 0:
        values = shard_levels(rng, shape, pieces, -0.22, 0.18) * values
    return jnp.clip(values, min=-most, max=most).astype(kind)


def setup_inputs(seed: int = 0) -> dict:
    seeds = jax.random.split(jax.random.key(seed), 13)
    tokens = noise(seeds[0], (TOKENS, D), 1.0, 6.0, ((0, 32),))
    lengths = draw_lengths(jax.random.fold_in(seeds[12], 71), 0)
    cotangent = noise(seeds[2], (TOKENS, D), 1.0, 6.0, ((0, 32),))
    w_query = noise(seeds[3], (D, D), D ** -0.5, 0.125, ((0, 4), (1, 8)))
    w_key = noise(seeds[4], (D, D), D ** -0.5, 0.125, ((0, 4), (1, 8)))
    w_value = noise(seeds[5], (D, D), D ** -0.5, 0.125, ((0, 4), (1, 8)))
    w_out = noise(seeds[6], (D, D), (max(1, 4 * D // min(LEN, WINDOW))) ** -0.5, 2.5, ((0, 4), (1, 8)))
    w_gate = noise(seeds[7], (D, FF), D ** -0.5, 0.125, ((0, 4), (1, 8)))
    w_up = noise(seeds[8], (D, FF), D ** -0.5, 0.125, ((0, 4), (1, 8)))
    w_down = noise(seeds[9], (D, FF), FF ** -0.5, 0.0625, ((0, 4), (1, 8)))
    gain_attn = jnp.clip(1.0 + 0.18 * jax.random.normal(seeds[10], (D,), jnp.float32), 0.099609375, 1.8984375).astype(jnp.bfloat16)
    gain_ffn = jnp.clip(1.0 + 0.18 * jax.random.normal(seeds[11], (D,), jnp.float32), 0.099609375, 1.8984375).astype(jnp.bfloat16)
    return dict(tokens=tokens, lengths=lengths, cotangent=cotangent, w_query=w_query, w_key=w_key, w_value=w_value, w_out=w_out, w_gate=w_gate, w_up=w_up, w_down=w_down, gain_attn=gain_attn, gain_ffn=gain_ffn)


EPSILON = 1e-05
NEGATIVE = -1e+30
HIGHEST = lax.Precision.HIGHEST

@jax.custom_vjp
def low(v):
    return lax.optimization_barrier(v.astype(jnp.bfloat16)).astype(jnp.float32)

@jax.custom_vjp
def low_back(v):
    return v

def low_keep(v):
    return (low(v), None)

def low_pass(kept, grad):
    return (grad,)

def back_keep(v):
    return (v, None)

def back_low(kept, grad):
    return (low(grad),)
low.defvjp(low_keep, low_pass)
low_back.defvjp(back_keep, back_low)

def product(left, right):
    return jnp.dot(left, right, precision=HIGHEST)

def rope_tables(seq_len):
    half_dim = HD // 2
    frequency = jnp.exp(-math.log(10000.0) * jnp.arange(half_dim, dtype=jnp.float32) * (2.0 / HD))
    angles = jnp.arange(seq_len, dtype=jnp.float32)[:, None] * frequency[None, :]
    return (jnp.cos(angles), jnp.sin(angles))

def rotate(values, cos_table, sine_table):
    half_dim = values.shape[-1] // 2
    first_half = values[..., :half_dim]
    second_half = values[..., half_dim:]
    cos_part = cos_table[:, None, :]
    sine_part = sine_table[:, None, :]
    return jnp.concatenate([first_half * cos_part - second_half * sine_part, second_half * cos_part + first_half * sine_part], axis=-1)

def rms_norm(values, gain):
    return values * lax.rsqrt(lax.optimization_barrier(jnp.mean(values * values, axis=-1, keepdims=True)) + EPSILON) * gain

def one_sequence(seq_rows, length, weights):
    query_w, key_w, value_w, out_w, gate_w, up_w, down_w, attn_gain, ffn_gain = weights
    positions = jnp.arange(LEN, dtype=jnp.int32)
    valid_mask = (positions < length).astype(jnp.float32)[:, None]
    normed1 = low(rms_norm(seq_rows, attn_gain))
    query_lin = low_back(product(normed1, query_w)).reshape(LEN, HEADS, HD)
    key_lin = low_back(product(normed1, key_w)).reshape(LEN, HEADS, HD)
    values = low(low_back(product(normed1, value_w))).reshape(LEN, HEADS, HD)
    cos_table, sine_table = rope_tables(LEN)
    queries = low(rotate(query_lin, cos_table, sine_table))
    key_rot = low(rotate(key_lin, cos_table, sine_table))
    block_rows = min(512, LEN)
    score_scale = 1.0 / math.sqrt(HD)

    def attend_block(row_start):
        query_part = lax.dynamic_slice_in_dim(queries, row_start, block_rows, 0)
        scores = jnp.einsum('qhd,khd->hqk', query_part, key_rot, precision=HIGHEST) * score_scale
        scores = low_back(scores)
        query_pos = row_start + jnp.arange(block_rows, dtype=jnp.int32)
        distance = query_pos[:, None] - positions[None, :]
        allowed = (distance >= 0) & (distance < WINDOW) & (positions < length)[None, :]
        scores = jnp.where(allowed[None], scores, NEGATIVE)
        row_max = lax.optimization_barrier(jnp.max(scores, axis=-1, keepdims=True))
        exponent = jnp.exp(scores - row_max)
        probabilities = low(exponent / lax.optimization_barrier(jnp.sum(exponent, axis=-1, keepdims=True)))
        return jnp.einsum('hqk,khd->qhd', probabilities, values, precision=HIGHEST)
    block_starts = jnp.arange(LEN // block_rows, dtype=jnp.int32) * block_rows
    attended = lax.map(jax.checkpoint(attend_block), block_starts).reshape(LEN, D)
    attended = low(low_back(attended))
    attn_branch = low_back(jnp.dot(attended, out_w.T, precision=HIGHEST))
    resid = seq_rows + attn_branch
    normed2 = low(rms_norm(resid, ffn_gain))
    gate_pre = low_back(product(normed2, gate_w))
    up_pre = low_back(product(normed2, up_w))
    activation = low(jax.nn.silu(gate_pre) * up_pre)
    ffn_branch = low_back(jnp.dot(activation, down_w.T, precision=HIGHEST))
    return valid_mask * (resid + ffn_branch)

def reference(tokens, lengths, cotangent, w_query, w_key, w_value, w_out, w_gate, w_up, w_down, gain_attn, gain_ffn):
    floats = tuple((array_in.astype(jnp.float32) for array_in in (tokens, w_query, w_key, w_value, w_out, w_gate, w_up, w_down, gain_attn, gain_ffn)))

    def block_forward(token_rows, *weights):

        def sequence_step(packed):
            seq_rows, length = packed
            return one_sequence(seq_rows, length, weights)
        stacked = lax.map(jax.checkpoint(sequence_step), (token_rows.reshape(SEQS, LEN, D), lengths))
        return stacked.reshape(TOKENS, D)
    output, pullback = jax.vjp(block_forward, *floats)
    gradients = pullback(cotangent.astype(jnp.float32))
    return (output.astype(jnp.bfloat16), gradients[0], gradients[1], gradients[2], gradients[3], gradients[4], gradients[5], gradients[6], gradients[7], gradients[8], gradients[9])
```

```python
import functools
import math

import jax
import jax.numpy as jnp
import numpy as np
from jax import lax
from jax.experimental import pallas as pl
from jax.experimental.pallas import tpu as pltpu
from jax.sharding import PartitionSpec as P

HD = 128
WINDOW = 2048
EPSILON = 1e-05
NEGATIVE = -1e30
LINE = 4
MESH = pl.DeviceIdType.MESH
VMEM_LIMIT = 60 * 1024 * 1024


def ring_index(place, count):
    columns = count // LINE
    column = place // LINE
    level = place % LINE
    odd = column % 2
    return (level + odd * (LINE - 1 - 2 * level)) * columns + column


def ring_place(index, count):
    columns = count // LINE
    level = index // columns
    column = index % columns
    odd = column % 2
    return column * LINE + level + odd * (LINE - 1 - 2 * level)


class Ring:
    def __init__(self, count):
        self.count = count
        self.half = count // 2
        self.index = lax.axis_index("seq")
        self.place = ring_place(self.index, count)
        self.next = (self.shifted(1), self.shifted(-1))

    def shifted(self, offset):
        return ring_index((self.place + offset + self.count) % self.count, self.count)

    def greet(self):
        barrier = pltpu.get_barrier_semaphore()
        for other in self.next:
            pl.semaphore_signal(barrier, inc=1, device_id={"seq": other}, device_id_type=MESH)
        pl.semaphore_wait(barrier, 2)


class RingGather:
    def __init__(self, ring, own, full, send, recv, local, parts=2):
        self.ring, self.own, self.full = ring, own, full
        self.send, self.recv, self.local = send, recv, local
        self.rows = own.shape[0]
        self.parts = parts

    @staticmethod
    def semaphores(count, parts=2):
        shape = (2, count // 2, parts)
        return [pltpu.SemaphoreType.DMA(shape), pltpu.SemaphoreType.DMA(shape), pltpu.SemaphoreType.DMA]

    def part_range(self, way, step):
        if step < self.ring.half - 1:
            return range(self.parts)
        middle = self.parts // 2
        return range(middle) if way == 0 else range(middle, self.parts)

    def copy(self, way, step, part):
        size = self.rows // self.parts
        owner = self.ring.shifted(step if way else -step)
        place = self.full.at[pl.ds(pl.multiple_of(owner * self.rows + part * size, size), size)]
        source = self.own.at[pl.ds(part * size, size)] if step == 0 else place
        return pltpu.make_async_remote_copy(
            src_ref=source,
            dst_ref=place,
            send_sem=self.send.at[way, step, part],
            recv_sem=self.recv.at[way, step, part],
            device_id={"seq": self.ring.next[way]},
            device_id_type=MESH,
        )

    def keep(self):
        place = self.full.at[pl.ds(pl.multiple_of(self.ring.index * self.rows, self.rows), self.rows)]
        return pltpu.make_async_copy(self.own, place, self.local)

    def start(self):
        for part in range(self.parts):
            for way in range(2):
                if part in self.part_range(way, 0):
                    self.copy(way, 0, part).start()
        self.keep().start()

    def advance(self, step):
        for part in range(self.parts):
            for way in range(2):
                if part in self.part_range(way, step - 1):
                    self.copy(way, step - 1, part).wait_recv()
                if step < self.ring.half and part in self.part_range(way, step):
                    self.copy(way, step, part).start()

    def finish(self):
        for step in range(self.ring.half):
            for way in range(2):
                for part in self.part_range(way, step):
                    self.copy(way, step, part).wait_send()
        self.keep().wait()


class RingReduce:
    def __init__(self, ring, own, slots, send, recv, parts=2):
        self.ring, self.own, self.slots = ring, own, slots
        self.send, self.recv = send, recv
        self.rows = slots.shape[2]
        self.parts = parts
        self.size = self.rows // parts

    @staticmethod
    def scratch(count, rows, width, parts=2):
        shape = (2, count // 2, parts)
        return [
            pltpu.VMEM((2, count // 2, rows, width), jnp.bfloat16),
            pltpu.SemaphoreType.DMA(shape),
            pltpu.SemaphoreType.DMA(shape),
        ]

    def part_range(self, way, step):
        if step > 0:
            return range(self.parts)
        middle = self.parts // 2
        return range(middle) if way == 0 else range(middle, self.parts)

    def target(self, way, step):
        left = self.ring.half - step
        return self.ring.shifted(-left if way else left)

    def mine(self, index, part):
        return pl.ds(pl.multiple_of(index * self.rows + part * self.size, self.size), self.size)

    def slot(self, way, step, part):
        return self.slots.at[way, step, pl.ds(part * self.size, self.size)]

    def copy(self, way, step, part):
        if step == 0 or (step == 1 and part not in self.part_range(way, 0)):
            source = self.own.at[self.mine(self.target(way, step), part)]
        else:
            source = self.slot(way, step - 1, part)
        return pltpu.make_async_remote_copy(
            src_ref=source,
            dst_ref=self.slot(way, step, part),
            send_sem=self.send.at[way, step, part],
            recv_sem=self.recv.at[way, step, part],
            device_id={"seq": self.ring.next[way]},
            device_id_type=MESH,
        )

    def start(self):
        for way in range(2):
            for part in self.part_range(way, 0):
                self.copy(way, 0, part).start()

    def advance(self, step):
        order = [(way, part) for part in range(self.parts) for way in range(2)]
        if step == 1:
            for way, part in order:
                if part not in self.part_range(way, 0):
                    self.copy(way, 1, part).start()
        for way, part in order:
            if part in self.part_range(way, step - 1):
                self.copy(way, step - 1, part).wait_recv()
                slot = self.slot(way, step - 1, part)
                mine = self.own[self.mine(self.target(way, step), part), :]
                slot[...] = (slot[...].astype(jnp.float32) + mine.astype(jnp.float32)).astype(slot.dtype)
                self.copy(way, step, part).start()

    def total(self, part):
        last = self.ring.half - 1
        for way in range(2):
            self.copy(way, last, part).wait_recv()
        mine = self.own[self.mine(self.ring.index, part), :].astype(jnp.float32)
        return (
            mine
            + self.slot(0, last, part)[...].astype(jnp.float32)
            + self.slot(1, last, part)[...].astype(jnp.float32)
        )

    def finish(self):
        for step in range(self.ring.half):
            for way in range(2):
                for part in self.part_range(way, step):
                    self.copy(way, step, part).wait_send()


def gather_kernel(count, own, full, *semaphores):
    ring = Ring(count)
    ring.greet()
    gather = RingGather(ring, own, full, *semaphores)
    gather.start()
    for step in range(1, ring.half + 1):
        gather.advance(step)
    gather.finish()


def ring_gather(rows, collective_id):
    count = lax.axis_size("seq")
    any_space = pl.BlockSpec(memory_space=pl.ANY)
    return pl.pallas_call(
        functools.partial(gather_kernel, count),
        out_shape=jax.ShapeDtypeStruct((count * rows.shape[0], rows.shape[1]), rows.dtype),
        in_specs=[any_space],
        out_specs=any_space,
        scratch_shapes=RingGather.semaphores(count),
        compiler_params=pltpu.CompilerParams(collective_id=collective_id, has_side_effects=True),
        cost_estimate=pl.CostEstimate(flops=0, bytes_accessed=200_000_000, transcendentals=0),
    )(rows)


def reduce_kernel(count, partial, total, own, load, *scratch):
    ring = Ring(count)
    loaded = pltpu.make_async_copy(partial, own, load)
    loaded.start()
    ring.greet()
    loaded.wait()
    reduce = RingReduce(ring, own, *scratch)
    reduce.start()
    for step in range(1, ring.half):
        reduce.advance(step)
    for part in range(reduce.parts):
        total[pl.ds(part * reduce.size, reduce.size), :] = reduce.total(part)
    reduce.finish()


def ring_reduce(partial, collective_id):
    count = lax.axis_size("seq")
    rows, width = partial.shape[0] // count, partial.shape[1]
    return pl.pallas_call(
        functools.partial(reduce_kernel, count),
        out_shape=jax.ShapeDtypeStruct((rows, width), jnp.float32),
        in_specs=[pl.BlockSpec(memory_space=pl.ANY)],
        out_specs=pl.BlockSpec(memory_space=pltpu.VMEM),
        scratch_shapes=[
            pltpu.VMEM(partial.shape, partial.dtype),
            pltpu.SemaphoreType.DMA,
            *RingReduce.scratch(count, rows, width),
        ],
        compiler_params=pltpu.CompilerParams(
            collective_id=collective_id, has_side_effects=True, vmem_limit_bytes=VMEM_LIMIT
        ),
        cost_estimate=pl.CostEstimate(flops=0, bytes_accessed=200_000_000, transcendentals=0),
    )(partial)


def rope_tables(seq_len):
    half_dim = HD // 2
    steps = np.arange(half_dim, dtype=np.float32) * np.float32(2.0 / HD)
    frequency = np.exp(np.float32(-math.log(10000.0)) * steps)
    angles = np.arange(seq_len, dtype=np.float32)[:, None] * frequency[None, :]
    cos, sin = np.cos(angles), np.sin(angles)
    return (
        np.concatenate([cos, cos], axis=1).astype(np.float32),
        np.concatenate([-sin, sin], axis=1).astype(np.float32),
    )


def turned(values, cos, sin):
    return values * cos + pltpu.roll(values, HD // 2, 1) * sin


def turned_back(values, cos, sin):
    return values * cos - pltpu.roll(values, HD // 2, 1) * sin


def dot(left, right, left_dim=1, right_dim=0):
    return lax.dot_general(
        left, right, (((left_dim,), (right_dim,)), ((), ())), preferred_element_type=jnp.float32
    )


def softmax_block(queries, keys, start, length):
    rows, count = queries.shape[0], keys.shape[0]
    scores = dot(queries, keys, 1, 1) * (1.0 / math.sqrt(HD))
    query_pos = start + lax.broadcasted_iota(jnp.int32, (rows, count), 0)
    key_pos = lax.broadcasted_iota(jnp.int32, (rows, count), 1)
    allowed = (key_pos <= query_pos) & (key_pos < length)
    if start + rows > WINDOW:
        allowed = allowed & (query_pos - key_pos < WINDOW)
    scores = jnp.where(allowed, scores, NEGATIVE)
    exponent = jnp.exp(scores - jnp.max(scores, axis=-1, keepdims=True))
    return exponent * (1.0 / jnp.sum(exponent, axis=-1, keepdims=True))


def attend_kernel(block, length, queries, keys, values, attended):
    seq_len, width = queries.shape
    limit = length[0]

    def one_head(head, carry):
        lanes = pl.ds(pl.multiple_of(head * HD, HD), HD)
        for start in range(0, seq_len, block):
            rows, upto = pl.ds(start, block), pl.ds(0, start + block)
            probs = softmax_block(queries[rows, lanes], keys[upto, lanes], start, limit)
            out = dot(probs.astype(jnp.bfloat16), values[upto, lanes])
            attended[rows, lanes] = out.astype(jnp.bfloat16)
        return carry

    lax.fori_loop(0, width // HD, one_head, 0)


def attend(length, queries, keys, values):
    vmem = pl.BlockSpec(memory_space=pltpu.VMEM)
    return pl.pallas_call(
        functools.partial(attend_kernel, 256),
        out_shape=jax.ShapeDtypeStruct(queries.shape, jnp.bfloat16),
        in_specs=[pl.BlockSpec(memory_space=pltpu.SMEM)] + [vmem] * 3,
        out_specs=vmem,
        compiler_params=pltpu.CompilerParams(vmem_limit_bytes=VMEM_LIMIT),
        cost_estimate=pl.CostEstimate(flops=8_000_000_000, bytes_accessed=4_000_000, transcendentals=0),
    )(length, queries, keys, values)


def attend_back_kernel(block, length, queries, keys, values, grad_out, cos, sin, out_q, out_k, out_v, sum_k, sum_v):
    seq_len, width = queries.shape
    limit = length[0]
    scale = 1.0 / math.sqrt(HD)

    def one_head(head, carry):
        lanes = pl.ds(pl.multiple_of(head * HD, HD), HD)
        sum_k[...] = jnp.zeros_like(sum_k)
        sum_v[...] = jnp.zeros_like(sum_v)
        for start in range(0, seq_len, block):
            rows, upto = pl.ds(start, block), pl.ds(0, start + block)
            query_part, grad_part = queries[rows, lanes], grad_out[rows, lanes]
            probs = softmax_block(query_part, keys[upto, lanes], start, limit)
            grad_probs = dot(grad_part, values[upto, lanes], 1, 1)
            inner = jnp.sum(probs * grad_probs, axis=-1, keepdims=True)
            grad_scores = (probs * (grad_probs - inner)).astype(jnp.bfloat16)
            sum_v[upto, :] += dot(probs.astype(jnp.bfloat16), grad_part, 0, 0)
            sum_k[upto, :] += dot(grad_scores, query_part, 0, 0)
            grad_query = dot(grad_scores, keys[upto, lanes]) * scale
            out_q[rows, lanes] = turned_back(grad_query, cos[rows, :], sin[rows, :]).astype(jnp.bfloat16)
        out_k[:, lanes] = turned_back(sum_k[...] * scale, cos[...], sin[...]).astype(jnp.bfloat16)
        out_v[:, lanes] = sum_v[...].astype(jnp.bfloat16)
        return carry

    lax.fori_loop(0, width // HD, one_head, 0)


def attend_back(length, queries, keys, values, grad_out, cos, sin):
    vmem = pl.BlockSpec(memory_space=pltpu.VMEM)
    seq_len = queries.shape[0]
    return pl.pallas_call(
        functools.partial(attend_back_kernel, 256),
        out_shape=[jax.ShapeDtypeStruct(queries.shape, jnp.bfloat16)] * 3,
        in_specs=[pl.BlockSpec(memory_space=pltpu.SMEM)] + [vmem] * 6,
        out_specs=[vmem] * 3,
        scratch_shapes=[pltpu.VMEM((seq_len, HD), jnp.float32)] * 2,
        compiler_params=pltpu.CompilerParams(vmem_limit_bytes=VMEM_LIMIT),
        cost_estimate=pl.CostEstimate(flops=20_000_000_000, bytes_accessed=8_000_000, transcendentals=0),
    )(length, queries, keys, values, grad_out, cos, sin)


def norm_factor(values):
    return lax.rsqrt(jnp.mean(values * values, axis=-1, keepdims=True) + EPSILON)


def norm_back(values, factor, gain, grad_normed):
    weighted = grad_normed * gain
    grad_values = factor * (
        weighted - values * factor * factor * jnp.mean(weighted * values, axis=-1, keepdims=True)
    )
    grad_gain = jnp.sum(grad_normed * values * factor, axis=0)
    return (grad_values, grad_gain)


def contract_rows(left, right):
    return lax.dot_general(
        left, right, (((0,), (0,)), ((), ())), preferred_element_type=jnp.float32
    )


def contract_cols(left, right):
    return lax.dot_general(
        left, right, (((1,), (1,)), ((), ())), preferred_element_type=jnp.float32
    )


def body(
    tokens,
    lengths,
    cotangent,
    w_query,
    w_key,
    w_value,
    w_out,
    w_gate,
    w_up,
    w_down,
    gain_attn,
    gain_ffn,
):
    tok_rows = tokens.shape[0]
    seq_len = tok_rows * lax.axis_size("seq")
    head_width = w_query.shape[1]
    heads_here = head_width // HD
    length = lengths[0]
    local_pos = lax.axis_index("seq") * tok_rows + jnp.arange(tok_rows, dtype=jnp.int32)
    valid_mask = (local_pos < length).astype(jnp.float32)[:, None]
    cos_table, sine_table = rope_tables(seq_len)
    cos_heads, sine_heads = np.tile(cos_table, (1, heads_here)), np.tile(sine_table, (1, heads_here))
    query_w, key_w, value_w, out_cols, gate_w, up_w, down_w, attn_gain_low, ffn_gain_low = (
        lax.all_gather(w_query, "dp", axis=0, tiled=True),
        lax.all_gather(w_key, "dp", axis=0, tiled=True),
        lax.all_gather(w_value, "dp", axis=0, tiled=True),
        lax.all_gather(w_out, "dp", axis=0, tiled=True),
        lax.all_gather(w_gate, "dp", axis=0, tiled=True),
        lax.all_gather(w_up, "dp", axis=0, tiled=True),
        lax.all_gather(w_down, "dp", axis=0, tiled=True),
        lax.all_gather(gain_attn, "dp", axis=0, tiled=True),
        lax.all_gather(gain_ffn, "dp", axis=0, tiled=True),
    )
    attn_gain = attn_gain_low.astype(jnp.float32)
    ffn_gain = ffn_gain_low.astype(jnp.float32)
    tok_float = tokens.astype(jnp.float32)
    factor1 = norm_factor(tok_float)
    normed1 = (tok_float * factor1 * attn_gain).astype(jnp.bfloat16)
    full1 = ring_gather(normed1, 1)
    query_lin = jnp.dot(full1, query_w, preferred_element_type=jnp.float32)
    key_lin = jnp.dot(full1, key_w, preferred_element_type=jnp.float32)
    values = jnp.dot(full1, value_w, preferred_element_type=jnp.float32).astype(jnp.bfloat16)

    def rotate(lin):
        halves = lin.reshape(seq_len, heads_here, 2, HD // 2)[:, :, ::-1].reshape(seq_len, head_width)
        return (lin * cos_heads + halves * sine_heads).astype(jnp.bfloat16)

    queries, key_rot = rotate(query_lin), rotate(key_lin)
    attended_heads = attend(lengths, queries, key_rot, values)
    out_full = lax.all_gather(out_cols, "seq", axis=1, tiled=True)
    attended_tok = lax.all_to_all(attended_heads, "seq", split_axis=0, concat_axis=1, tiled=True)
    attn_branch = contract_cols(attended_tok, out_full)
    resid = tok_float + attn_branch
    factor2 = norm_factor(resid)
    normed2 = (resid * factor2 * ffn_gain).astype(jnp.bfloat16)
    full2 = ring_gather(normed2, 2)
    gate_pre = jnp.dot(full2, gate_w, preferred_element_type=jnp.float32)
    up_pre = jnp.dot(full2, up_w, preferred_element_type=jnp.float32)
    sigmoid_gate = jax.nn.sigmoid(gate_pre)
    silu_gate = gate_pre * sigmoid_gate
    activation = (silu_gate * up_pre).astype(jnp.bfloat16)
    ffn_branch = ring_reduce(contract_cols(activation, down_w).astype(jnp.bfloat16), 4)
    output = (valid_mask * (resid + ffn_branch)).astype(jnp.bfloat16)
    grad_sum = valid_mask * cotangent.astype(jnp.float32)
    grad_ffn = grad_sum.astype(jnp.bfloat16)
    grad_full = ring_gather(grad_ffn, 3)
    grad_w_down = contract_rows(grad_full, activation)
    grad_act = jnp.dot(grad_full, down_w, preferred_element_type=jnp.float32)
    grad_gate = (grad_act * up_pre * sigmoid_gate * (1.0 + gate_pre * (1.0 - sigmoid_gate))).astype(
        jnp.bfloat16
    )
    grad_up = (grad_act * silu_gate).astype(jnp.bfloat16)
    grad_w_gate = contract_rows(full2, grad_gate)
    grad_w_up = contract_rows(full2, grad_up)
    grad_normed2 = ring_reduce(
        (contract_cols(grad_gate, gate_w) + contract_cols(grad_up, up_w)).astype(jnp.bfloat16), 5
    )
    grad_norm2, grad_gain_ffn = norm_back(resid, factor2, ffn_gain, grad_normed2)
    grad_resid = grad_sum + grad_norm2
    grad_attn = grad_resid.astype(jnp.bfloat16)
    grad_attended = jnp.dot(grad_attn, out_full, preferred_element_type=jnp.float32).astype(
        jnp.bfloat16
    )
    grad_heads = lax.all_to_all(grad_attended, "seq", split_axis=1, concat_axis=0, tiled=True)
    grad_out_whole = contract_rows(grad_attn, attended_tok)
    grad_w_out = lax.psum_scatter(
        grad_out_whole.astype(jnp.bfloat16), "seq", scatter_dimension=1, tiled=True
    )
    grad_query_lin, grad_key_lin, grad_value_lin = attend_back(
        lengths, queries, key_rot, values, grad_heads, cos_table, sine_table
    )
    grad_w_query = contract_rows(full1, grad_query_lin)
    grad_w_key = contract_rows(full1, grad_key_lin)
    grad_w_value = contract_rows(full1, grad_value_lin)
    grad_normed1 = ring_reduce(
        (
            contract_cols(grad_query_lin, query_w)
            + contract_cols(grad_key_lin, key_w)
            + contract_cols(grad_value_lin, value_w)
        ).astype(jnp.bfloat16),
        6,
    )
    grad_norm1, grad_gain_attn = norm_back(tok_float, factor1, attn_gain, grad_normed1)
    grad_tokens = grad_resid + grad_norm1
    owned_query, owned_key, owned_value, owned_out, owned_gate, owned_up, owned_down = (
        lax.psum_scatter(
            grad_w_query.astype(jnp.bfloat16), "dp", scatter_dimension=0, tiled=True
        ).astype(jnp.float32),
        lax.psum_scatter(
            grad_w_key.astype(jnp.bfloat16), "dp", scatter_dimension=0, tiled=True
        ).astype(jnp.float32),
        lax.psum_scatter(
            grad_w_value.astype(jnp.bfloat16), "dp", scatter_dimension=0, tiled=True
        ).astype(jnp.float32),
        lax.psum_scatter(grad_w_out, "dp", scatter_dimension=0, tiled=True).astype(jnp.float32),
        lax.psum_scatter(
            grad_w_gate.astype(jnp.bfloat16), "dp", scatter_dimension=0, tiled=True
        ).astype(jnp.float32),
        lax.psum_scatter(
            grad_w_up.astype(jnp.bfloat16), "dp", scatter_dimension=0, tiled=True
        ).astype(jnp.float32),
        lax.psum_scatter(
            grad_w_down.astype(jnp.bfloat16), "dp", scatter_dimension=0, tiled=True
        ).astype(jnp.float32),
    )
    owned_gain_attn, owned_gain_ffn = (
        lax.psum_scatter(grad_gain_attn, ("dp", "seq"), scatter_dimension=0, tiled=True),
        lax.psum_scatter(grad_gain_ffn, ("dp", "seq"), scatter_dimension=0, tiled=True),
    )
    return (
        output,
        grad_tokens,
        owned_query,
        owned_key,
        owned_value,
        owned_out,
        owned_gate,
        owned_up,
        owned_down,
        owned_gain_attn,
        owned_gain_ffn,
    )


def solution(mesh):
    placed = (
        P(("dp", "seq"), None),
        P("dp"),
        P(("dp", "seq"), None),
        P("dp", "seq"),
        P("dp", "seq"),
        P("dp", "seq"),
        P("dp", "seq"),
        P("dp", "seq"),
        P("dp", "seq"),
        P("dp", "seq"),
        P("dp"),
        P("dp"),
    )
    return jax.shard_map(
        body,
        mesh=mesh,
        in_specs=placed,
        out_specs=(
            P(("dp", "seq"), None),
            P(("dp", "seq"), None),
            P("dp", "seq"),
            P("dp", "seq"),
            P("dp", "seq"),
            P("dp", "seq"),
            P("dp", "seq"),
            P("dp", "seq"),
            P("dp", "seq"),
            P(("dp", "seq")),
            P(("dp", "seq")),
        ),
        check_vma=False,
    )
```

```python
import functools
import math

import jax
import jax.numpy as jnp
import numpy as np
from jax import lax
from jax.experimental import pallas as pl
from jax.experimental.pallas import tpu as pltpu
from jax.sharding import PartitionSpec as P

HD = 128
WINDOW = 2048
EPSILON = 1e-05
NEGATIVE = -1e30
LINE = 4
CORES = 2
PARTS = 2
MESH = pl.DeviceIdType.MESH
VMEM_LIMIT = 60 * 1024 * 1024

ANY = pl.BlockSpec(memory_space=pl.ANY)
VMEM = pl.BlockSpec(memory_space=pltpu.VMEM)
SMEM = pl.BlockSpec(memory_space=pltpu.SMEM)
low = jnp.bfloat16
full = jnp.float32


def shape_of(shape, dtype):
    return jax.ShapeDtypeStruct(shape, dtype)


def span(start, size):
    if isinstance(start, int):
        return pl.ds(start, size)
    return pl.ds(pl.multiple_of(start, size), size)


def dot(left, right, left_dim=1, right_dim=0):
    return lax.dot_general(
        left, right, (((left_dim,), (right_dim,)), ((), ())), preferred_element_type=jnp.float32
    )


def greet(targets):
    barrier = pltpu.get_barrier_semaphore()
    for target in targets:
        pl.semaphore_signal(barrier, inc=1, device_id=target, device_id_type=MESH)
    pl.semaphore_wait(barrier, len(targets))


def send_to(target, source, place, send, recv):
    return pltpu.make_async_remote_copy(
        src_ref=source, dst_ref=place, send_sem=send, recv_sem=recv, device_id=target, device_id_type=MESH
    )


def weave(tasks, events):
    done = 0
    for number, task in enumerate(tasks):
        task()
        upto = (number + 1) * len(events) // len(tasks)
        for event in events[done:upto]:
            event()
        done = upto


def ring_index(place, count):
    columns = count // LINE
    column = place // LINE
    level = place % LINE
    odd = column % 2
    return (level + odd * (LINE - 1 - 2 * level)) * columns + column


def ring_place(index, count):
    columns = count // LINE
    level = index // columns
    column = index % columns
    odd = column % 2
    return column * LINE + level + odd * (LINE - 1 - 2 * level)


class Ring:
    def __init__(self, count):
        self.count = count
        self.half = count // 2
        self.index = lax.axis_index("seq")
        self.place = ring_place(self.index, count)
        self.next = ({"seq": self.shifted(1)}, {"seq": self.shifted(-1)})

    def shifted(self, offset):
        return ring_index((self.place + offset + self.count) % self.count, self.count)


def ring_semaphores(count):
    return [pltpu.SemaphoreType.DMA((2, count // 2, PARTS))] * 2


class RingGather:
    def __init__(self, ring, source, place, send, recv):
        self.ring, self.source, self.place = ring, source, place
        self.send, self.recv = send, recv

    def pieces(self, way, step):
        if step < self.ring.half - 1:
            return range(PARTS)
        return range(PARTS // 2) if way == 0 else range(PARTS // 2, PARTS)

    def copy(self, way, step, part):
        place = self.place(self.ring.shifted(step if way else -step), part)
        return send_to(
            self.ring.next[way],
            self.source(part) if step == 0 else place,
            place,
            self.send.at[way, step, part],
            self.recv.at[way, step, part],
        )

    def start(self):
        for part in range(PARTS):
            for way in range(2):
                if part in self.pieces(way, 0):
                    self.copy(way, 0, part).start()

    def advance(self, step):
        for part in range(PARTS):
            for way in range(2):
                if part in self.pieces(way, step - 1):
                    self.copy(way, step - 1, part).wait_recv()
                if step < self.ring.half and part in self.pieces(way, step):
                    self.copy(way, step, part).start()

    def finish(self):
        for step in range(self.ring.half):
            for way in range(2):
                for part in self.pieces(way, step):
                    self.copy(way, step, part).wait_send()

    def steps(self):
        return [functools.partial(self.advance, step) for step in range(1, self.ring.half + 1)]


class RingReduce:
    def __init__(self, ring, mine, slots, terms, send, recv, load):
        self.ring, self.mine, self.slots, self.terms = ring, mine, slots, terms
        self.send, self.recv, self.load = send, recv, load
        self.size = slots.shape[2] // PARTS

    @staticmethod
    def scratch(count, rows, width):
        return [
            pltpu.VMEM((2, count // 2, rows, width), low),
            pltpu.VMEM((2, 2, rows, width), low),
            *ring_semaphores(count),
            pltpu.SemaphoreType.DMA((2, 2, PARTS)),
        ]

    def pieces(self, way, step):
        if step > 0:
            return range(PARTS)
        return range(PARTS // 2) if way == 0 else range(PARTS // 2, PARTS)

    def summed(self, way, step):
        return self.pieces(way, 0) if step == 1 else range(PARTS)

    def target(self, way, step):
        left = self.ring.half - step
        return self.ring.shifted(-left if way else left)

    def slot(self, way, step, part):
        return self.slots.at[way, step, pl.ds(part * self.size, self.size)]

    def term(self, way, step, part):
        return self.terms.at[step % 2, way, pl.ds(part * self.size, self.size)]

    def fetch(self, way, step, part):
        return pltpu.make_async_copy(
            self.mine(self.target(way, step), part), self.term(way, step, part), self.load.at[step % 2, way, part]
        )

    def fetch_all(self, step):
        for part in range(PARTS):
            for way in range(2 if step < self.ring.half else 1):
                if part in self.summed(way, step):
                    self.fetch(way, step, part).start()

    def copy(self, way, step, part):
        alone = step == 0 or part not in self.summed(way, step)
        source = self.mine(self.target(way, step), part) if alone else self.slot(way, step - 1, part)
        return send_to(
            self.ring.next[way],
            source,
            self.slot(way, step, part),
            self.send.at[way, step, part],
            self.recv.at[way, step, part],
        )

    def start(self):
        for way in range(2):
            for part in self.pieces(way, 0):
                self.copy(way, 0, part).start()
        self.fetch_all(1)

    def advance(self, step):
        self.fetch_all(step + 1)
        order = [(way, part) for part in range(PARTS) for way in range(2)]
        for way, part in order:
            if part not in self.summed(way, step):
                self.copy(way, step, part).start()
        for way, part in order:
            if part in self.summed(way, step):
                self.fetch(way, step, part).wait()
                self.copy(way, step - 1, part).wait_recv()
                slot = self.slot(way, step - 1, part)
                total = slot[...].astype(full) + self.term(way, step, part)[...].astype(full)
                slot[...] = total.astype(slot.dtype)
                self.copy(way, step, part).start()

    def steps(self):
        return [functools.partial(self.advance, step) for step in range(1, self.ring.half)]

    def total(self, part):
        last = self.ring.half - 1
        self.fetch(0, last + 1, part).wait()
        for way in range(2):
            self.copy(way, last, part).wait_recv()
        return (
            self.term(0, last + 1, part)[...].astype(full)
            + self.slot(0, last, part)[...].astype(full)
            + self.slot(1, last, part)[...].astype(full)
        )

    def finish(self):
        for step in range(self.ring.half):
            for way in range(2):
                for part in self.pieces(way, step):
                    self.copy(way, step, part).wait_send()


def row_piece(ref, rows):
    size = rows // PARTS
    return lambda index, part: ref.at[span(index * rows + part * size, size)]


class Shards:
    def __init__(self, count):
        self.count = count
        self.chips = count // CORES
        self.index = lax.axis_index("dp")
        self.chip = self.index // CORES
        self.core = self.index % CORES
        self.sibling = {"dp": self.chip * CORES + 1 - self.core}

    def chip_at(self, offset):
        return (self.chip + offset) % self.chips

    def device(self, chip, core):
        return chip * CORES + core

    def others(self):
        return [{"dp": (self.index + offset) % self.count} for offset in range(1, self.count)]

    def greeted(self):
        return [self.sibling] + [
            {"dp": self.device(self.chip_at(offset), self.core)} for offset in range(1, self.chips)
        ]


class ShardGather:
    def __init__(self, shards, own, whole, send, recv, local):
        self.shards, self.own, self.whole = shards, own, whole
        self.send, self.recv, self.local = send, recv, local
        self.rows = own.shape[0]
        self.size = self.rows // PARTS

    @staticmethod
    def semaphores(count):
        shape = (2, count // CORES, PARTS)
        return [pltpu.SemaphoreType.DMA(shape), pltpu.SemaphoreType.DMA(shape), pltpu.SemaphoreType.DMA]

    def source(self, part):
        return self.own.at[pl.ds(part * self.size, self.size)]

    def place(self, shard, part):
        return self.whole.at[span(shard * self.rows + part * self.size, self.size)]

    def across(self, offset, part):
        shards = self.shards
        target = {"dp": shards.device(shards.chip_at(offset), shards.core)}
        return send_to(
            target,
            self.source(part),
            self.place(shards.index, part),
            self.send.at[0, offset, part],
            self.recv.at[0, offset, part],
        )

    def beside(self, offset, part):
        shards = self.shards
        place = self.place(shards.device(shards.chip_at(shards.chips - offset), shards.core), part)
        return send_to(
            shards.sibling,
            place if offset else self.source(part),
            place,
            self.send.at[1, offset, part],
            self.recv.at[1, offset, part],
        )

    def keep(self):
        return pltpu.make_async_copy(
            self.own, self.whole.at[span(self.shards.index * self.rows, self.rows)], self.local
        )

    def start(self):
        for part in range(PARTS):
            for offset in range(1, self.shards.chips):
                self.across(offset, part).start()
            self.beside(0, part).start()
        self.keep().start()

    def pass_on(self):
        for part in range(PARTS):
            for offset in range(1, self.shards.chips):
                self.across(offset, part).wait_recv()
                self.beside(offset, part).start()

    def finish(self):
        for part in range(PARTS):
            for offset in range(self.shards.chips):
                self.beside(offset, part).wait_recv()
                self.beside(offset, part).wait_send()
                if offset:
                    self.across(offset, part).wait_send()
        self.keep().wait()


class ShardReduce:
    def __init__(self, shards, whole, own, beside_slots, across_slots, loads, beside_sems, across_sems):
        self.shards, self.whole = shards, whole
        self.own, self.beside_slots, self.across_slots = own, beside_slots, across_slots
        self.loads, self.beside_sems, self.across_sems = loads, beside_sems, across_sems
        self.rows = own.shape[1]
        self.offsets = [*range(1, shards.chips), 0]

    @staticmethod
    def scratch(count, rows, width):
        chips = count // CORES
        return [
            pltpu.VMEM((chips, rows, width), low),
            pltpu.VMEM((chips, rows, width), low),
            pltpu.VMEM((chips - 1, rows, width), low),
            pltpu.SemaphoreType.DMA((chips,)),
            pltpu.SemaphoreType.DMA((2, chips)),
            pltpu.SemaphoreType.DMA((2, chips)),
        ]

    def block(self, offset, core):
        shard = self.shards.device(self.shards.chip_at(offset), core)
        return self.whole.at[span(shard * self.rows, self.rows)]

    def beside(self, offset):
        return send_to(
            self.shards.sibling,
            self.block(offset, 1 - self.shards.core),
            self.beside_slots.at[offset],
            self.beside_sems.at[0, offset],
            self.beside_sems.at[1, offset],
        )

    def load(self, offset):
        return pltpu.make_async_copy(
            self.block(offset, self.shards.core), self.own.at[offset], self.loads.at[offset]
        )

    def across(self, offset):
        return send_to(
            {"dp": self.shards.device(self.shards.chip_at(offset), self.shards.core)},
            self.beside_slots.at[offset],
            self.across_slots.at[offset - 1],
            self.across_sems.at[0, offset],
            self.across_sems.at[1, offset],
        )

    def start(self):
        for offset in self.offsets:
            self.beside(offset).start()
            self.load(offset).start()

    def spread(self):
        for offset in self.offsets:
            self.beside(offset).wait_recv()
            self.load(offset).wait()
            total = self.beside_slots[offset].astype(full) + self.own[offset].astype(full)
            self.beside_slots[offset] = total.astype(low)
            if offset:
                self.across(offset).start()

    def total(self):
        total = self.beside_slots[0].astype(full)
        for offset in range(1, self.shards.chips):
            self.across(offset).wait_recv()
            total += self.across_slots[offset - 1].astype(full)
        return total

    def finish(self):
        for offset in self.offsets:
            self.beside(offset).wait_send()
            if offset:
                self.across(offset).wait_send()


def grouped(refs, size):
    return [refs[number : number + size] for number in range(0, len(refs), size)]


def norm_gather_kernel(count, shard_count, weights, *refs):
    tokens, gains, *shard_refs = refs[: 2 + weights]
    all_rows, gain_rows, *whole_refs = refs[2 + weights : 4 + 2 * weights]
    own, all_gains, send, recv, local, ring_send, ring_recv, *shard_sems = refs[4 + 2 * weights :]
    ring, shards = Ring(count), Shards(shard_count)
    greet([*ring.next, *shards.others()])
    copies = [
        send_to(target, gains, all_gains.at[shards.index], send.at[offset], recv.at[offset])
        for offset, target in enumerate(shards.others())
    ]
    for copy in copies:
        copy.start()
    gathers = [
        ShardGather(shards, shard, whole, *sems)
        for shard, whole, sems in zip(shard_refs, whole_refs, grouped(shard_sems, 3))
    ]
    early, late = gathers[:-1], gathers[-1]
    for gather in early:
        gather.start()
    all_gains[shards.index] = gains[...]
    rows = tokens[...].astype(full)
    factor = lax.rsqrt(jnp.mean(rows * rows, axis=-1, keepdims=True) + EPSILON)
    rows = rows * factor
    for copy in copies:
        copy.wait_recv()
    width = gains.shape[1]
    for shard in range(shard_count):
        gain_rows[:, shard * width : (shard + 1) * width] = all_gains[shard, :8, :].astype(full)
    own[...] = (rows * gain_rows[0:1, :]).astype(low)
    place = row_piece(all_rows, own.shape[0])
    size = own.shape[0] // PARTS
    gather = RingGather(ring, lambda part: own.at[pl.ds(part * size, size)], place, ring_send, ring_recv)
    gather.start()
    kept = pltpu.make_async_copy(own, all_rows.at[span(ring.index * own.shape[0], own.shape[0])], local)
    kept.start()
    for number, step in enumerate(gather.steps()):
        step()
        if number == 0:
            late.start()
        elif number == 1:
            for other in early[:-1]:
                other.pass_on()
        elif number == 2:
            early[-1].pass_on()
    late.pass_on()
    gather.finish()
    for other in gathers:
        other.finish()
    kept.wait()
    for copy in copies:
        copy.wait_send()


def norm_gather(tokens, gains, weights, collective_id):
    count, shard_count = lax.axis_size("seq"), lax.axis_size("dp")
    rows, width = tokens.shape
    return pl.pallas_call(
        functools.partial(norm_gather_kernel, count, shard_count, len(weights)),
        out_shape=[
            shape_of((count * rows, width), low),
            shape_of((8, width), full),
            *[shape_of((shard_count * weight.shape[0], weight.shape[1]), low) for weight in weights],
        ],
        in_specs=[VMEM, VMEM] + [ANY] * len(weights),
        out_specs=[ANY, VMEM] + [ANY] * len(weights),
        scratch_shapes=[
            pltpu.VMEM((rows, width), low),
            pltpu.VMEM((shard_count, *gains.shape), low),
            pltpu.SemaphoreType.DMA((shard_count - 1,)),
            pltpu.SemaphoreType.DMA((shard_count - 1,)),
            pltpu.SemaphoreType.DMA,
            *ring_semaphores(count),
            *ShardGather.semaphores(shard_count) * len(weights),
        ],
        compiler_params=pltpu.CompilerParams(
            collective_id=collective_id, has_side_effects=True, vmem_limit_bytes=VMEM_LIMIT
        ),
        cost_estimate=pl.CostEstimate(flops=0, bytes_accessed=200_000_000, transcendentals=0),
    )(tokens, gains, *weights)


def rope_tables(seq_len):
    half_dim = HD // 2
    steps = np.arange(half_dim, dtype=np.float32) * np.float32(2.0 / HD)
    frequency = np.exp(np.float32(-math.log(10000.0)) * steps)
    angles = np.arange(seq_len, dtype=np.float32)[:, None] * frequency[None, :]
    cos, sin = np.cos(angles), np.sin(angles)
    return (
        np.concatenate([cos, cos], axis=1).astype(np.float32),
        np.concatenate([-sin, sin], axis=1).astype(np.float32),
    )


def turned(values, cos, sin):
    return values * cos + pltpu.roll(values, HD // 2, 1) * sin


def turned_back(values, cos, sin):
    return values * cos - pltpu.roll(values, HD // 2, 1) * sin


def softmax_block(queries, keys, start, length):
    rows, count = queries.shape[0], keys.shape[0]
    scores = dot(queries, keys, 1, 1) * (1.0 / math.sqrt(HD))
    query_pos = start + lax.broadcasted_iota(jnp.int32, (rows, count), 0)
    key_pos = lax.broadcasted_iota(jnp.int32, (rows, count), 1)
    allowed = (key_pos <= query_pos) & (key_pos < length)
    if start + rows > WINDOW:
        allowed = allowed & (query_pos - key_pos < WINDOW)
    scores = jnp.where(allowed, scores, NEGATIVE)
    exponent = jnp.exp(scores - jnp.max(scores, axis=-1, keepdims=True))
    return exponent * (1.0 / jnp.sum(exponent, axis=-1, keepdims=True))


BLOCK = 256


def attend_kernel(
    count,
    shard_count,
    length,
    rows_in,
    query_w,
    key_w,
    value_w,
    cos_in,
    sin_in,
    grad_own,
    out_own,
    down_own,
    queries,
    keys,
    values,
    attended,
    grad_rows,
    down_all,
    out_all,
    out_mine,
    rows,
    weights,
    cos,
    sin,
    loads,
    local,
    grad_send,
    grad_recv,
    out_send,
    out_recv,
    *shard_sems,
):
    ring, shards = Ring(count), Shards(shard_count)
    seq_len, width = queries.shape
    own_rows = grad_own.shape[0]
    out_rows, out_width = out_own.shape
    blocks = seq_len // BLOCK
    weight_loads = [
        pltpu.make_async_copy(source, weights.at[number], loads.at[blocks + number])
        for number, source in enumerate((query_w, key_w, value_w))
    ]
    table_loads = [
        pltpu.make_async_copy(cos_in, cos, loads.at[blocks + 3]),
        pltpu.make_async_copy(sin_in, sin, loads.at[blocks + 4]),
    ]
    row_loads = [
        pltpu.make_async_copy(rows_in.at[pl.ds(n * BLOCK, BLOCK)], rows.at[pl.ds(n * BLOCK, BLOCK)], loads.at[n])
        for n in range(blocks)
    ]
    for load in (*weight_loads, row_loads[0], *table_loads, *row_loads[1:]):
        load.start()
    greet([*ring.next, *shards.greeted()])

    out_size, grad_size = out_rows // PARTS, own_rows // PARTS
    out_gather = RingGather(
        ring,
        lambda part: out_own.at[pl.ds(part * out_size, out_size)],
        lambda index, part: out_mine.at[pl.ds(part * out_size, out_size), span(index * out_width, out_width)],
        out_send,
        out_recv,
    )
    grad_gather = RingGather(
        ring,
        lambda part: grad_own.at[pl.ds(part * grad_size, grad_size)],
        row_piece(grad_rows, own_rows),
        grad_send,
        grad_recv,
    )
    out_gather.start()
    grad_gather.start()
    kept = [
        pltpu.make_async_copy(
            out_own, out_mine.at[:, span(ring.index * out_width, out_width)], local.at[0]
        ),
        pltpu.make_async_copy(grad_own, grad_rows.at[span(ring.index * own_rows, own_rows)], local.at[1]),
    ]
    for copy in kept:
        copy.start()
    down_sems, out_sems = grouped(shard_sems, 3)
    down_gather = ShardGather(shards, down_own, down_all, *down_sems)
    shard_gather = ShardGather(shards, out_mine, out_all, *out_sems)
    down_gather.start()

    def spread_out():
        kept[0].wait()
        out_gather.finish()
        shard_gather.start()

    grad_steps = grad_gather.steps()
    events = [*out_gather.steps(), spread_out, *grad_steps[:2], down_gather.pass_on, *grad_steps[2:-1]]
    events += [shard_gather.pass_on, grad_steps[-1]]

    def project(n):
        if n == 0:
            for load in (*weight_loads, *table_loads):
                load.wait()
        row_loads[n].wait()
        here = pl.ds(n * BLOCK, BLOCK)
        block = rows[here, :]
        for number, place in enumerate((queries, keys, values)):
            linear = dot(block, weights[number])
            for head in range(width // HD):
                lanes = slice(head * HD, (head + 1) * HD)
                one = linear[:, lanes]
                if number < 2:
                    one = turned(one, cos[here, :], sin[here, :])
                place[here, lanes] = one.astype(low)

    limit = length[0]

    def attend(head, n):
        lanes = slice(head * HD, (head + 1) * HD)
        here, upto = pl.ds(n * BLOCK, BLOCK), pl.ds(0, (n + 1) * BLOCK)
        probs = softmax_block(queries[here, lanes], keys[upto, lanes], n * BLOCK, limit)
        attended[here, lanes] = dot(probs.astype(low), values[upto, lanes]).astype(low)

    tasks = [functools.partial(project, n) for n in range(blocks)]
    tasks += [functools.partial(attend, head, n) for head in range(width // HD) for n in range(blocks)]
    weave(tasks, events)
    grad_gather.finish()
    down_gather.finish()
    shard_gather.finish()
    kept[1].wait()


def attend(length, rows, query_w, key_w, value_w, tables, grad_own, out_own, down_own, collective_id):
    count, shard_count = lax.axis_size("seq"), lax.axis_size("dp")
    seq_len, model = rows.shape
    heads = shape_of((seq_len, query_w.shape[1]), low)
    out_rows = out_own.shape[0]
    return pl.pallas_call(
        functools.partial(attend_kernel, count, shard_count),
        out_shape=[heads] * 4
        + [
            shape_of(rows.shape, low),
            shape_of((model, down_own.shape[1]), low),
            shape_of((model, model), low),
        ],
        in_specs=[SMEM] + [ANY] * 9,
        out_specs=[VMEM] * 4 + [ANY] * 3,
        scratch_shapes=[
            pltpu.VMEM((out_rows, model), low),
            pltpu.VMEM(rows.shape, low),
            pltpu.VMEM((3, *query_w.shape), low),
            pltpu.VMEM((seq_len, HD), full),
            pltpu.VMEM((seq_len, HD), full),
            pltpu.SemaphoreType.DMA((seq_len // BLOCK + 5,)),
            pltpu.SemaphoreType.DMA((2,)),
            *ring_semaphores(count),
            *ring_semaphores(count),
            *ShardGather.semaphores(shard_count) * 2,
        ],
        compiler_params=pltpu.CompilerParams(
            collective_id=collective_id, has_side_effects=True, vmem_limit_bytes=VMEM_LIMIT
        ),
        cost_estimate=pl.CostEstimate(flops=0, bytes_accessed=250_000_000, transcendentals=0),
    )(length, rows, query_w, key_w, value_w, *tables, grad_own, out_own, down_own)


TILE = 256


def ffn_kernel(
    count,
    attended,
    out_in,
    tokens,
    gain_rows,
    gate_in,
    up_in,
    down_in,
    grad_rows,
    attended_own,
    resid,
    normed_rows,
    act_out,
    grad_gate_out,
    grad_up_out,
    partial,
    out_w,
    gate_w,
    up_w,
    down_w,
    own,
    normed,
    grads,
    hidden,
    back,
    loads,
    row_loads,
    stores,
    swap_send,
    swap_recv,
    ring_send,
    ring_recv,
    local,
):
    ring = Ring(count)
    size, model = tokens.shape
    heads = attended.shape[1]
    units = gate_w.shape[1]
    weight_loads = [
        pltpu.make_async_copy(source, place, loads.at[number])
        for number, (source, place) in enumerate(
            ((out_in, out_w), (gate_in, gate_w), (up_in, up_w), (down_in, down_w))
        )
    ]
    others = [{"seq": (ring.index + offset) % count} for offset in range(1, count)]
    weight_loads[0].start()
    greet(others)
    place = attended_own.at[:, span(ring.index * heads, heads)]
    swaps = [
        send_to(
            other, attended.at[span(other["seq"] * size, size)], place, swap_send.at[number], swap_recv.at[number]
        )
        for number, other in enumerate(others)
    ]
    for swap in swaps:
        swap.start()
    kept = pltpu.make_async_copy(attended.at[span(ring.index * size, size)], place, local.at[0])
    kept.start()
    for load in weight_loads[1:]:
        load.start()
    weight_loads[0].wait()
    kept.wait()
    for swap in swaps:
        swap.wait_recv()

    def project(tile, carry):
        lanes = span(tile * TILE, TILE)
        resid[:, lanes] = tokens[:, lanes].astype(full) + dot(attended_own[...], out_w[lanes, :], 1, 1)
        return carry

    lax.fori_loop(0, model // TILE, project, 0)
    rows = resid[...]
    factor = lax.rsqrt(jnp.mean(rows * rows, axis=-1, keepdims=True) + EPSILON)
    own[...] = (rows * factor * gain_rows[1:2, :]).astype(low)
    piece = size // PARTS
    gather = RingGather(
        ring, lambda part: own.at[pl.ds(part * piece, piece)], row_piece(normed_rows, size), ring_send, ring_recv
    )
    gather.start()
    kept = pltpu.make_async_copy(own, normed_rows.at[span(ring.index * size, size)], local.at[1])
    kept.start()

    def owners(step):
        if step in (0, ring.half):
            return [ring.shifted(step)]
        return [ring.shifted(-step), ring.shifted(step)]

    def grad_loads(step):
        return [
            pltpu.make_async_copy(
                grad_rows.at[span(owner * size, size)],
                grads.at[step % 2, pl.ds(side * size, size)],
                row_loads.at[step % 2, side],
            )
            for side, owner in enumerate(owners(step))
        ]

    def normed_loads(step):
        return [
            pltpu.make_async_copy(
                own if step == 0 else normed_rows.at[span(owner * size, size)],
                normed.at[pl.ds(side * size, size)],
                row_loads.at[2, side],
            )
            for side, owner in enumerate(owners(step))
        ]

    def result_stores(step):
        results = []
        for side, owner in enumerate(owners(step)):
            here, there = pl.ds(side * size, size), span(owner * size, size)
            for number, place in enumerate((act_out, grad_gate_out, grad_up_out)):
                results.append(
                    pltpu.make_async_copy(hidden.at[number, here], place.at[there], stores.at[side, number])
                )
            results.append(pltpu.make_async_copy(back.at[here], partial.at[there], stores.at[side, 3]))
        return results

    def block(step):
        for load in normed_loads(step):
            load.start()
        if step < ring.half:
            for load in grad_loads(step + 1):
                load.start()
        if step > 0:
            for store in result_stores(step - 1):
                store.wait()
        if step == 0:
            for load in weight_loads[1:]:
                load.wait()
        for load in (*normed_loads(step), *grad_loads(step)):
            load.wait()
        rows = pl.ds(0, size * len(owners(step)))
        slot = step % 2

        def forward(tile, carry):
            lanes = span(tile * TILE, TILE)
            gate = dot(normed[rows, :], gate_w[:, lanes])
            up = dot(normed[rows, :], up_w[:, lanes])
            grad_act = dot(grads[slot, rows, :], down_w[:, lanes])
            sigmoid = 1.0 / (1.0 + jnp.exp(-gate))
            silu = gate * sigmoid
            hidden[0, rows, lanes] = (silu * up).astype(low)
            hidden[1, rows, lanes] = (grad_act * up * sigmoid * (1.0 + gate * (1.0 - sigmoid))).astype(low)
            hidden[2, rows, lanes] = (grad_act * silu).astype(low)
            return carry

        lax.fori_loop(0, units // TILE, forward, 0)

        def backward(tile, carry):
            lanes = span(tile * TILE, TILE)
            total = dot(hidden[1, rows, :], gate_w[lanes, :], 1, 1) + dot(hidden[2, rows, :], up_w[lanes, :], 1, 1)
            back[rows, lanes] = total.astype(low)
            return carry

        lax.fori_loop(0, model // TILE, backward, 0)
        for store in result_stores(step):
            store.start()

    for load in grad_loads(0):
        load.start()
    block(0)
    for step in range(1, ring.half + 1):
        gather.advance(step)
        block(step)
    for store in result_stores(ring.half):
        store.wait()
    gather.finish()
    kept.wait()
    for swap in swaps:
        swap.wait_send()


def ffn(attended, out_w, tokens, gain_rows, gate_w, up_w, down_w, grad_rows, collective_id):
    count = lax.axis_size("seq")
    size, model = tokens.shape
    seq_len, units = grad_rows.shape[0], gate_w.shape[1]
    hidden = shape_of((seq_len, units), low)
    return pl.pallas_call(
        functools.partial(ffn_kernel, count),
        out_shape=[
            shape_of((size, model), low),
            shape_of((size, model), full),
            shape_of((seq_len, model), low),
            hidden,
            hidden,
            hidden,
            shape_of((seq_len, model), low),
        ],
        in_specs=[ANY, ANY, VMEM, VMEM, ANY, ANY, ANY, ANY],
        out_specs=[VMEM, VMEM, ANY, ANY, ANY, ANY, ANY],
        scratch_shapes=[
            pltpu.VMEM(out_w.shape, low),
            pltpu.VMEM(gate_w.shape, low),
            pltpu.VMEM(up_w.shape, low),
            pltpu.VMEM(down_w.shape, low),
            pltpu.VMEM((size, model), low),
            pltpu.VMEM((2 * size, model), low),
            pltpu.VMEM((2, 2 * size, model), low),
            pltpu.VMEM((3, 2 * size, units), low),
            pltpu.VMEM((2 * size, model), low),
            pltpu.SemaphoreType.DMA((4,)),
            pltpu.SemaphoreType.DMA((3, 2)),
            pltpu.SemaphoreType.DMA((2, 4)),
            pltpu.SemaphoreType.DMA((count - 1,)),
            pltpu.SemaphoreType.DMA((count - 1,)),
            *ring_semaphores(count),
            pltpu.SemaphoreType.DMA((2,)),
        ],
        compiler_params=pltpu.CompilerParams(
            collective_id=collective_id, has_side_effects=True, vmem_limit_bytes=VMEM_LIMIT
        ),
        cost_estimate=pl.CostEstimate(flops=0, bytes_accessed=300_000_000, transcendentals=0),
    )(attended, out_w, tokens, gain_rows, gate_w, up_w, down_w, grad_rows)


def ffn_back_kernel(
    count,
    partial,
    normed_rows,
    grad_rows,
    act_in,
    grad_gate_in,
    grad_up_in,
    down_in,
    out_in,
    resid,
    grad_own,
    gain_rows,
    grad_gate_w,
    grad_up_w,
    grad_down_w,
    branch,
    grad_resid,
    grad_attn,
    gain_sum,
    grad_heads,
    hidden,
    down_w,
    out_w,
    tiles,
    staged,
    branch_tile,
    attended,
    loads,
    tile_loads,
    stores,
    swap_send,
    swap_recv,
    local,
    slots,
    terms,
    ring_send,
    ring_recv,
    term_loads,
):
    ring = Ring(count)
    size, model = resid.shape
    heads = grad_heads.shape[1]
    others = [{"seq": (ring.index + offset) % count} for offset in range(1, count)]
    inputs = [
        pltpu.make_async_copy(source, place, loads.at[number])
        for number, (source, place) in enumerate(
            (
                (grad_gate_in, hidden.at[1]),
                (grad_up_in, hidden.at[2]),
                (act_in, hidden.at[0]),
                (down_in, down_w),
                (out_in, out_w),
            )
        )
    ]
    greet(others)
    reduce = RingReduce(ring, row_piece(partial, size), slots, terms, ring_send, ring_recv, term_loads)
    reduce.start()

    def fetch(tile):
        lanes = span(tile * TILE, TILE)
        return [
            pltpu.make_async_copy(source.at[:, lanes], tiles.at[tile % 2, number], tile_loads.at[tile % 2, number])
            for number, source in enumerate((normed_rows, grad_rows))
        ]

    def store(tile):
        lanes, slot = span(tile * TILE, TILE), tile % 2
        copies = [
            pltpu.make_async_copy(staged.at[slot, number], place.at[lanes], stores.at[slot, number])
            for number, place in enumerate((grad_gate_w, grad_up_w, grad_down_w))
        ]
        copies.append(pltpu.make_async_copy(branch_tile.at[slot], branch.at[:, lanes], stores.at[slot, 3]))
        return copies

    count_tiles = model // TILE
    for copy in (inputs[0], *fetch(0), *inputs[1:]):
        copy.start()

    def weights(tile):
        slot = tile % 2
        if tile == 0:
            for copy in inputs[:4]:
                copy.wait()
        if tile + 1 < count_tiles:
            for copy in fetch(tile + 1):
                copy.start()
        if tile >= 2:
            for copy in store(tile - 2):
                copy.wait()
        for copy in fetch(tile):
            copy.wait()
        staged[slot, 0] = dot(tiles[slot, 0], hidden[1], 0, 0).astype(low)
        staged[slot, 1] = dot(tiles[slot, 0], hidden[2], 0, 0).astype(low)
        staged[slot, 2] = dot(tiles[slot, 1], hidden[0], 0, 0).astype(low)
        branch_tile[slot] = dot(hidden[0], down_w[pl.ds(tile * TILE, TILE), :], 1, 1).astype(low)
        for copy in store(tile):
            copy.start()

    tasks = [functools.partial(weights, tile) for tile in range(count_tiles)]
    weave(tasks, [*reduce.steps(), lambda: None])
    inputs[4].wait()
    gain_total = jnp.zeros((1, model), full)
    for part in range(PARTS):
        here = pl.ds(part * reduce.size, reduce.size)
        grad_normed, rows = reduce.total(part), resid[here, :]
        factor = lax.rsqrt(jnp.mean(rows * rows, axis=-1, keepdims=True) + EPSILON)
        weighted = grad_normed * gain_rows[1:2, :]
        inner = jnp.mean(weighted * rows, axis=-1, keepdims=True)
        grad = grad_own[here, :].astype(full) + factor * (weighted - rows * (factor * factor * inner))
        grad_resid[here, :] = grad
        grad_attn[here, :] = grad.astype(low)
        gain_total += jnp.sum(grad_normed * rows * factor, axis=0, keepdims=True)
    gain_sum[...] = jnp.broadcast_to(gain_total, gain_sum.shape)
    place = grad_heads.at[span(ring.index * size, size)]
    swaps = []
    for number, index in enumerate([other["seq"] for other in others] + [ring.index]):
        lanes = span(index * heads, heads)
        attended[:, lanes] = dot(grad_attn[...], out_w[:, lanes]).astype(low)
        if number < count - 1:
            swap = send_to(others[number], attended.at[:, lanes], place, swap_send.at[number], swap_recv.at[number])
        else:
            swap = pltpu.make_async_copy(attended.at[:, lanes], place, local)
        swap.start()
        swaps.append(swap)
    reduce.finish()
    for tile in (count_tiles - 2, count_tiles - 1):
        for copy in store(tile):
            copy.wait()
    for swap in swaps:
        swap.wait()


def ffn_back(partial, normed_rows, grad_rows, hidden, down_w, out_w, resid, grad_own, gain_rows, heads, collective_id):
    count = lax.axis_size("seq")
    size, model = resid.shape
    seq_len, units = hidden[0].shape
    grad_w = shape_of((model, units), low)
    return pl.pallas_call(
        functools.partial(ffn_back_kernel, count),
        out_shape=[
            grad_w,
            grad_w,
            grad_w,
            shape_of((seq_len, model), low),
            shape_of((size, model), full),
            shape_of((size, model), low),
            shape_of((8, model), full),
            shape_of((seq_len, heads), low),
        ],
        in_specs=[ANY] * 8 + [VMEM] * 3,
        out_specs=[ANY] * 4 + [VMEM] * 3 + [ANY],
        scratch_shapes=[
            pltpu.VMEM((3, seq_len, units), low),
            pltpu.VMEM(down_w.shape, low),
            pltpu.VMEM(out_w.shape, low),
            pltpu.VMEM((2, 2, seq_len, TILE), low),
            pltpu.VMEM((2, 3, TILE, units), low),
            pltpu.VMEM((2, seq_len, TILE), low),
            pltpu.VMEM((size, model), low),
            pltpu.SemaphoreType.DMA((5,)),
            pltpu.SemaphoreType.DMA((2, 2)),
            pltpu.SemaphoreType.DMA((2, 4)),
            pltpu.SemaphoreType.DMA((count - 1,)),
            pltpu.SemaphoreType.DMA((count - 1,)),
            pltpu.SemaphoreType.DMA,
            *RingReduce.scratch(count, size, model),
        ],
        compiler_params=pltpu.CompilerParams(
            collective_id=collective_id, has_side_effects=True, vmem_limit_bytes=VMEM_LIMIT
        ),
        cost_estimate=pl.CostEstimate(flops=0, bytes_accessed=300_000_000, transcendentals=0),
    )(partial, normed_rows, grad_rows, *hidden, down_w, out_w, resid, grad_own, gain_rows)


def attend_back_kernel(
    count,
    shard_count,
    length,
    grad_heads,
    queries,
    keys,
    values,
    cos_in,
    sin_in,
    rows_in,
    query_w,
    key_w,
    value_w,
    branch,
    resid,
    grad_attn,
    attended_own,
    unit_grad_w,
    output,
    partial,
    grad_w,
    gain_sum,
    out_sum,
    owned_w,
    cos,
    sin,
    weights,
    grads,
    sum_k,
    sum_v,
    row_tiles,
    staged,
    grad_staged,
    out_staged,
    out_beside,
    out_across,
    loads,
    tile_loads,
    stores,
    grad_stores,
    beside_sems,
    across_sems,
    slots,
    terms,
    ring_send,
    ring_recv,
    term_loads,
    *shard_scratch,
):
    ring, shards = Ring(count), Shards(shard_count)
    seq_len, width = queries.shape
    size, model = resid.shape
    blocks, tiles = seq_len // BLOCK, model // TILE
    scale = 1.0 / math.sqrt(HD)
    limit = length[0]
    inputs = [
        pltpu.make_async_copy(source, place, loads.at[number])
        for number, (source, place) in enumerate(
            (
                (cos_in, cos),
                (sin_in, sin),
                (query_w, weights.at[:, pl.ds(0, width)]),
                (key_w, weights.at[:, pl.ds(width, width)]),
                (value_w, weights.at[:, pl.ds(2 * width, width)]),
            )
        )
    ]
    greet([*ring.next, *shards.greeted()])
    reduce = RingReduce(ring, row_piece(branch, size), slots, terms, ring_send, ring_recv, term_loads)
    reduce.start()
    shard_reduce = ShardReduce(shards, unit_grad_w, *shard_scratch)
    shard_reduce.start()
    for load in inputs:
        load.start()

    out_rows = model // shard_count

    def out_term(shard, lanes):
        return dot(grad_attn[:, span(shard * out_rows, out_rows)], attended_own[:, lanes], 0, 0)

    def beside(offset):
        return send_to(
            shards.sibling,
            out_staged.at[offset],
            out_beside.at[offset],
            beside_sems.at[0, offset],
            beside_sems.at[1, offset],
        )

    def across(offset):
        return send_to(
            {"dp": shards.device(shards.chip_at(offset), shards.core)},
            out_beside.at[offset],
            out_across.at[offset - 1],
            across_sems.at[0, offset],
            across_sems.at[1, offset],
        )

    offsets = [*range(1, shards.chips), 0]
    out_tile = 512

    def out_start(offset):
        shard = shards.device(shards.chip_at(offset), 1 - shards.core)

        def tile(number, carry):
            lanes = span(number * out_tile, out_tile)
            out_staged[offset, :, lanes] = out_term(shard, lanes).astype(low)
            return carry

        lax.fori_loop(0, model // out_tile, tile, 0)
        beside(offset).start()

    def out_middle(offset):
        shard = shards.device(shards.chip_at(offset), shards.core)
        beside(offset).wait_recv()

        def tile(number, carry):
            lanes = span(number * out_tile, out_tile)
            total = out_beside[offset, :, lanes].astype(full) + out_term(shard, lanes)
            out_beside[offset, :, lanes] = total.astype(low)
            return carry

        lax.fori_loop(0, model // out_tile, tile, 0)
        if offset:
            across(offset).start()

    def out_finish():
        for offset in range(1, shards.chips):
            across(offset).wait_recv()

        def tile(number, carry):
            lanes = span(number * out_tile, out_tile)
            total = out_beside[0, :, lanes].astype(full)
            for offset in range(1, shards.chips):
                total += out_across[offset - 1, :, lanes].astype(full)
            out_sum[:, lanes] = total.astype(low)
            return carry

        lax.fori_loop(0, model // out_tile, tile, 0)
        for offset in offsets:
            beside(offset).wait_send()
            if offset:
                across(offset).wait_send()

    def attend_block(head, number):
        lanes = slice(head * HD, (head + 1) * HD)
        here, upto = pl.ds(number * BLOCK, BLOCK), pl.ds(0, (number + 1) * BLOCK)
        if number == 0:
            sum_k[...] = jnp.zeros_like(sum_k)
            sum_v[...] = jnp.zeros_like(sum_v)
            if head == 0:
                for load in inputs[:2]:
                    load.wait()
        query_part, grad_part = queries[here, lanes], grad_heads[here, lanes]
        probs = softmax_block(query_part, keys[upto, lanes], number * BLOCK, limit)
        grad_probs = dot(grad_part, values[upto, lanes], 1, 1)
        inner = jnp.sum(probs * grad_probs, axis=-1, keepdims=True)
        grad_scores = (probs * (grad_probs - inner)).astype(low)
        sum_v[upto, :] += dot(probs.astype(low), grad_part, 0, 0)
        sum_k[upto, :] += dot(grad_scores, query_part, 0, 0)
        grad_query = dot(grad_scores, keys[upto, lanes]) * scale
        grads[here, lanes] = turned_back(grad_query, cos[here, :], sin[here, :]).astype(low)
        if number == blocks - 1:
            key_lanes = slice(width + head * HD, width + (head + 1) * HD)
            value_lanes = slice(2 * width + head * HD, 2 * width + (head + 1) * HD)
            grads[:, key_lanes] = turned_back(sum_k[...] * scale, cos[...], sin[...]).astype(low)
            grads[:, value_lanes] = sum_v[...].astype(low)

    def fetch(tile):
        return pltpu.make_async_copy(
            rows_in.at[:, pl.ds(tile * TILE, TILE)], row_tiles.at[tile % 2], tile_loads.at[tile % 2]
        )

    def store(number):
        return pltpu.make_async_copy(
            staged.at[number % 2], partial.at[pl.ds(number * BLOCK, BLOCK)], stores.at[number % 2]
        )

    def grad_store(tile):
        return pltpu.make_async_copy(
            grad_staged.at[tile % 2], grad_w.at[pl.ds(tile * TILE, TILE)], grad_stores.at[tile % 2]
        )

    def rows_back(number):
        if number == 0:
            for load in inputs[2:]:
                load.wait()
            fetch(0).start()
        if number >= 2:
            store(number - 2).wait()
        staged[number % 2] = dot(grads[pl.ds(number * BLOCK, BLOCK), :], weights[...], 1, 1).astype(low)
        store(number).start()

    def weights_back(tile):
        if tile + 1 < tiles:
            fetch(tile + 1).start()
        if tile >= 2:
            grad_store(tile - 2).wait()
        fetch(tile).wait()
        grad = dot(row_tiles[tile % 2], grads[...], 0, 0)
        grad_staged[tile % 2] = grad.astype(low)
        grad_store(tile).start()
        shared = grad * weights[pl.ds(tile * TILE, TILE), :].astype(full)
        gain_sum[:, pl.ds(tile * TILE, TILE)] = lax.dot_general(
            jnp.ones((8, shared.shape[1]), full),
            shared,
            (((1,), (1,)), ((), ())),
            precision=lax.Precision.HIGHEST,
            preferred_element_type=full,
        )

    def finish_output():
        for part in range(PARTS):
            here = pl.ds(part * reduce.size, reduce.size)
            position = (
                ring.index * size + part * reduce.size + lax.broadcasted_iota(jnp.int32, (reduce.size, model), 0)
            )
            total = resid[here, :] + reduce.total(part)
            output[here, :] = jnp.where(position < limit, total, 0.0).astype(low)

    tasks = [functools.partial(out_start, offset) for offset in offsets] + [shard_reduce.spread]
    attention = [
        functools.partial(attend_block, head, number) for head in range(width // HD) for number in range(blocks)
    ]
    tasks += attention[:2] + [functools.partial(out_middle, offset) for offset in offsets] + attention[2:]
    tasks += [functools.partial(rows_back, number) for number in range(blocks)]
    tasks += [functools.partial(weights_back, tile) for tile in range(tiles)]
    weave(tasks, [*reduce.steps(), lambda: None])
    for number in (blocks - 2, blocks - 1):
        store(number).wait()
    for tile in (tiles - 2, tiles - 1):
        grad_store(tile).wait()
    owned_w[...] = shard_reduce.total()
    out_finish()
    finish_output()
    reduce.finish()
    shard_reduce.finish()


def attend_back(
    length,
    grad_heads,
    queries,
    keys,
    values,
    tables,
    rows,
    query_w,
    key_w,
    value_w,
    branch,
    resid,
    grad_attn,
    attended_own,
    unit_grad_w,
    collective_id,
):
    count, shard_count = lax.axis_size("seq"), lax.axis_size("dp")
    seq_len, width = queries.shape
    size, model = resid.shape
    chips, out_rows, units = shard_count // CORES, model // shard_count, unit_grad_w.shape[1]
    return pl.pallas_call(
        functools.partial(attend_back_kernel, count, shard_count),
        out_shape=[
            shape_of((size, model), low),
            shape_of((seq_len, model), low),
            shape_of((model, 3 * width), low),
            shape_of((8, model), full),
            shape_of((out_rows, model), low),
            shape_of((out_rows, units), full),
        ],
        in_specs=[SMEM] + [VMEM] * 4 + [ANY] * 7 + [VMEM] * 3 + [ANY],
        out_specs=[VMEM, ANY, ANY, VMEM, VMEM, VMEM],
        scratch_shapes=[
            pltpu.VMEM((seq_len, HD), full),
            pltpu.VMEM((seq_len, HD), full),
            pltpu.VMEM((model, 3 * width), low),
            pltpu.VMEM((seq_len, 3 * width), low),
            pltpu.VMEM((seq_len, HD), full),
            pltpu.VMEM((seq_len, HD), full),
            pltpu.VMEM((2, seq_len, TILE), low),
            pltpu.VMEM((2, BLOCK, model), low),
            pltpu.VMEM((2, TILE, 3 * width), low),
            pltpu.VMEM((chips, out_rows, model), low),
            pltpu.VMEM((chips, out_rows, model), low),
            pltpu.VMEM((chips - 1, out_rows, model), low),
            pltpu.SemaphoreType.DMA((5,)),
            pltpu.SemaphoreType.DMA((2,)),
            pltpu.SemaphoreType.DMA((2,)),
            pltpu.SemaphoreType.DMA((2,)),
            pltpu.SemaphoreType.DMA((2, chips)),
            pltpu.SemaphoreType.DMA((2, chips)),
            *RingReduce.scratch(count, size, model),
            *ShardReduce.scratch(shard_count, out_rows, units),
        ],
        compiler_params=pltpu.CompilerParams(
            collective_id=collective_id, has_side_effects=True, vmem_limit_bytes=VMEM_LIMIT
        ),
        cost_estimate=pl.CostEstimate(flops=0, bytes_accessed=250_000_000, transcendentals=0),
    )(
        length,
        grad_heads,
        queries,
        keys,
        values,
        *tables,
        rows,
        query_w,
        key_w,
        value_w,
        branch,
        resid,
        grad_attn,
        attended_own,
        unit_grad_w,
    )


def last_kernel(
    count,
    shard_count,
    partial,
    grad_w,
    up_grad_w,
    down_grad_w,
    out_sum,
    tokens,
    gain_rows,
    grad_resid,
    gain_blocks,
    grad_tokens,
    grad_query_w,
    grad_key_w,
    grad_value_w,
    grad_out_w,
    grad_up_w,
    grad_down_w,
    gains,
    gain_slots,
    gain_sum,
    gain_shards,
    gain_sems,
    shard_gain_sems,
    *scratch,
):
    out_scratch, ring_scratch = scratch[:5], scratch[5:10]
    shard_scratch = grouped(scratch[10:], 6)
    ring, shards = Ring(count), Shards(shard_count)
    size = tokens.shape[0]
    rows, width = grad_out_w.shape
    others = [{"seq": (ring.index + offset) % count} for offset in range(1, count)]
    greet([*others, *shards.others()])

    def out_piece(index, part):
        piece = rows // PARTS
        return out_sum.at[pl.ds(part * piece, piece), span(index * width, width)]

    reduce = RingReduce(ring, row_piece(partial, size), *ring_scratch)
    out_reduce = RingReduce(ring, out_piece, *out_scratch)
    reduce.start()
    out_reduce.start()
    weights = [
        ShardReduce(shards, whole, *one) for whole, one in zip((up_grad_w, down_grad_w, grad_w), shard_scratch)
    ]
    gain_copies = [
        send_to(
            other,
            gain_blocks.at[other["seq"]],
            gain_slots.at[ring.index],
            gain_sems.at[0, number],
            gain_sems.at[1, number],
        )
        for number, other in enumerate(others)
    ]
    shard_gain_copies = [
        send_to(
            other, gain_sum, gain_shards.at[shards.index], shard_gain_sems.at[0, number], shard_gain_sems.at[1, number]
        )
        for number, other in enumerate(shards.others())
    ]
    for copy in gain_copies:
        copy.start()
    for weight in weights:
        weight.start()
    for weight in weights:
        weight.spread()
    gain_slots[ring.index] = gain_blocks[ring.index]
    for copy in gain_copies:
        copy.wait_recv()
    gain_sum[...] = jnp.sum(gain_slots[...], axis=0)
    for copy in shard_gain_copies:
        copy.start()

    def finish_gains():
        gain_shards[shards.index] = gain_sum[...]
        for copy in shard_gain_copies:
            copy.wait_recv()
        gains[...] = jnp.sum(gain_shards[...], axis=0)

    def finish_qkv():
        total = weights[2].total()
        for number, place in enumerate((grad_query_w, grad_key_w, grad_value_w)):
            place[...] = total[:, number * width : (number + 1) * width]

    def finish_up():
        grad_up_w[...] = weights[0].total()

    def finish_down():
        grad_down_w[...] = weights[1].total()

    out_steps, steps = out_reduce.steps(), reduce.steps()
    finals = [finish_gains, finish_up, finish_down]
    for number, step in enumerate(steps):
        out_steps[number]()
        step()
        if number < len(finals):
            finals[number]()
    finish_qkv()
    for part in range(PARTS):
        grad_out_w[pl.ds(part * out_reduce.size, out_reduce.size), :] = out_reduce.total(part)
    for part in range(PARTS):
        here = pl.ds(part * reduce.size, reduce.size)
        grad_normed, values = reduce.total(part), tokens[here, :].astype(full)
        factor = lax.rsqrt(jnp.mean(values * values, axis=-1, keepdims=True) + EPSILON)
        weighted = grad_normed * gain_rows[0:1, :]
        inner = jnp.mean(weighted * values, axis=-1, keepdims=True)
        grad_tokens[here, :] = grad_resid[here, :] + factor * (weighted - values * (factor * factor * inner))
    reduce.finish()
    out_reduce.finish()
    for weight in weights:
        weight.finish()
    for copy in (*gain_copies, *shard_gain_copies):
        copy.wait_send()


def last(partial, grad_w, up_grad_w, down_grad_w, out_sum, tokens, gain_rows, grad_resid, gain_blocks, collective_id):
    count, shard_count = lax.axis_size("seq"), lax.axis_size("dp")
    size = tokens.shape[0]
    rows, model = out_sum.shape
    width, units = model // count, up_grad_w.shape[1]
    block = gain_blocks.shape[1:]
    return pl.pallas_call(
        functools.partial(last_kernel, count, shard_count),
        out_shape=[
            shape_of(tokens.shape, full),
            *[shape_of((rows, width), full)] * 4,
            *[shape_of((rows, units), full)] * 2,
            shape_of(block, full),
        ],
        in_specs=[ANY] * 5 + [VMEM] * 4,
        out_specs=[VMEM] * 8,
        scratch_shapes=[
            pltpu.VMEM((count, *block), full),
            pltpu.VMEM(block, full),
            pltpu.VMEM((shard_count, *block), full),
            pltpu.SemaphoreType.DMA((2, count - 1)),
            pltpu.SemaphoreType.DMA((2, shard_count - 1)),
            *RingReduce.scratch(count, rows, width),
            *RingReduce.scratch(count, size, model),
            *ShardReduce.scratch(shard_count, rows, units),
            *ShardReduce.scratch(shard_count, rows, units),
            *ShardReduce.scratch(shard_count, rows, 3 * width),
        ],
        compiler_params=pltpu.CompilerParams(
            collective_id=collective_id, has_side_effects=True, vmem_limit_bytes=VMEM_LIMIT
        ),
        cost_estimate=pl.CostEstimate(flops=0, bytes_accessed=200_000_000, transcendentals=0),
    )(partial, grad_w, up_grad_w, down_grad_w, out_sum, tokens, gain_rows, grad_resid, gain_blocks)


def body(
    tokens,
    lengths,
    cotangent,
    w_query,
    w_key,
    w_value,
    w_out,
    w_gate,
    w_up,
    w_down,
    gain_attn,
    gain_ffn,
):
    tok_rows = tokens.shape[0]
    seq_len = tok_rows * lax.axis_size("seq")
    head_width = w_query.shape[1]
    length = lengths[0]
    local_pos = lax.axis_index("seq") * tok_rows + jnp.arange(tok_rows, dtype=jnp.int32)
    valid_mask = (local_pos < length).astype(jnp.float32)[:, None]
    tables = rope_tables(seq_len)
    gains = jnp.concatenate(
        [gain_attn[None], gain_ffn[None], jnp.zeros((14, gain_attn.shape[0]), gain_attn.dtype)], axis=0
    )
    grad_ffn = jnp.where(valid_mask > 0, cotangent, jnp.zeros_like(cotangent))

    full1, gain_rows, query_w, key_w, value_w, gate_w, up_w = norm_gather(
        tokens, gains, (w_query, w_key, w_value, w_gate, w_up), 1
    )
    queries, key_rot, values, attended_heads, grad_full, down_w, out_full = attend(
        lengths, full1, query_w, key_w, value_w, tables, grad_ffn, w_out, w_down, 2
    )
    attended_tok, resid, full2, activation, grad_gate, grad_up, partial2 = ffn(
        attended_heads, out_full, tokens, gain_rows, gate_w, up_w, down_w, grad_full, 3
    )
    grad_w_gate, grad_w_up, grad_w_down, branch, grad_resid, grad_attn, gain_ffn_sum, grad_heads = ffn_back(
        partial2,
        full2,
        grad_full,
        (activation, grad_gate, grad_up),
        down_w,
        out_full,
        resid,
        grad_ffn,
        gain_rows,
        head_width,
        4,
    )
    output, partial1, grad_w, gain_attn_sum, out_sum, owned_gate = attend_back(
        lengths,
        grad_heads,
        queries,
        key_rot,
        values,
        tables,
        full1,
        query_w,
        key_w,
        value_w,
        branch,
        resid,
        grad_attn,
        attended_tok,
        grad_w_gate,
        5,
    )
    count, shard_count = lax.axis_size("seq"), lax.axis_size("dp")
    gain_sums = jnp.stack([gain_attn_sum[0] / gain_rows[0], gain_ffn_sum[0]])
    piece = gain_sums.shape[1] // (count * shard_count)
    gain_blocks = gain_sums.reshape(2, shard_count, count, piece).transpose(2, 1, 0, 3)
    gain_blocks = gain_blocks.reshape(count, shard_count, 2 * piece)
    gain_blocks = jnp.pad(gain_blocks, ((0, 0), (0, 8 - shard_count), (0, 128 - 2 * piece)))
    grad_tokens, owned_query, owned_key, owned_value, owned_out, owned_up, owned_down, owned_gains = last(
        partial1, grad_w, grad_w_up, grad_w_down, out_sum, tokens, gain_rows, grad_resid, gain_blocks, 6
    )
    owned_gains = lax.dynamic_index_in_dim(owned_gains, lax.axis_index("dp"), 0, keepdims=False)
    owned_gain_attn, owned_gain_ffn = owned_gains[:piece], owned_gains[piece : 2 * piece]
    return (
        output,
        grad_tokens,
        owned_query,
        owned_key,
        owned_value,
        owned_out,
        owned_gate,
        owned_up,
        owned_down,
        owned_gain_attn,
        owned_gain_ffn,
    )


def solution(mesh):
    rows, shard = P(("dp", "seq"), None), P("dp", "seq")
    gains = P(("dp", "seq"))
    return jax.shard_map(
        body,
        mesh=mesh,
        in_specs=(rows, P("dp"), rows, *[shard] * 7, P("dp"), P("dp")),
        out_specs=(rows, rows, *[shard] * 7, gains, gains),
        check_vma=False,
    )
```

```python
import functools
import math

import jax
import jax.numpy as jnp
import numpy as np
from jax import lax
from jax.experimental import pallas as pl
from jax.experimental.pallas import tpu as pltpu
from jax.sharding import PartitionSpec as P

HD = 128
WINDOW = 2048
EPSILON = 1e-05
NEGATIVE = -1e30
BLOCK = 256
TILE = 256
LINE = 4
CORES = 2
PARTS = 2
MESH = pl.DeviceIdType.MESH
VMEM_LIMIT = 60 * 1024 * 1024

ANY = pl.BlockSpec(memory_space=pl.ANY)
VMEM = pl.BlockSpec(memory_space=pltpu.VMEM)
SMEM = pl.BlockSpec(memory_space=pltpu.SMEM)
low = jnp.bfloat16
full = jnp.float32


def shape_of(shape, dtype):
    return jax.ShapeDtypeStruct(shape, dtype)


def span(start, size):
    if isinstance(start, int):
        return pl.ds(start, size)
    return pl.ds(pl.multiple_of(start, size), size)


def dot(left, right, left_dim=1, right_dim=0):
    return lax.dot_general(
        left, right, (((left_dim,), (right_dim,)), ((), ())), preferred_element_type=jnp.float32
    )


def greet(targets):
    barrier = pltpu.get_barrier_semaphore()
    for target in targets:
        pl.semaphore_signal(barrier, inc=1, device_id=target, device_id_type=MESH)
    pl.semaphore_wait(barrier, len(targets))


def send_to(target, source, place, send, recv):
    return pltpu.make_async_remote_copy(
        src_ref=source, dst_ref=place, send_sem=send, recv_sem=recv, device_id=target, device_id_type=MESH
    )


def weave(tasks, events):
    done = 0
    for number, task in enumerate(tasks):
        task()
        upto = (number + 1) * len(events) // len(tasks)
        for event in events[done:upto]:
            event()
        done = upto


def ring_index(place, count):
    columns = count // LINE
    column = place // LINE
    level = place % LINE
    odd = column % 2
    return (level + odd * (LINE - 1 - 2 * level)) * columns + column


def ring_place(index, count):
    columns = count // LINE
    level = index // columns
    column = index % columns
    odd = column % 2
    return column * LINE + level + odd * (LINE - 1 - 2 * level)


class Ring:
    def __init__(self, count):
        self.count = count
        self.half = count // 2
        self.index = lax.axis_index("seq")
        self.place = ring_place(self.index, count)
        self.next = ({"seq": self.shifted(1)}, {"seq": self.shifted(-1)})

    def shifted(self, offset):
        return ring_index((self.place + offset + self.count) % self.count, self.count)


def ring_semaphores(count):
    return [pltpu.SemaphoreType.DMA((2, count // 2, PARTS))] * 2


class RingGather:
    def __init__(self, ring, source, place, send, recv):
        self.ring, self.source, self.place = ring, source, place
        self.send, self.recv = send, recv

    def pieces(self, way, step):
        if step < self.ring.half - 1:
            return range(PARTS)
        return range(PARTS // 2) if way == 0 else range(PARTS // 2, PARTS)

    def copy(self, way, step, part):
        place = self.place(self.ring.shifted(step if way else -step), part)
        return send_to(
            self.ring.next[way],
            self.source(part) if step == 0 else place,
            place,
            self.send.at[way, step, part],
            self.recv.at[way, step, part],
        )

    def start(self):
        for part in range(PARTS):
            for way in range(2):
                if part in self.pieces(way, 0):
                    self.copy(way, 0, part).start()

    def advance(self, step):
        for part in range(PARTS):
            for way in range(2):
                if part in self.pieces(way, step - 1):
                    self.copy(way, step - 1, part).wait_recv()
                if step < self.ring.half and part in self.pieces(way, step):
                    self.copy(way, step, part).start()

    def finish(self):
        for step in range(self.ring.half):
            for way in range(2):
                for part in self.pieces(way, step):
                    self.copy(way, step, part).wait_send()

    def steps(self):
        return [functools.partial(self.advance, step) for step in range(1, self.ring.half + 1)]


class RingReduce:
    def __init__(self, ring, mine, slots, terms, send, recv, load):
        self.ring, self.mine, self.slots, self.terms = ring, mine, slots, terms
        self.send, self.recv, self.load = send, recv, load
        self.size = slots.shape[2] // PARTS

    @staticmethod
    def scratch(count, rows, width):
        return [
            pltpu.VMEM((2, count // 2, rows, width), low),
            pltpu.VMEM((2, 2, rows, width), low),
            *ring_semaphores(count),
            pltpu.SemaphoreType.DMA((2, 2, PARTS)),
        ]

    def pieces(self, way, step):
        if step > 0:
            return range(PARTS)
        return range(PARTS // 2) if way == 0 else range(PARTS // 2, PARTS)

    def summed(self, way, step):
        return self.pieces(way, 0) if step == 1 else range(PARTS)

    def target(self, way, step):
        left = self.ring.half - step
        return self.ring.shifted(-left if way else left)

    def slot(self, way, step, part):
        return self.slots.at[way, step, pl.ds(part * self.size, self.size)]

    def term(self, way, step, part):
        return self.terms.at[step % 2, way, pl.ds(part * self.size, self.size)]

    def fetch(self, way, step, part):
        return pltpu.make_async_copy(
            self.mine(self.target(way, step), part), self.term(way, step, part), self.load.at[step % 2, way, part]
        )

    def fetch_all(self, step):
        for part in range(PARTS):
            for way in range(2 if step < self.ring.half else 1):
                if part in self.summed(way, step):
                    self.fetch(way, step, part).start()

    def copy(self, way, step, part):
        alone = step == 0 or part not in self.summed(way, step)
        source = self.mine(self.target(way, step), part) if alone else self.slot(way, step - 1, part)
        return send_to(
            self.ring.next[way],
            source,
            self.slot(way, step, part),
            self.send.at[way, step, part],
            self.recv.at[way, step, part],
        )

    def start(self):
        for way in range(2):
            for part in self.pieces(way, 0):
                self.copy(way, 0, part).start()
        self.fetch_all(1)

    def advance(self, step):
        self.fetch_all(step + 1)
        order = [(way, part) for part in range(PARTS) for way in range(2)]
        for way, part in order:
            if part not in self.summed(way, step):
                self.copy(way, step, part).start()
        for way, part in order:
            if part in self.summed(way, step):
                self.fetch(way, step, part).wait()
                self.copy(way, step - 1, part).wait_recv()
                slot = self.slot(way, step - 1, part)
                total = slot[...].astype(full) + self.term(way, step, part)[...].astype(full)
                slot[...] = total.astype(slot.dtype)
                self.copy(way, step, part).start()

    def steps(self):
        return [functools.partial(self.advance, step) for step in range(1, self.ring.half)]

    def total(self, part):
        last = self.ring.half - 1
        self.fetch(0, last + 1, part).wait()
        for way in range(2):
            self.copy(way, last, part).wait_recv()
        return (
            self.term(0, last + 1, part)[...].astype(full)
            + self.slot(0, last, part)[...].astype(full)
            + self.slot(1, last, part)[...].astype(full)
        )

    def finish(self):
        for step in range(self.ring.half):
            for way in range(2):
                for part in self.pieces(way, step):
                    self.copy(way, step, part).wait_send()


def row_piece(ref, rows):
    size = rows // PARTS
    return lambda index, part: ref.at[span(index * rows + part * size, size)]


class Shards:
    def __init__(self, count):
        self.count = count
        self.chips = count // CORES
        self.index = lax.axis_index("dp")
        self.chip = self.index // CORES
        self.core = self.index % CORES
        self.sibling = {"dp": self.chip * CORES + 1 - self.core}

    def chip_at(self, offset):
        return (self.chip + offset) % self.chips

    def device(self, chip, core):
        return chip * CORES + core

    def others(self):
        return [{"dp": (self.index + offset) % self.count} for offset in range(1, self.count)]

    def greeted(self):
        return [self.sibling] + [
            {"dp": self.device(self.chip_at(offset), self.core)} for offset in range(1, self.chips)
        ]


class ShardGather:
    def __init__(self, shards, own, whole, send, recv, local):
        self.shards, self.own, self.whole = shards, own, whole
        self.send, self.recv, self.local = send, recv, local
        self.rows = whole.shape[0] // shards.count
        self.size = self.rows // PARTS

    @staticmethod
    def semaphores(count):
        shape = (2, count // CORES, PARTS)
        return [pltpu.SemaphoreType.DMA(shape), pltpu.SemaphoreType.DMA(shape), pltpu.SemaphoreType.DMA]

    def source(self, part):
        if self.own is None:
            return self.place(self.shards.index, part)
        return self.own.at[pl.ds(part * self.size, self.size)]

    def place(self, shard, part):
        return self.whole.at[span(shard * self.rows + part * self.size, self.size)]

    def across(self, offset, part):
        shards = self.shards
        target = {"dp": shards.device(shards.chip_at(offset), shards.core)}
        return send_to(
            target,
            self.source(part),
            self.place(shards.index, part),
            self.send.at[0, offset, part],
            self.recv.at[0, offset, part],
        )

    def beside(self, offset, part):
        shards = self.shards
        place = self.place(shards.device(shards.chip_at(shards.chips - offset), shards.core), part)
        return send_to(
            shards.sibling,
            place if offset else self.source(part),
            place,
            self.send.at[1, offset, part],
            self.recv.at[1, offset, part],
        )

    def keep(self):
        place = self.whole.at[span(self.shards.index * self.rows, self.rows)]
        return pltpu.make_async_copy(self.own, place, self.local)

    def start(self):
        for part in range(PARTS):
            for offset in range(1, self.shards.chips):
                self.across(offset, part).start()
            self.beside(0, part).start()
        if self.own is not None:
            self.keep().start()

    def pass_on(self):
        for part in range(PARTS):
            for offset in range(1, self.shards.chips):
                self.across(offset, part).wait_recv()
                self.beside(offset, part).start()

    def arrive(self):
        for part in range(PARTS):
            for offset in range(self.shards.chips):
                self.beside(offset, part).wait_recv()
        if self.own is not None:
            self.keep().wait()

    def finish(self):
        for part in range(PARTS):
            for offset in range(self.shards.chips):
                self.beside(offset, part).wait_send()
                if offset:
                    self.across(offset, part).wait_send()


class ShardReduce:
    def __init__(self, shards, whole, own, beside_slots, across_slots, loads, beside_sems, across_sems):
        self.shards, self.whole = shards, whole
        self.own, self.beside_slots, self.across_slots = own, beside_slots, across_slots
        self.loads, self.beside_sems, self.across_sems = loads, beside_sems, across_sems
        self.rows = own.shape[1]
        self.offsets = [*range(1, shards.chips), 0]

    @staticmethod
    def scratch(count, rows, width):
        chips = count // CORES
        return [
            pltpu.VMEM((chips, rows, width), low),
            pltpu.VMEM((chips, rows, width), low),
            pltpu.VMEM((chips - 1, rows, width), low),
            pltpu.SemaphoreType.DMA((chips,)),
            pltpu.SemaphoreType.DMA((2, chips)),
            pltpu.SemaphoreType.DMA((2, chips)),
        ]

    def block(self, offset, core):
        shard = self.shards.device(self.shards.chip_at(offset), core)
        return self.whole.at[span(shard * self.rows, self.rows)]

    def beside(self, offset):
        return send_to(
            self.shards.sibling,
            self.block(offset, 1 - self.shards.core),
            self.beside_slots.at[offset],
            self.beside_sems.at[0, offset],
            self.beside_sems.at[1, offset],
        )

    def load(self, offset):
        return pltpu.make_async_copy(
            self.block(offset, self.shards.core), self.own.at[offset], self.loads.at[offset]
        )

    def across(self, offset):
        return send_to(
            {"dp": self.shards.device(self.shards.chip_at(offset), self.shards.core)},
            self.beside_slots.at[offset],
            self.across_slots.at[offset - 1],
            self.across_sems.at[0, offset],
            self.across_sems.at[1, offset],
        )

    def start(self):
        for offset in self.offsets:
            self.beside(offset).start()
            self.load(offset).start()

    def spread(self):
        for offset in self.offsets:
            self.beside(offset).wait_recv()
            self.load(offset).wait()
            total = self.beside_slots[offset].astype(full) + self.own[offset].astype(full)
            self.beside_slots[offset] = total.astype(low)
            if offset:
                self.across(offset).start()

    def total(self):
        total = self.beside_slots[0].astype(full)
        for offset in range(1, self.shards.chips):
            self.across(offset).wait_recv()
            total += self.across_slots[offset - 1].astype(full)
        return total

    def finish(self):
        for offset in self.offsets:
            self.beside(offset).wait_send()
            if offset:
                self.across(offset).wait_send()


def grouped(refs, size):
    return [refs[number : number + size] for number in range(0, len(refs), size)]


def rope_tables(seq_len):
    half_dim = HD // 2
    steps = np.arange(half_dim, dtype=np.float32) * np.float32(2.0 / HD)
    frequency = np.exp(np.float32(-math.log(10000.0)) * steps)
    angles = np.arange(seq_len, dtype=np.float32)[:, None] * frequency[None, :]
    cos, sin = np.cos(angles), np.sin(angles)
    return (
        np.concatenate([cos, cos], axis=1).astype(np.float32),
        np.concatenate([-sin, sin], axis=1).astype(np.float32),
    )


def turned(values, cos, sin):
    return values * cos + pltpu.roll(values, HD // 2, 1) * sin


def turned_back(values, cos, sin):
    return values * cos - pltpu.roll(values, HD // 2, 1) * sin


def softmax_block(queries, keys, start, length):
    rows, count = queries.shape[0], keys.shape[0]
    scores = dot(queries, keys, 1, 1) * (1.0 / math.sqrt(HD))
    query_pos = start + lax.broadcasted_iota(jnp.int32, (rows, count), 0)
    key_pos = lax.broadcasted_iota(jnp.int32, (rows, count), 1)
    allowed = (key_pos <= query_pos) & (key_pos < length)
    if start + rows > WINDOW:
        allowed = allowed & (query_pos - key_pos < WINDOW)
    scores = jnp.where(allowed, scores, NEGATIVE)
    exponent = jnp.exp(scores - jnp.max(scores, axis=-1, keepdims=True))
    return exponent * (1.0 / jnp.sum(exponent, axis=-1, keepdims=True))


def forward_kernel(count, shard_count, *refs):
    (length, tokens, gains, cotangent, query_in, key_in, value_in, out_in, gate_in, up_in, down_in, cos_in, sin_in) = (
        refs[:13]
    )
    (gain_rows, queries, keys, values, grad_own, attended_own, resid) = refs[13:20]
    (all_rows, grad_rows, normed_rows, qkv_out, out_out, down_out, act_out, grad_gate_out, grad_up_out, partial) = (
        refs[20:30]
    )
    (all_gains, qkv_w, out_w, gate_w, up_w, down_w, cos, sin, own, attended, normed, grads, hidden, back) = refs[30:44]
    (gain_sems, local, row_loads, stores, weight_stores, swap_sems) = refs[44:50]
    sems = refs[50:]
    out_sems, row_sems, grad_sems, normed_sems = grouped(sems[:8], 2)
    shard_sems = grouped(sems[8:], 3)

    ring, shards = Ring(count), Shards(shard_count)
    size, model = tokens.shape
    seq_len, width = queries.shape
    units = gate_w.shape[1]
    limit = length[0]
    others = [{"seq": (ring.index + offset) % count} for offset in range(1, count)]
    tables = [pltpu.make_async_copy(cos_in, cos, local.at[0]), pltpu.make_async_copy(sin_in, sin, local.at[1])]
    for table in tables:
        table.start()
    greet([*others, *shards.others()])

    out_rows, out_width = out_in.shape
    out_mine = out_w.at[span(shards.index * out_rows, out_rows)]
    out_piece = out_rows // PARTS
    out_gather = RingGather(
        ring,
        lambda part: out_in.at[pl.ds(part * out_piece, out_piece)],
        lambda index, part: out_w.at[
            span(shards.index * out_rows + part * out_piece, out_piece), span(index * out_width, out_width)
        ],
        *out_sems,
    )
    out_kept = pltpu.make_async_copy(out_in, out_mine.at[:, span(ring.index * out_width, out_width)], local.at[2])
    out_gather.start()
    out_kept.start()
    gain_copies = [
        send_to(target, gains, all_gains.at[shards.index], gain_sems.at[0, number], gain_sems.at[1, number])
        for number, target in enumerate(shards.others())
    ]
    for copy in gain_copies:
        copy.start()
    qkv_gathers = [
        ShardGather(shards, source, qkv_w.at[:, pl.ds(number * width, width)], *shard_sems[number])
        for number, source in enumerate((query_in, key_in, value_in))
    ]
    out_shards = ShardGather(shards, None, out_w, *shard_sems[3])
    gate_gather, up_gather, down_gather = (
        ShardGather(shards, source, whole, *shard_sems[4 + number])
        for number, (source, whole) in enumerate(((gate_in, gate_w), (up_in, up_w), (down_in, down_w)))
    )
    for gather in qkv_gathers:
        gather.start()

    piece = size // PARTS
    rows = tokens[...].astype(full)
    rows = rows * lax.rsqrt(jnp.mean(rows * rows, axis=-1, keepdims=True) + EPSILON)
    all_gains[shards.index] = gains[...]
    for copy in gain_copies:
        copy.wait_recv()
    gain_width = gains.shape[1]
    for shard in range(shard_count):
        gain_rows[:, shard * gain_width : (shard + 1) * gain_width] = all_gains[shard, :8, :].astype(full)
    own[0] = (rows * gain_rows[0:1, :]).astype(low)

    def own_gather(source, whole, pair):
        return RingGather(ring, lambda part: source.at[pl.ds(part * piece, piece)], row_piece(whole, size), *pair)

    def own_kept(source, whole, number):
        return pltpu.make_async_copy(source, whole.at[span(ring.index * size, size)], local.at[number])

    row_gather = own_gather(own.at[0], all_rows, row_sems)
    row_gather.start()
    row_kept = own_kept(own.at[0], all_rows, 3)
    row_kept.start()
    gate_gather.start()
    position = ring.index * size + lax.broadcasted_iota(jnp.int32, (size, model), 0)
    grad_own[...] = jnp.where(position < limit, cotangent[...].astype(full), 0.0).astype(low)
    grad_gather = own_gather(grad_own, grad_rows, grad_sems)
    grad_kept = own_kept(grad_own, grad_rows, 4)
    grad_kept.start()

    def owners(step):
        if step in (0, ring.half):
            return [ring.shifted(step)]
        return [ring.shifted(-step), ring.shifted(step)]

    def normed_loads(step, mine, whole):
        return [
            pltpu.make_async_copy(
                mine if step == 0 else whole.at[span(owner * size, size)],
                normed.at[pl.ds(side * size, size)],
                row_loads.at[2, side],
            )
            for side, owner in enumerate(owners(step))
        ]

    def project(step):
        loads = normed_loads(step, own.at[0], all_rows)
        for load in loads:
            load.start()
        for load in loads:
            load.wait()
        linear = dot(normed[pl.ds(0, size * len(loads)), :], qkv_w[...])
        for side, owner in enumerate(owners(step)):
            here = span(owner * size, size)
            side_cos, side_sin = cos[here, :], sin[here, :]
            for number, place in enumerate((queries, keys, values)):
                for head in range(width // HD):
                    lanes = slice(head * HD, (head + 1) * HD)
                    first = number * width + head * HD
                    one = linear[side * size : (side + 1) * size, first : first + HD]
                    if number < 2:
                        one = turned(one, side_cos, side_sin)
                    place[here, lanes] = one.astype(low)

    for step in out_gather.steps():
        step()
    out_kept.wait()
    for gather in qkv_gathers:
        gather.pass_on()
    out_shards.start()
    row_gather.advance(1)
    up_gather.start()
    for table in tables:
        table.wait()
    for gather in qkv_gathers:
        gather.arrive()
    qkv_store = pltpu.make_async_copy(qkv_w, qkv_out, weight_stores.at[0])
    qkv_store.start()
    project(0)
    project(1)
    for step in range(2, ring.half + 1):
        row_gather.advance(step)
        if step == 2:
            gate_gather.pass_on()
        if step == ring.half:
            grad_gather.start()
            down_gather.start()
        project(step)

    blocks = seq_len // BLOCK

    def swap(head, number):
        other = others[number]
        lanes = pl.ds(head * HD, HD)
        return send_to(
            other,
            attended.at[span(other["seq"] * size, size), lanes],
            attended_own.at[:, span(ring.index * width + head * HD, HD)],
            swap_sems.at[0, head, number],
            swap_sems.at[1, head, number],
        )

    swap_kept = pltpu.make_async_copy(
        attended.at[span(ring.index * size, size)],
        attended_own.at[:, span(ring.index * width, width)],
        local.at[5],
    )
    for head in range(width // HD):
        lanes = slice(head * HD, (head + 1) * HD)
        for number in range(blocks):
            here, upto = pl.ds(number * BLOCK, BLOCK), pl.ds(0, (number + 1) * BLOCK)
            probs = softmax_block(queries[here, lanes], keys[upto, lanes], number * BLOCK, limit)
            attended[here, lanes] = dot(probs.astype(low), values[upto, lanes]).astype(low)
        for number in range(count - 1):
            swap(head, number).start()
    swap_kept.start()
    up_gather.pass_on()
    grad_gather.advance(1)
    out_shards.pass_on()
    out_shards.arrive()
    out_store = pltpu.make_async_copy(out_w, out_out, weight_stores.at[1])
    out_store.start()
    swap_kept.wait()
    for head in range(width // HD):
        for number in range(count - 1):
            swap(head, number).wait_recv()

    def out_project(tile, carry):
        lanes = span(tile * TILE, TILE)
        resid[:, lanes] = tokens[:, lanes].astype(full) + dot(attended_own[...], out_w[lanes, :], 1, 1)
        return carry

    lax.fori_loop(0, model // TILE, out_project, 0)
    rows = resid[...]
    factor = lax.rsqrt(jnp.mean(rows * rows, axis=-1, keepdims=True) + EPSILON)
    own[1] = (rows * factor * gain_rows[1:2, :]).astype(low)
    normed_gather = own_gather(own.at[1], normed_rows, normed_sems)
    normed_gather.start()
    normed_kept = own_kept(own.at[1], normed_rows, 6)
    normed_kept.start()

    def grad_loads(step):
        return [
            pltpu.make_async_copy(
                grad_own if step == 0 else grad_rows.at[span(owner * size, size)],
                grads.at[step % 2, pl.ds(side * size, size)],
                row_loads.at[step % 2, side],
            )
            for side, owner in enumerate(owners(step))
        ]

    def result_stores(step):
        results = []
        for side, owner in enumerate(owners(step)):
            here, there = pl.ds(side * size, size), span(owner * size, size)
            for number, place in enumerate((act_out, grad_gate_out, grad_up_out)):
                results.append(
                    pltpu.make_async_copy(hidden.at[number, here], place.at[there], stores.at[side, number])
                )
            results.append(pltpu.make_async_copy(back.at[here], partial.at[there], stores.at[side, 3]))
        return results

    def feed(step):
        for load in (*normed_loads(step, own.at[1], normed_rows), *grad_loads(step)):
            load.start()
        if step > 0:
            for store in result_stores(step - 1):
                store.wait()
        for load in (*normed_loads(step, own.at[1], normed_rows), *grad_loads(step)):
            load.wait()
        rows = pl.ds(0, size * len(owners(step)))
        slot = step % 2

        def forward(tile, carry):
            lanes = span(tile * TILE, TILE)
            gate = dot(normed[rows, :], gate_w[:, lanes])
            up = dot(normed[rows, :], up_w[:, lanes])
            grad_act = dot(grads[slot, rows, :], down_w[:, lanes])
            sigmoid = 1.0 / (1.0 + jnp.exp(-gate))
            silu = gate * sigmoid
            hidden[0, rows, lanes] = (silu * up).astype(low)
            hidden[1, rows, lanes] = (grad_act * up * sigmoid * (1.0 + gate * (1.0 - sigmoid))).astype(low)
            hidden[2, rows, lanes] = (grad_act * silu).astype(low)
            return carry

        lax.fori_loop(0, units // TILE, forward, 0)

        def backward(tile, carry):
            lanes = span(tile * TILE, TILE)
            total = dot(hidden[1, rows, :], gate_w[lanes, :], 1, 1) + dot(hidden[2, rows, :], up_w[lanes, :], 1, 1)
            back[rows, lanes] = total.astype(low)
            return carry

        lax.fori_loop(0, model // TILE, backward, 0)
        for store in result_stores(step):
            store.start()

    grad_gather.advance(2)
    down_gather.pass_on()
    gate_gather.arrive()
    up_gather.arrive()
    down_gather.arrive()
    down_store = pltpu.make_async_copy(down_w, down_out, weight_stores.at[2])
    down_store.start()
    feed(0)
    for step in range(3, ring.half + 1):
        grad_gather.advance(step)
    for step in range(1, ring.half + 1):
        normed_gather.advance(step)
        feed(step)
    for store in result_stores(ring.half):
        store.wait()
    for gather in (out_gather, row_gather, grad_gather, normed_gather):
        gather.finish()
    for gather in (*qkv_gathers, out_shards, gate_gather, up_gather, down_gather):
        gather.finish()
    for copy in (row_kept, grad_kept, normed_kept, qkv_store, out_store, down_store):
        copy.wait()
    for copy in gain_copies:
        copy.wait_send()
    for head in range(width // HD):
        for number in range(count - 1):
            swap(head, number).wait_send()


def forward(length, tokens, gains, cotangent, weights, tables, collective_id):
    count, shard_count = lax.axis_size("seq"), lax.axis_size("dp")
    size, model = tokens.shape
    seq_len, width, units = size * count, weights[0].shape[1], weights[4].shape[1]
    heads, hidden, rows = shape_of((seq_len, width), low), shape_of((seq_len, units), low), shape_of((size, model), low)
    all_rows = shape_of((seq_len, model), low)
    dma = pltpu.SemaphoreType.DMA
    return pl.pallas_call(
        functools.partial(forward_kernel, count, shard_count),
        out_shape=[
            shape_of((8, model), full),
            heads,
            heads,
            heads,
            rows,
            rows,
            shape_of((size, model), full),
            all_rows,
            all_rows,
            all_rows,
            shape_of((model, 3 * width), low),
            shape_of((model, model), low),
            shape_of((model, units), low),
            hidden,
            hidden,
            hidden,
            all_rows,
        ],
        in_specs=[SMEM] + [VMEM] * 3 + [ANY] * 9,
        out_specs=[VMEM] * 7 + [ANY] * 10,
        scratch_shapes=[
            pltpu.VMEM((shard_count, *gains.shape), low),
            pltpu.VMEM((model, 3 * width), low),
            pltpu.VMEM((model, model), low),
            *[pltpu.VMEM((model, units), low)] * 3,
            *[pltpu.VMEM((seq_len, HD), full)] * 2,
            pltpu.VMEM((2, size, model), low),
            pltpu.VMEM((seq_len, width), low),
            pltpu.VMEM((2 * size, model), low),
            pltpu.VMEM((2, 2 * size, model), low),
            pltpu.VMEM((3, 2 * size, units), low),
            pltpu.VMEM((2 * size, model), low),
            dma((2, shard_count - 1)),
            dma((7,)),
            dma((3, 2)),
            dma((2, 4)),
            dma((3,)),
            dma((2, width // HD, count - 1)),
            *ring_semaphores(count) * 4,
            *ShardGather.semaphores(shard_count) * 7,
        ],
        compiler_params=pltpu.CompilerParams(
            collective_id=collective_id, has_side_effects=True, vmem_limit_bytes=VMEM_LIMIT
        ),
        cost_estimate=pl.CostEstimate(flops=0, bytes_accessed=600_000_000, transcendentals=0),
    )(length, tokens, gains, cotangent, *weights, *tables)


def ffn_back_kernel(
    count,
    partial,
    normed_rows,
    grad_rows,
    act_in,
    grad_gate_in,
    grad_up_in,
    down_in,
    out_in,
    resid,
    grad_own,
    gain_rows,
    grad_gate_w,
    grad_up_w,
    grad_down_w,
    branch,
    grad_resid,
    grad_attn,
    gain_sum,
    grad_heads,
    hidden,
    down_w,
    out_w,
    tiles,
    staged,
    branch_tile,
    attended,
    loads,
    tile_loads,
    stores,
    swap_send,
    swap_recv,
    local,
    slots,
    terms,
    ring_send,
    ring_recv,
    term_loads,
):
    ring = Ring(count)
    size, model = resid.shape
    heads = grad_heads.shape[1]
    others = [{"seq": (ring.index + offset) % count} for offset in range(1, count)]
    inputs = [
        pltpu.make_async_copy(source, place, loads.at[number])
        for number, (source, place) in enumerate(
            (
                (grad_gate_in, hidden.at[1]),
                (grad_up_in, hidden.at[2]),
                (act_in, hidden.at[0]),
                (down_in, down_w),
                (out_in, out_w),
            )
        )
    ]
    greet(others)
    reduce = RingReduce(ring, row_piece(partial, size), slots, terms, ring_send, ring_recv, term_loads)
    reduce.start()

    def fetch(tile):
        lanes = span(tile * TILE, TILE)
        return [
            pltpu.make_async_copy(source.at[:, lanes], tiles.at[tile % 2, number], tile_loads.at[tile % 2, number])
            for number, source in enumerate((normed_rows, grad_rows))
        ]

    def store(tile):
        lanes, slot = span(tile * TILE, TILE), tile % 2
        copies = [
            pltpu.make_async_copy(staged.at[slot, number], place.at[lanes], stores.at[slot, number])
            for number, place in enumerate((grad_gate_w, grad_up_w, grad_down_w))
        ]
        copies.append(pltpu.make_async_copy(branch_tile.at[slot], branch.at[:, lanes], stores.at[slot, 3]))
        return copies

    count_tiles = model // TILE
    for copy in (inputs[0], *fetch(0), *inputs[1:]):
        copy.start()

    def weights(tile):
        slot = tile % 2
        if tile == 0:
            for copy in inputs[:4]:
                copy.wait()
        if tile + 1 < count_tiles:
            for copy in fetch(tile + 1):
                copy.start()
        if tile >= 2:
            for copy in store(tile - 2):
                copy.wait()
        for copy in fetch(tile):
            copy.wait()
        staged[slot, 0] = dot(tiles[slot, 0], hidden[1], 0, 0).astype(low)
        staged[slot, 1] = dot(tiles[slot, 0], hidden[2], 0, 0).astype(low)
        staged[slot, 2] = dot(tiles[slot, 1], hidden[0], 0, 0).astype(low)
        branch_tile[slot] = dot(hidden[0], down_w[pl.ds(tile * TILE, TILE), :], 1, 1).astype(low)
        for copy in store(tile):
            copy.start()

    tasks = [functools.partial(weights, tile) for tile in range(count_tiles)]
    weave(tasks, [*reduce.steps(), lambda: None])
    inputs[4].wait()
    gain_total = jnp.zeros((1, model), full)
    for part in range(PARTS):
        here = pl.ds(part * reduce.size, reduce.size)
        grad_normed, rows = reduce.total(part), resid[here, :]
        factor = lax.rsqrt(jnp.mean(rows * rows, axis=-1, keepdims=True) + EPSILON)
        weighted = grad_normed * gain_rows[1:2, :]
        inner = jnp.mean(weighted * rows, axis=-1, keepdims=True)
        grad = grad_own[here, :].astype(full) + factor * (weighted - rows * (factor * factor * inner))
        grad_resid[here, :] = grad
        grad_attn[here, :] = grad.astype(low)
        gain_total += jnp.sum(grad_normed * rows * factor, axis=0, keepdims=True)
    gain_sum[...] = jnp.broadcast_to(gain_total, gain_sum.shape)
    place = grad_heads.at[span(ring.index * size, size)]
    swaps = []
    for number, index in enumerate([other["seq"] for other in others] + [ring.index]):
        lanes = span(index * heads, heads)
        attended[:, lanes] = dot(grad_attn[...], out_w[:, lanes]).astype(low)
        if number < count - 1:
            swap = send_to(others[number], attended.at[:, lanes], place, swap_send.at[number], swap_recv.at[number])
        else:
            swap = pltpu.make_async_copy(attended.at[:, lanes], place, local)
        swap.start()
        swaps.append(swap)
    reduce.finish()
    for tile in (count_tiles - 2, count_tiles - 1):
        for copy in store(tile):
            copy.wait()
    for swap in swaps:
        swap.wait()


def ffn_back(partial, normed_rows, grad_rows, hidden, down_w, out_w, resid, grad_own, gain_rows, heads, collective_id):
    count = lax.axis_size("seq")
    size, model = resid.shape
    seq_len, units = hidden[0].shape
    grad_w = shape_of((model, units), low)
    return pl.pallas_call(
        functools.partial(ffn_back_kernel, count),
        out_shape=[
            grad_w,
            grad_w,
            grad_w,
            shape_of((seq_len, model), low),
            shape_of((size, model), full),
            shape_of((size, model), low),
            shape_of((8, model), full),
            shape_of((seq_len, heads), low),
        ],
        in_specs=[ANY] * 8 + [VMEM] * 3,
        out_specs=[ANY] * 4 + [VMEM] * 3 + [ANY],
        scratch_shapes=[
            pltpu.VMEM((3, seq_len, units), low),
            pltpu.VMEM(down_w.shape, low),
            pltpu.VMEM(out_w.shape, low),
            pltpu.VMEM((2, 2, seq_len, TILE), low),
            pltpu.VMEM((2, 3, TILE, units), low),
            pltpu.VMEM((2, seq_len, TILE), low),
            pltpu.VMEM((size, model), low),
            pltpu.SemaphoreType.DMA((5,)),
            pltpu.SemaphoreType.DMA((2, 2)),
            pltpu.SemaphoreType.DMA((2, 4)),
            pltpu.SemaphoreType.DMA((count - 1,)),
            pltpu.SemaphoreType.DMA((count - 1,)),
            pltpu.SemaphoreType.DMA,
            *RingReduce.scratch(count, size, model),
        ],
        compiler_params=pltpu.CompilerParams(
            collective_id=collective_id, has_side_effects=True, vmem_limit_bytes=VMEM_LIMIT
        ),
        cost_estimate=pl.CostEstimate(flops=0, bytes_accessed=300_000_000, transcendentals=0),
    )(partial, normed_rows, grad_rows, *hidden, down_w, out_w, resid, grad_own, gain_rows)


def attend_back_kernel(
    count,
    shard_count,
    length,
    grad_heads,
    queries,
    keys,
    values,
    cos_in,
    sin_in,
    rows_in,
    qkv_w,
    branch,
    resid,
    grad_attn,
    attended_own,
    unit_grad_w,
    output,
    partial,
    grad_w,
    gain_sum,
    out_sum,
    owned_w,
    cos,
    sin,
    weights,
    grads,
    sum_k,
    sum_v,
    row_tiles,
    staged,
    grad_staged,
    out_staged,
    out_beside,
    out_across,
    loads,
    tile_loads,
    stores,
    grad_stores,
    beside_sems,
    across_sems,
    slots,
    terms,
    ring_send,
    ring_recv,
    term_loads,
    *shard_scratch,
):
    ring, shards = Ring(count), Shards(shard_count)
    seq_len, width = queries.shape
    size, model = resid.shape
    blocks, tiles = seq_len // BLOCK, model // TILE
    scale = 1.0 / math.sqrt(HD)
    limit = length[0]
    inputs = [
        pltpu.make_async_copy(source, place, loads.at[number])
        for number, (source, place) in enumerate(
            (
                (cos_in, cos),
                (sin_in, sin),
                (qkv_w, weights),
            )
        )
    ]
    greet([*ring.next, *shards.greeted()])
    reduce = RingReduce(ring, row_piece(branch, size), slots, terms, ring_send, ring_recv, term_loads)
    reduce.start()
    shard_reduce = ShardReduce(shards, unit_grad_w, *shard_scratch)
    shard_reduce.start()
    for load in inputs:
        load.start()

    out_rows = model // shard_count

    def out_term(shard, lanes):
        return dot(grad_attn[:, span(shard * out_rows, out_rows)], attended_own[:, lanes], 0, 0)

    def beside(offset):
        return send_to(
            shards.sibling,
            out_staged.at[offset],
            out_beside.at[offset],
            beside_sems.at[0, offset],
            beside_sems.at[1, offset],
        )

    def across(offset):
        return send_to(
            {"dp": shards.device(shards.chip_at(offset), shards.core)},
            out_beside.at[offset],
            out_across.at[offset - 1],
            across_sems.at[0, offset],
            across_sems.at[1, offset],
        )

    offsets = [*range(1, shards.chips), 0]
    out_tile = 512

    def out_start(offset):
        shard = shards.device(shards.chip_at(offset), 1 - shards.core)

        def tile(number, carry):
            lanes = span(number * out_tile, out_tile)
            out_staged[offset, :, lanes] = out_term(shard, lanes).astype(low)
            return carry

        lax.fori_loop(0, model // out_tile, tile, 0)
        beside(offset).start()

    def out_middle(offset):
        shard = shards.device(shards.chip_at(offset), shards.core)
        beside(offset).wait_recv()

        def tile(number, carry):
            lanes = span(number * out_tile, out_tile)
            total = out_beside[offset, :, lanes].astype(full) + out_term(shard, lanes)
            out_beside[offset, :, lanes] = total.astype(low)
            return carry

        lax.fori_loop(0, model // out_tile, tile, 0)
        if offset:
            across(offset).start()

    def out_finish():
        for offset in range(1, shards.chips):
            across(offset).wait_recv()

        def tile(number, carry):
            lanes = span(number * out_tile, out_tile)
            total = out_beside[0, :, lanes].astype(full)
            for offset in range(1, shards.chips):
                total += out_across[offset - 1, :, lanes].astype(full)
            out_sum[:, lanes] = total.astype(low)
            return carry

        lax.fori_loop(0, model // out_tile, tile, 0)
        for offset in offsets:
            beside(offset).wait_send()
            if offset:
                across(offset).wait_send()

    def attend_block(head, number):
        lanes = slice(head * HD, (head + 1) * HD)
        here, upto = pl.ds(number * BLOCK, BLOCK), pl.ds(0, (number + 1) * BLOCK)
        if number == 0:
            sum_k[...] = jnp.zeros_like(sum_k)
            sum_v[...] = jnp.zeros_like(sum_v)
            if head == 0:
                for load in inputs[:2]:
                    load.wait()
        query_part, grad_part = queries[here, lanes], grad_heads[here, lanes]
        probs = softmax_block(query_part, keys[upto, lanes], number * BLOCK, limit)
        grad_probs = dot(grad_part, values[upto, lanes], 1, 1)
        inner = jnp.sum(probs * grad_probs, axis=-1, keepdims=True)
        grad_scores = (probs * (grad_probs - inner)).astype(low)
        sum_v[upto, :] += dot(probs.astype(low), grad_part, 0, 0)
        sum_k[upto, :] += dot(grad_scores, query_part, 0, 0)
        grad_query = dot(grad_scores, keys[upto, lanes]) * scale
        grads[here, lanes] = turned_back(grad_query, cos[here, :], sin[here, :]).astype(low)
        if number == blocks - 1:
            key_lanes = slice(width + head * HD, width + (head + 1) * HD)
            value_lanes = slice(2 * width + head * HD, 2 * width + (head + 1) * HD)
            grads[:, key_lanes] = turned_back(sum_k[...] * scale, cos[...], sin[...]).astype(low)
            grads[:, value_lanes] = sum_v[...].astype(low)

    def fetch(tile):
        return pltpu.make_async_copy(
            rows_in.at[:, pl.ds(tile * TILE, TILE)], row_tiles.at[tile % 2], tile_loads.at[tile % 2]
        )

    def store(number):
        return pltpu.make_async_copy(
            staged.at[number % 2], partial.at[pl.ds(number * BLOCK, BLOCK)], stores.at[number % 2]
        )

    def grad_store(tile):
        return pltpu.make_async_copy(
            grad_staged.at[tile % 2], grad_w.at[pl.ds(tile * TILE, TILE)], grad_stores.at[tile % 2]
        )

    def rows_back(number):
        if number == 0:
            for load in inputs[2:]:
                load.wait()
            fetch(0).start()
        if number >= 2:
            store(number - 2).wait()
        staged[number % 2] = dot(grads[pl.ds(number * BLOCK, BLOCK), :], weights[...], 1, 1).astype(low)
        store(number).start()

    def weights_back(tile):
        if tile + 1 < tiles:
            fetch(tile + 1).start()
        if tile >= 2:
            grad_store(tile - 2).wait()
        fetch(tile).wait()
        grad = dot(row_tiles[tile % 2], grads[...], 0, 0)
        grad_staged[tile % 2] = grad.astype(low)
        grad_store(tile).start()
        shared = grad * weights[pl.ds(tile * TILE, TILE), :].astype(full)
        gain_sum[:, pl.ds(tile * TILE, TILE)] = lax.dot_general(
            jnp.ones((8, shared.shape[1]), full),
            shared,
            (((1,), (1,)), ((), ())),
            precision=lax.Precision.HIGHEST,
            preferred_element_type=full,
        )

    def finish_output():
        for part in range(PARTS):
            here = pl.ds(part * reduce.size, reduce.size)
            position = (
                ring.index * size + part * reduce.size + lax.broadcasted_iota(jnp.int32, (reduce.size, model), 0)
            )
            total = resid[here, :] + reduce.total(part)
            output[here, :] = jnp.where(position < limit, total, 0.0).astype(low)

    tasks = [functools.partial(out_start, offset) for offset in offsets] + [shard_reduce.spread]
    attention = [
        functools.partial(attend_block, head, number) for head in range(width // HD) for number in range(blocks)
    ]
    tasks += attention[:2] + [functools.partial(out_middle, offset) for offset in offsets] + attention[2:]
    tasks += [functools.partial(rows_back, number) for number in range(blocks)]
    tasks += [functools.partial(weights_back, tile) for tile in range(tiles)]
    weave(tasks, [*reduce.steps(), lambda: None])
    for number in (blocks - 2, blocks - 1):
        store(number).wait()
    for tile in (tiles - 2, tiles - 1):
        grad_store(tile).wait()
    owned_w[...] = shard_reduce.total()
    out_finish()
    finish_output()
    reduce.finish()
    shard_reduce.finish()


def attend_back(
    length,
    grad_heads,
    queries,
    keys,
    values,
    tables,
    rows,
    qkv_w,
    branch,
    resid,
    grad_attn,
    attended_own,
    unit_grad_w,
    collective_id,
):
    count, shard_count = lax.axis_size("seq"), lax.axis_size("dp")
    seq_len, width = queries.shape
    size, model = resid.shape
    chips, out_rows, units = shard_count // CORES, model // shard_count, unit_grad_w.shape[1]
    return pl.pallas_call(
        functools.partial(attend_back_kernel, count, shard_count),
        out_shape=[
            shape_of((size, model), low),
            shape_of((seq_len, model), low),
            shape_of((model, 3 * width), low),
            shape_of((8, model), full),
            shape_of((out_rows, model), low),
            shape_of((out_rows, units), full),
        ],
        in_specs=[SMEM] + [VMEM] * 4 + [ANY] * 5 + [VMEM] * 3 + [ANY],
        out_specs=[VMEM, ANY, ANY, VMEM, VMEM, VMEM],
        scratch_shapes=[
            pltpu.VMEM((seq_len, HD), full),
            pltpu.VMEM((seq_len, HD), full),
            pltpu.VMEM((model, 3 * width), low),
            pltpu.VMEM((seq_len, 3 * width), low),
            pltpu.VMEM((seq_len, HD), full),
            pltpu.VMEM((seq_len, HD), full),
            pltpu.VMEM((2, seq_len, TILE), low),
            pltpu.VMEM((2, BLOCK, model), low),
            pltpu.VMEM((2, TILE, 3 * width), low),
            pltpu.VMEM((chips, out_rows, model), low),
            pltpu.VMEM((chips, out_rows, model), low),
            pltpu.VMEM((chips - 1, out_rows, model), low),
            pltpu.SemaphoreType.DMA((3,)),
            pltpu.SemaphoreType.DMA((2,)),
            pltpu.SemaphoreType.DMA((2,)),
            pltpu.SemaphoreType.DMA((2,)),
            pltpu.SemaphoreType.DMA((2, chips)),
            pltpu.SemaphoreType.DMA((2, chips)),
            *RingReduce.scratch(count, size, model),
            *ShardReduce.scratch(shard_count, out_rows, units),
        ],
        compiler_params=pltpu.CompilerParams(
            collective_id=collective_id, has_side_effects=True, vmem_limit_bytes=VMEM_LIMIT
        ),
        cost_estimate=pl.CostEstimate(flops=0, bytes_accessed=250_000_000, transcendentals=0),
    )(
        length,
        grad_heads,
        queries,
        keys,
        values,
        *tables,
        rows,
        qkv_w,
        branch,
        resid,
        grad_attn,
        attended_own,
        unit_grad_w,
    )


def last_kernel(
    count,
    shard_count,
    partial,
    grad_w,
    up_grad_w,
    down_grad_w,
    out_sum,
    tokens,
    gain_rows,
    grad_resid,
    gain_blocks,
    grad_tokens,
    grad_query_w,
    grad_key_w,
    grad_value_w,
    grad_out_w,
    grad_up_w,
    grad_down_w,
    gains,
    gain_slots,
    gain_sum,
    gain_shards,
    gain_sems,
    shard_gain_sems,
    *scratch,
):
    out_scratch, ring_scratch = scratch[:5], scratch[5:10]
    shard_scratch = grouped(scratch[10:], 6)
    ring, shards = Ring(count), Shards(shard_count)
    size = tokens.shape[0]
    rows, width = grad_out_w.shape
    others = [{"seq": (ring.index + offset) % count} for offset in range(1, count)]
    greet([*others, *shards.others()])

    def out_piece(index, part):
        piece = rows // PARTS
        return out_sum.at[pl.ds(part * piece, piece), span(index * width, width)]

    reduce = RingReduce(ring, row_piece(partial, size), *ring_scratch)
    out_reduce = RingReduce(ring, out_piece, *out_scratch)
    reduce.start()
    out_reduce.start()
    weights = [
        ShardReduce(shards, whole, *one) for whole, one in zip((up_grad_w, down_grad_w, grad_w), shard_scratch)
    ]
    gain_copies = [
        send_to(
            other,
            gain_blocks.at[other["seq"]],
            gain_slots.at[ring.index],
            gain_sems.at[0, number],
            gain_sems.at[1, number],
        )
        for number, other in enumerate(others)
    ]
    shard_gain_copies = [
        send_to(
            other, gain_sum, gain_shards.at[shards.index], shard_gain_sems.at[0, number], shard_gain_sems.at[1, number]
        )
        for number, other in enumerate(shards.others())
    ]
    for copy in gain_copies:
        copy.start()
    for weight in weights:
        weight.start()
    for weight in weights:
        weight.spread()
    gain_slots[ring.index] = gain_blocks[ring.index]
    for copy in gain_copies:
        copy.wait_recv()
    gain_sum[...] = jnp.sum(gain_slots[...], axis=0)
    for copy in shard_gain_copies:
        copy.start()

    def finish_gains():
        gain_shards[shards.index] = gain_sum[...]
        for copy in shard_gain_copies:
            copy.wait_recv()
        gains[...] = jnp.sum(gain_shards[...], axis=0)

    def finish_qkv():
        total = weights[2].total()
        for number, place in enumerate((grad_query_w, grad_key_w, grad_value_w)):
            place[...] = total[:, number * width : (number + 1) * width]

    def finish_up():
        grad_up_w[...] = weights[0].total()

    def finish_down():
        grad_down_w[...] = weights[1].total()

    out_steps, steps = out_reduce.steps(), reduce.steps()
    for number, step in enumerate(steps):
        out_steps[number]()
        step()
    finish_gains()
    finish_up()
    finish_down()
    finish_qkv()
    for part in range(PARTS):
        grad_out_w[pl.ds(part * out_reduce.size, out_reduce.size), :] = out_reduce.total(part)
    for part in range(PARTS):
        here = pl.ds(part * reduce.size, reduce.size)
        grad_normed, values = reduce.total(part), tokens[here, :].astype(full)
        factor = lax.rsqrt(jnp.mean(values * values, axis=-1, keepdims=True) + EPSILON)
        weighted = grad_normed * gain_rows[0:1, :]
        inner = jnp.mean(weighted * values, axis=-1, keepdims=True)
        grad_tokens[here, :] = grad_resid[here, :] + factor * (weighted - values * (factor * factor * inner))
    reduce.finish()
    out_reduce.finish()
    for weight in weights:
        weight.finish()
    for copy in (*gain_copies, *shard_gain_copies):
        copy.wait_send()


def last(partial, grad_w, up_grad_w, down_grad_w, out_sum, tokens, gain_rows, grad_resid, gain_blocks, collective_id):
    count, shard_count = lax.axis_size("seq"), lax.axis_size("dp")
    size = tokens.shape[0]
    rows, model = out_sum.shape
    width, units = model // count, up_grad_w.shape[1]
    block = gain_blocks.shape[1:]
    return pl.pallas_call(
        functools.partial(last_kernel, count, shard_count),
        out_shape=[
            shape_of(tokens.shape, full),
            *[shape_of((rows, width), full)] * 4,
            *[shape_of((rows, units), full)] * 2,
            shape_of(block, full),
        ],
        in_specs=[ANY] * 5 + [VMEM] * 4,
        out_specs=[VMEM] * 8,
        scratch_shapes=[
            pltpu.VMEM((count, *block), full),
            pltpu.VMEM(block, full),
            pltpu.VMEM((shard_count, *block), full),
            pltpu.SemaphoreType.DMA((2, count - 1)),
            pltpu.SemaphoreType.DMA((2, shard_count - 1)),
            *RingReduce.scratch(count, rows, width),
            *RingReduce.scratch(count, size, model),
            *ShardReduce.scratch(shard_count, rows, units),
            *ShardReduce.scratch(shard_count, rows, units),
            *ShardReduce.scratch(shard_count, rows, 3 * width),
        ],
        compiler_params=pltpu.CompilerParams(
            collective_id=collective_id, has_side_effects=True, vmem_limit_bytes=VMEM_LIMIT
        ),
        cost_estimate=pl.CostEstimate(flops=0, bytes_accessed=200_000_000, transcendentals=0),
    )(partial, grad_w, up_grad_w, down_grad_w, out_sum, tokens, gain_rows, grad_resid, gain_blocks)


def body(
    tokens,
    lengths,
    cotangent,
    w_query,
    w_key,
    w_value,
    w_out,
    w_gate,
    w_up,
    w_down,
    gain_attn,
    gain_ffn,
):
    seq_len = tokens.shape[0] * lax.axis_size("seq")
    head_width = w_query.shape[1]
    tables = rope_tables(seq_len)
    gains = jnp.concatenate(
        [gain_attn[None], gain_ffn[None], jnp.zeros((14, gain_attn.shape[0]), gain_attn.dtype)], axis=0
    )
    (
        gain_rows,
        queries,
        keys,
        values,
        grad_ffn,
        attended_tok,
        resid,
        full1,
        grad_full,
        full2,
        qkv_w,
        out_full,
        down_w,
        activation,
        grad_gate,
        grad_up,
        partial2,
    ) = forward(
        lengths, tokens, gains, cotangent, (w_query, w_key, w_value, w_out, w_gate, w_up, w_down), tables, 1
    )
    grad_w_gate, grad_w_up, grad_w_down, branch, grad_resid, grad_attn, gain_ffn_sum, grad_heads = ffn_back(
        partial2,
        full2,
        grad_full,
        (activation, grad_gate, grad_up),
        down_w,
        out_full,
        resid,
        grad_ffn,
        gain_rows,
        head_width,
        4,
    )
    output, partial1, grad_w, gain_attn_sum, out_sum, owned_gate = attend_back(
        lengths,
        grad_heads,
        queries,
        keys,
        values,
        tables,
        full1,
        qkv_w,
        branch,
        resid,
        grad_attn,
        attended_tok,
        grad_w_gate,
        5,
    )
    count, shard_count = lax.axis_size("seq"), lax.axis_size("dp")
    gain_sums = jnp.stack([gain_attn_sum[0] / gain_rows[0], gain_ffn_sum[0]])
    piece = gain_sums.shape[1] // (count * shard_count)
    gain_blocks = gain_sums.reshape(2, shard_count, count, piece).transpose(2, 1, 0, 3)
    gain_blocks = gain_blocks.reshape(count, shard_count, 2 * piece)
    gain_blocks = jnp.pad(gain_blocks, ((0, 0), (0, 8 - shard_count), (0, 128 - 2 * piece)))
    grad_tokens, owned_query, owned_key, owned_value, owned_out, owned_up, owned_down, owned_gains = last(
        partial1, grad_w, grad_w_up, grad_w_down, out_sum, tokens, gain_rows, grad_resid, gain_blocks, 6
    )
    owned_gains = lax.dynamic_index_in_dim(owned_gains, lax.axis_index("dp"), 0, keepdims=False)
    owned_gain_attn, owned_gain_ffn = owned_gains[:piece], owned_gains[piece : 2 * piece]
    return (
        output,
        grad_tokens,
        owned_query,
        owned_key,
        owned_value,
        owned_out,
        owned_gate,
        owned_up,
        owned_down,
        owned_gain_attn,
        owned_gain_ffn,
    )


def solution(mesh):
    rows, shard = P(("dp", "seq"), None), P("dp", "seq")
    gains = P(("dp", "seq"))
    return jax.shard_map(
        body,
        mesh=mesh,
        in_specs=(rows, P("dp"), rows, *[shard] * 7, P("dp"), P("dp")),
        out_specs=(rows, rows, *[shard] * 7, gains, gains),
        check_vma=False,
    )
```

```python
import functools
import math

import jax
import jax.numpy as jnp
import numpy as np
from jax import lax
from jax.experimental import pallas as pl
from jax.experimental.pallas import tpu as pltpu
from jax.sharding import PartitionSpec as P

HD = 128
WINDOW = 2048
EPSILON = 1e-05
NEGATIVE = -1e30
BLOCK = 256
TILE = 256
LINE = 4
CORES = 2
PARTS = 2
MESH = pl.DeviceIdType.MESH
VMEM_LIMIT = 60 * 1024 * 1024

ANY = pl.BlockSpec(memory_space=pl.ANY)
VMEM = pl.BlockSpec(memory_space=pltpu.VMEM)
SMEM = pl.BlockSpec(memory_space=pltpu.SMEM)
low = jnp.bfloat16
full = jnp.float32


def shape_of(shape, dtype):
    return jax.ShapeDtypeStruct(shape, dtype)


def span(start, size):
    if isinstance(start, int):
        return pl.ds(start, size)
    return pl.ds(pl.multiple_of(start, size), size)


def dot(left, right, left_dim=1, right_dim=0):
    return lax.dot_general(
        left, right, (((left_dim,), (right_dim,)), ((), ())), preferred_element_type=jnp.float32
    )


def greet(targets):
    barrier = pltpu.get_barrier_semaphore()
    for target in targets:
        pl.semaphore_signal(barrier, inc=1, device_id=target, device_id_type=MESH)
    pl.semaphore_wait(barrier, len(targets))


def send_to(target, source, place, send, recv):
    return pltpu.make_async_remote_copy(
        src_ref=source, dst_ref=place, send_sem=send, recv_sem=recv, device_id=target, device_id_type=MESH
    )


def weave(tasks, events):
    done = 0
    for number, task in enumerate(tasks):
        task()
        upto = (number + 1) * len(events) // len(tasks)
        for event in events[done:upto]:
            event()
        done = upto


def ring_index(place, count):
    columns = count // LINE
    column = place // LINE
    level = place % LINE
    odd = column % 2
    return (level + odd * (LINE - 1 - 2 * level)) * columns + column


def ring_place(index, count):
    columns = count // LINE
    level = index // columns
    column = index % columns
    odd = column % 2
    return column * LINE + level + odd * (LINE - 1 - 2 * level)


class Ring:
    def __init__(self, count):
        self.count = count
        self.half = count // 2
        self.index = lax.axis_index("seq")
        self.place = ring_place(self.index, count)
        self.next = ({"seq": self.shifted(1)}, {"seq": self.shifted(-1)})

    def shifted(self, offset):
        return ring_index((self.place + offset + self.count) % self.count, self.count)


def ring_semaphores(count):
    return [pltpu.SemaphoreType.DMA((2, count // 2, PARTS))] * 2


class RingGather:
    def __init__(self, ring, source, place, send, recv):
        self.ring, self.source, self.place = ring, source, place
        self.send, self.recv = send, recv

    def pieces(self, way, step):
        if step < self.ring.half - 1:
            return range(PARTS)
        return range(PARTS // 2) if way == 0 else range(PARTS // 2, PARTS)

    def copy(self, way, step, part):
        place = self.place(self.ring.shifted(step if way else -step), part)
        return send_to(
            self.ring.next[way],
            self.source(part) if step == 0 else place,
            place,
            self.send.at[way, step, part],
            self.recv.at[way, step, part],
        )

    def start(self):
        for part in range(PARTS):
            for way in range(2):
                if part in self.pieces(way, 0):
                    self.copy(way, 0, part).start()

    def advance(self, step):
        for part in range(PARTS):
            for way in range(2):
                if part in self.pieces(way, step - 1):
                    self.copy(way, step - 1, part).wait_recv()
                if step < self.ring.half and part in self.pieces(way, step):
                    self.copy(way, step, part).start()

    def finish(self):
        for step in range(self.ring.half):
            for way in range(2):
                for part in self.pieces(way, step):
                    self.copy(way, step, part).wait_send()

    def steps(self):
        return [functools.partial(self.advance, step) for step in range(1, self.ring.half + 1)]


class RingReduce:
    def __init__(self, ring, mine, slots, terms, send, recv, load):
        self.ring, self.mine, self.slots, self.terms = ring, mine, slots, terms
        self.send, self.recv, self.load = send, recv, load
        self.size = slots.shape[2] // PARTS

    @staticmethod
    def scratch(count, rows, width):
        return [
            pltpu.VMEM((2, count // 2, rows, width), low),
            pltpu.VMEM((2, 2, rows, width), low),
            *ring_semaphores(count),
            pltpu.SemaphoreType.DMA((2, 2, PARTS)),
        ]

    def pieces(self, way, step):
        if step > 0:
            return range(PARTS)
        return range(PARTS // 2) if way == 0 else range(PARTS // 2, PARTS)

    def summed(self, way, step):
        return self.pieces(way, 0) if step == 1 else range(PARTS)

    def target(self, way, step):
        left = self.ring.half - step
        return self.ring.shifted(-left if way else left)

    def slot(self, way, step, part):
        return self.slots.at[way, step, pl.ds(part * self.size, self.size)]

    def term(self, way, step, part):
        return self.terms.at[step % 2, way, pl.ds(part * self.size, self.size)]

    def fetch(self, way, step, part):
        return pltpu.make_async_copy(
            self.mine(self.target(way, step), part), self.term(way, step, part), self.load.at[step % 2, way, part]
        )

    def fetch_all(self, step):
        for part in range(PARTS):
            for way in range(2 if step < self.ring.half else 1):
                if part in self.summed(way, step):
                    self.fetch(way, step, part).start()

    def copy(self, way, step, part):
        alone = step == 0 or part not in self.summed(way, step)
        source = self.mine(self.target(way, step), part) if alone else self.slot(way, step - 1, part)
        return send_to(
            self.ring.next[way],
            source,
            self.slot(way, step, part),
            self.send.at[way, step, part],
            self.recv.at[way, step, part],
        )

    def start(self):
        for way in range(2):
            for part in self.pieces(way, 0):
                self.copy(way, 0, part).start()
        self.fetch_all(1)

    def advance(self, step):
        self.fetch_all(step + 1)
        order = [(way, part) for part in range(PARTS) for way in range(2)]
        for way, part in order:
            if part not in self.summed(way, step):
                self.copy(way, step, part).start()
        for way, part in order:
            if part in self.summed(way, step):
                self.fetch(way, step, part).wait()
                self.copy(way, step - 1, part).wait_recv()
                slot = self.slot(way, step - 1, part)
                total = slot[...].astype(full) + self.term(way, step, part)[...].astype(full)
                slot[...] = total.astype(slot.dtype)
                self.copy(way, step, part).start()

    def steps(self):
        return [functools.partial(self.advance, step) for step in range(1, self.ring.half)]

    def total(self, part):
        last = self.ring.half - 1
        self.fetch(0, last + 1, part).wait()
        for way in range(2):
            self.copy(way, last, part).wait_recv()
        return (
            self.term(0, last + 1, part)[...].astype(full)
            + self.slot(0, last, part)[...].astype(full)
            + self.slot(1, last, part)[...].astype(full)
        )

    def finish(self):
        for step in range(self.ring.half):
            for way in range(2):
                for part in self.pieces(way, step):
                    self.copy(way, step, part).wait_send()

    def free(self, sems):
        for way in range(2):
            pl.semaphore_signal(sems.at[way], inc=1, device_id=self.ring.next[way], device_id_type=MESH)

    def wait_free(self, sems):
        for way in range(2):
            pl.semaphore_wait(sems.at[way], 1)


def row_piece(ref, rows):
    size = rows // PARTS
    return lambda index, part: ref.at[span(index * rows + part * size, size)]


class Shards:
    def __init__(self, count):
        self.count = count
        self.chips = count // CORES
        self.index = lax.axis_index("dp")
        self.chip = self.index // CORES
        self.core = self.index % CORES
        self.sibling = {"dp": self.chip * CORES + 1 - self.core}

    def chip_at(self, offset):
        return (self.chip + offset) % self.chips

    def device(self, chip, core):
        return chip * CORES + core

    def others(self):
        return [{"dp": (self.index + offset) % self.count} for offset in range(1, self.count)]

    def greeted(self):
        return [self.sibling] + [
            {"dp": self.device(self.chip_at(offset), self.core)} for offset in range(1, self.chips)
        ]


class ShardGather:
    def __init__(self, shards, own, whole, send, recv, local):
        self.shards, self.own, self.whole = shards, own, whole
        self.send, self.recv, self.local = send, recv, local
        self.rows = whole.shape[0] // shards.count
        self.size = self.rows // PARTS

    @staticmethod
    def semaphores(count):
        shape = (2, count // CORES, PARTS)
        return [pltpu.SemaphoreType.DMA(shape), pltpu.SemaphoreType.DMA(shape), pltpu.SemaphoreType.DMA]

    def source(self, part):
        if self.own is None:
            return self.place(self.shards.index, part)
        return self.own.at[pl.ds(part * self.size, self.size)]

    def place(self, shard, part):
        return self.whole.at[span(shard * self.rows + part * self.size, self.size)]

    def across(self, offset, part):
        shards = self.shards
        target = {"dp": shards.device(shards.chip_at(offset), shards.core)}
        return send_to(
            target,
            self.source(part),
            self.place(shards.index, part),
            self.send.at[0, offset, part],
            self.recv.at[0, offset, part],
        )

    def beside(self, offset, part):
        shards = self.shards
        place = self.place(shards.device(shards.chip_at(shards.chips - offset), shards.core), part)
        return send_to(
            shards.sibling,
            place if offset else self.source(part),
            place,
            self.send.at[1, offset, part],
            self.recv.at[1, offset, part],
        )

    def keep(self):
        place = self.whole.at[span(self.shards.index * self.rows, self.rows)]
        return pltpu.make_async_copy(self.own, place, self.local)

    def start(self):
        for part in range(PARTS):
            for offset in range(1, self.shards.chips):
                self.across(offset, part).start()
            self.beside(0, part).start()
        if self.own is not None:
            self.keep().start()

    def pass_on(self):
        for part in range(PARTS):
            for offset in range(1, self.shards.chips):
                self.across(offset, part).wait_recv()
                self.beside(offset, part).start()

    def arrive(self):
        for part in range(PARTS):
            for offset in range(self.shards.chips):
                self.beside(offset, part).wait_recv()
        if self.own is not None:
            self.keep().wait()

    def finish(self):
        for part in range(PARTS):
            for offset in range(self.shards.chips):
                self.beside(offset, part).wait_send()
                if offset:
                    self.across(offset, part).wait_send()


class ShardReduce:
    def __init__(self, shards, whole, beside_slots, across_slots, work, loads, stores, beside_sems, across_sems):
        self.shards, self.whole = shards, whole
        self.beside_slots, self.across_slots = beside_slots, across_slots
        self.work, self.loads, self.stores = work, loads, stores
        self.beside_sems, self.across_sems = beside_sems, across_sems
        self.rows = whole.shape[0] // shards.count
        self.lanes = pl.ds(0, whole.shape[1])
        self.offsets = [*range(1, shards.chips), 0]

    def block(self, offset, core):
        shard = self.shards.device(self.shards.chip_at(offset), core)
        return self.whole.at[span(shard * self.rows, self.rows)]

    def beside(self, offset):
        return send_to(
            self.shards.sibling,
            self.block(offset, 1 - self.shards.core),
            self.beside_slots.at[offset],
            self.beside_sems.at[0, offset],
            self.beside_sems.at[1, offset],
        )

    def across(self, offset):
        return send_to(
            {"dp": self.shards.device(self.shards.chip_at(offset), self.shards.core)},
            self.beside_slots.at[offset],
            self.across_slots.at[offset - 1],
            self.across_sems.at[0, offset],
            self.across_sems.at[1, offset],
        )

    def fetches(self, offset):
        sources = (self.beside_slots.at[offset], self.block(offset, self.shards.core))
        return [
            pltpu.make_async_copy(source, self.work.at[offset, number, :, self.lanes], self.loads.at[offset, number])
            for number, source in enumerate(sources)
        ]

    def keep(self, offset):
        return pltpu.make_async_copy(
            self.work.at[offset, 0, :, self.lanes], self.beside_slots.at[offset], self.stores.at[offset]
        )

    def start(self):
        for offset in self.offsets:
            self.beside(offset).start()

    def load(self):
        for offset in self.offsets:
            self.beside(offset).wait_recv()
            for fetch in self.fetches(offset):
                fetch.start()

    def add(self):
        for offset in self.offsets:
            for fetch in self.fetches(offset):
                fetch.wait()
            total = self.work[offset, 0, :, self.lanes].astype(full) + self.work[offset, 1, :, self.lanes].astype(full)
            self.work[offset, 0, :, self.lanes] = total.astype(low)
            self.keep(offset).start()

    def stored(self):
        for offset in self.offsets:
            self.keep(offset).wait()

    def cross(self):
        for offset in self.offsets[:-1]:
            self.across(offset).start()

    def pass_on(self):
        self.stored()
        self.cross()

    def arrive(self):
        for offset in self.offsets[:-1]:
            self.across(offset).wait_recv()

    def finish(self):
        for offset in self.offsets:
            self.beside(offset).wait_send()
            if offset:
                self.across(offset).wait_send()


def grouped(refs, size):
    return [refs[number : number + size] for number in range(0, len(refs), size)]


def rope_tables(seq_len):
    half_dim = HD // 2
    steps = np.arange(half_dim, dtype=np.float32) * np.float32(2.0 / HD)
    frequency = np.exp(np.float32(-math.log(10000.0)) * steps)
    angles = np.arange(seq_len, dtype=np.float32)[:, None] * frequency[None, :]
    cos, sin = np.cos(angles), np.sin(angles)
    return (
        np.concatenate([cos, cos], axis=1).astype(np.float32),
        np.concatenate([-sin, sin], axis=1).astype(np.float32),
    )


def turned(values, cos, sin):
    return values * cos + pltpu.roll(values, HD // 2, 1) * sin


def turned_back(values, cos, sin):
    return values * cos - pltpu.roll(values, HD // 2, 1) * sin


def softmax_block(queries, keys, start, length):
    rows, count = queries.shape[0], keys.shape[0]
    scores = dot(queries, keys, 1, 1) * (1.0 / math.sqrt(HD))
    query_pos = start + lax.broadcasted_iota(jnp.int32, (rows, count), 0)
    key_pos = lax.broadcasted_iota(jnp.int32, (rows, count), 1)
    allowed = (key_pos <= query_pos) & (key_pos < length)
    if start + rows > WINDOW:
        allowed = allowed & (query_pos - key_pos < WINDOW)
    scores = jnp.where(allowed, scores, NEGATIVE)
    exponent = jnp.exp(scores - jnp.max(scores, axis=-1, keepdims=True))
    return exponent * (1.0 / jnp.sum(exponent, axis=-1, keepdims=True))


def forward_kernel(count, shard_count, *refs):
    (length, tokens, gains, cotangent, query_in, key_in, value_in, out_in, gate_in, up_in, down_in, cos_in, sin_in) = (
        refs[:13]
    )
    gain_rows, *results = refs[13:20]
    (all_rows, grad_rows, normed_rows, qkv_out, out_out, down_out, act_out, grad_gate_out, grad_up_out, partial) = (
        refs[20:30]
    )
    (all_gains, qkv_w, out_w, gate_w, up_w, down_w, cos, sin, own, attended, normed, grads, hidden, back) = refs[30:44]
    (gain_sems, local, row_loads, stores, weight_stores, swap_sems) = refs[44:50]
    queries, keys, values, grad_own, attended_own, resid, result_sems = refs[50:57]
    result_copies = [
        pltpu.make_async_copy(source, place, result_sems.at[number])
        for number, (source, place) in enumerate(
            zip((queries, keys, values, grad_own, attended_own, resid), results)
        )
    ]
    sems = refs[57:]
    out_sems, row_sems, grad_sems, normed_sems = grouped(sems[:8], 2)
    shard_sems = grouped(sems[8:], 3)

    ring, shards = Ring(count), Shards(shard_count)
    size, model = tokens.shape
    seq_len, width = queries.shape
    units = gate_w.shape[1]
    limit = length[0]
    others = [{"seq": (ring.index + offset) % count} for offset in range(1, count)]
    tables = [pltpu.make_async_copy(cos_in, cos, local.at[0]), pltpu.make_async_copy(sin_in, sin, local.at[1])]
    for table in tables:
        table.start()
    greet([*others, *shards.others()])

    out_rows, out_width = out_in.shape
    out_mine = out_w.at[span(shards.index * out_rows, out_rows)]
    out_piece = out_rows // PARTS
    out_gather = RingGather(
        ring,
        lambda part: out_in.at[pl.ds(part * out_piece, out_piece)],
        lambda index, part: out_w.at[
            span(shards.index * out_rows + part * out_piece, out_piece), span(index * out_width, out_width)
        ],
        *out_sems,
    )
    out_kept = pltpu.make_async_copy(out_in, out_mine.at[:, span(ring.index * out_width, out_width)], local.at[2])
    out_gather.start()
    out_kept.start()
    gain_copies = [
        send_to(target, gains, all_gains.at[shards.index], gain_sems.at[0, number], gain_sems.at[1, number])
        for number, target in enumerate(shards.others())
    ]
    for copy in gain_copies:
        copy.start()
    qkv_gathers = [
        ShardGather(shards, source, qkv_w.at[:, pl.ds(number * width, width)], *shard_sems[number])
        for number, source in enumerate((query_in, key_in, value_in))
    ]
    out_shards = ShardGather(shards, None, out_w, *shard_sems[3])
    gate_gather, up_gather, down_gather = (
        ShardGather(shards, source, whole, *shard_sems[4 + number])
        for number, (source, whole) in enumerate(((gate_in, gate_w), (up_in, up_w), (down_in, down_w)))
    )
    for gather in qkv_gathers:
        gather.start()

    piece = size // PARTS
    rows = tokens[...].astype(full)
    rows = rows * lax.rsqrt(jnp.mean(rows * rows, axis=-1, keepdims=True) + EPSILON)
    all_gains[shards.index] = gains[...]
    for copy in gain_copies:
        copy.wait_recv()
    gain_width = gains.shape[1]
    for shard in range(shard_count):
        gain_rows[:, shard * gain_width : (shard + 1) * gain_width] = all_gains[shard, :8, :].astype(full)
    own[0] = (rows * gain_rows[0:1, :]).astype(low)

    def own_gather(source, whole, pair):
        return RingGather(ring, lambda part: source.at[pl.ds(part * piece, piece)], row_piece(whole, size), *pair)

    def own_kept(source, whole, number):
        return pltpu.make_async_copy(source, whole.at[span(ring.index * size, size)], local.at[number])

    row_gather = own_gather(own.at[0], all_rows, row_sems)
    row_gather.start()
    row_kept = own_kept(own.at[0], all_rows, 3)
    row_kept.start()
    gate_gather.start()
    position = ring.index * size + lax.broadcasted_iota(jnp.int32, (size, model), 0)
    grad_own[...] = jnp.where(position < limit, cotangent[...].astype(full), 0.0).astype(low)
    grad_gather = own_gather(grad_own, grad_rows, grad_sems)
    grad_kept = own_kept(grad_own, grad_rows, 4)
    grad_kept.start()

    def owners(step):
        if step in (0, ring.half):
            return [ring.shifted(step)]
        return [ring.shifted(-step), ring.shifted(step)]

    def normed_loads(step, mine, whole):
        return [
            pltpu.make_async_copy(
                mine if step == 0 else whole.at[span(owner * size, size)],
                normed.at[pl.ds(side * size, size)],
                row_loads.at[2, side],
            )
            for side, owner in enumerate(owners(step))
        ]

    def project(step):
        loads = normed_loads(step, own.at[0], all_rows)
        for load in loads:
            load.start()
        for load in loads:
            load.wait()
        linear = dot(normed[pl.ds(0, size * len(loads)), :], qkv_w[...])
        for side, owner in enumerate(owners(step)):
            here = span(owner * size, size)
            side_cos, side_sin = cos[here, :], sin[here, :]
            for number, place in enumerate((queries, keys, values)):
                for head in range(width // HD):
                    lanes = slice(head * HD, (head + 1) * HD)
                    first = number * width + head * HD
                    one = linear[side * size : (side + 1) * size, first : first + HD]
                    if number < 2:
                        one = turned(one, side_cos, side_sin)
                    place[here, lanes] = one.astype(low)

    for step in out_gather.steps():
        step()
    out_kept.wait()
    for gather in qkv_gathers:
        gather.pass_on()
    out_shards.start()
    row_gather.advance(1)
    up_gather.start()
    for table in tables:
        table.wait()
    for gather in qkv_gathers:
        gather.arrive()
    qkv_store = pltpu.make_async_copy(qkv_w, qkv_out, weight_stores.at[0])
    qkv_store.start()
    project(0)
    project(1)
    for step in range(2, ring.half + 1):
        row_gather.advance(step)
        if step == 2:
            gate_gather.pass_on()
        if step == ring.half:
            grad_gather.start()
            down_gather.start()
        project(step)

    for copy in result_copies[:4]:
        copy.start()

    blocks = seq_len // BLOCK

    def swap(head, number):
        other = others[number]
        lanes = pl.ds(head * HD, HD)
        return send_to(
            other,
            attended.at[span(other["seq"] * size, size), lanes],
            attended_own.at[:, span(ring.index * width + head * HD, HD)],
            swap_sems.at[0, head, number],
            swap_sems.at[1, head, number],
        )

    swap_kept = pltpu.make_async_copy(
        attended.at[span(ring.index * size, size)],
        attended_own.at[:, span(ring.index * width, width)],
        local.at[5],
    )
    for head in range(width // HD):
        lanes = slice(head * HD, (head + 1) * HD)
        for number in range(blocks):
            here, upto = pl.ds(number * BLOCK, BLOCK), pl.ds(0, (number + 1) * BLOCK)
            probs = softmax_block(queries[here, lanes], keys[upto, lanes], number * BLOCK, limit)
            attended[here, lanes] = dot(probs.astype(low), values[upto, lanes]).astype(low)
        for number in range(count - 1):
            swap(head, number).start()
    swap_kept.start()
    up_gather.pass_on()
    grad_gather.advance(1)
    out_shards.pass_on()
    out_shards.arrive()
    out_store = pltpu.make_async_copy(out_w, out_out, weight_stores.at[1])
    out_store.start()
    swap_kept.wait()
    for head in range(width // HD):
        for number in range(count - 1):
            swap(head, number).wait_recv()

    def out_project(tile, carry):
        lanes = span(tile * TILE, TILE)
        resid[:, lanes] = tokens[:, lanes].astype(full) + dot(attended_own[...], out_w[lanes, :], 1, 1)
        return carry

    lax.fori_loop(0, model // TILE, out_project, 0)
    rows = resid[...]
    factor = lax.rsqrt(jnp.mean(rows * rows, axis=-1, keepdims=True) + EPSILON)
    own[1] = (rows * factor * gain_rows[1:2, :]).astype(low)
    for copy in result_copies[4:]:
        copy.start()
    normed_gather = own_gather(own.at[1], normed_rows, normed_sems)
    normed_gather.start()
    normed_kept = own_kept(own.at[1], normed_rows, 6)
    normed_kept.start()

    def grad_loads(step):
        return [
            pltpu.make_async_copy(
                grad_own if step == 0 else grad_rows.at[span(owner * size, size)],
                grads.at[step % 2, pl.ds(side * size, size)],
                row_loads.at[step % 2, side],
            )
            for side, owner in enumerate(owners(step))
        ]

    def result_stores(step):
        results = []
        for side, owner in enumerate(owners(step)):
            here, there = pl.ds(side * size, size), span(owner * size, size)
            for number, place in enumerate((act_out, grad_gate_out, grad_up_out)):
                results.append(
                    pltpu.make_async_copy(hidden.at[number, here], place.at[there], stores.at[side, number])
                )
            results.append(pltpu.make_async_copy(back.at[here], partial.at[there], stores.at[side, 3]))
        return results

    def feed(step):
        for load in (*normed_loads(step, own.at[1], normed_rows), *grad_loads(step)):
            load.start()
        if step > 0:
            for store in result_stores(step - 1):
                store.wait()
        for load in (*normed_loads(step, own.at[1], normed_rows), *grad_loads(step)):
            load.wait()
        rows = pl.ds(0, size * len(owners(step)))
        slot = step % 2

        def forward(tile, carry):
            lanes = span(tile * TILE, TILE)
            gate = dot(normed[rows, :], gate_w[:, lanes])
            up = dot(normed[rows, :], up_w[:, lanes])
            grad_act = dot(grads[slot, rows, :], down_w[:, lanes])
            sigmoid = 1.0 / (1.0 + jnp.exp(-gate))
            silu = gate * sigmoid
            hidden[0, rows, lanes] = (silu * up).astype(low)
            hidden[1, rows, lanes] = (grad_act * up * sigmoid * (1.0 + gate * (1.0 - sigmoid))).astype(low)
            hidden[2, rows, lanes] = (grad_act * silu).astype(low)
            return carry

        lax.fori_loop(0, units // TILE, forward, 0)

        def backward(tile, carry):
            lanes = span(tile * TILE, TILE)
            total = dot(hidden[1, rows, :], gate_w[lanes, :], 1, 1) + dot(hidden[2, rows, :], up_w[lanes, :], 1, 1)
            back[rows, lanes] = total.astype(low)
            return carry

        lax.fori_loop(0, model // TILE, backward, 0)
        for store in result_stores(step):
            store.start()

    grad_gather.advance(2)
    down_gather.pass_on()
    gate_gather.arrive()
    up_gather.arrive()
    down_gather.arrive()
    down_store = pltpu.make_async_copy(down_w, down_out, weight_stores.at[2])
    down_store.start()
    feed(0)
    for step in range(1, ring.half + 1):
        normed_gather.advance(step)
        if step + 2 <= ring.half:
            grad_gather.advance(step + 2)
        feed(step)
    for store in result_stores(ring.half):
        store.wait()
    for gather in (out_gather, row_gather, grad_gather, normed_gather):
        gather.finish()
    for gather in (*qkv_gathers, out_shards, gate_gather, up_gather, down_gather):
        gather.finish()
    for copy in (row_kept, grad_kept, normed_kept, qkv_store, out_store, down_store, *result_copies):
        copy.wait()
    for copy in gain_copies:
        copy.wait_send()
    for head in range(width // HD):
        for number in range(count - 1):
            swap(head, number).wait_send()


def forward(length, tokens, gains, cotangent, weights, tables, collective_id):
    count, shard_count = lax.axis_size("seq"), lax.axis_size("dp")
    size, model = tokens.shape
    seq_len, width, units = size * count, weights[0].shape[1], weights[4].shape[1]
    heads, hidden, rows = shape_of((seq_len, width), low), shape_of((seq_len, units), low), shape_of((size, model), low)
    all_rows = shape_of((seq_len, model), low)
    dma = pltpu.SemaphoreType.DMA
    return pl.pallas_call(
        functools.partial(forward_kernel, count, shard_count),
        out_shape=[
            shape_of((8, model), full),
            heads,
            heads,
            heads,
            rows,
            rows,
            shape_of((size, model), full),
            all_rows,
            all_rows,
            all_rows,
            shape_of((model, 3 * width), low),
            shape_of((model, model), low),
            shape_of((model, units), low),
            hidden,
            hidden,
            hidden,
            all_rows,
        ],
        in_specs=[SMEM] + [VMEM] * 3 + [ANY] * 9,
        out_specs=[VMEM] + [ANY] * 16,
        scratch_shapes=[
            pltpu.VMEM((shard_count, *gains.shape), low),
            pltpu.VMEM((model, 3 * width), low),
            pltpu.VMEM((model, model), low),
            *[pltpu.VMEM((model, units), low)] * 3,
            *[pltpu.VMEM((seq_len, HD), full)] * 2,
            pltpu.VMEM((2, size, model), low),
            pltpu.VMEM((seq_len, width), low),
            pltpu.VMEM((2 * size, model), low),
            pltpu.VMEM((2, 2 * size, model), low),
            pltpu.VMEM((3, 2 * size, units), low),
            pltpu.VMEM((2 * size, model), low),
            dma((2, shard_count - 1)),
            dma((7,)),
            dma((3, 2)),
            dma((2, 4)),
            dma((3,)),
            dma((2, width // HD, count - 1)),
            *[pltpu.VMEM((seq_len, width), low)] * 3,
            *[pltpu.VMEM((size, model), low)] * 2,
            pltpu.VMEM((size, model), full),
            dma((6,)),
            *ring_semaphores(count) * 4,
            *ShardGather.semaphores(shard_count) * 7,
        ],
        compiler_params=pltpu.CompilerParams(
            collective_id=collective_id, has_side_effects=True, vmem_limit_bytes=VMEM_LIMIT
        ),
        cost_estimate=pl.CostEstimate(flops=0, bytes_accessed=600_000_000, transcendentals=0),
    )(length, tokens, gains, cotangent, *weights, *tables)


def ffn_back_kernel(count, shard_count, *refs):
    (partial, normed_rows, grad_rows, act_in, grad_gate_in, grad_up_in, down_in, out_in) = refs[:8]
    resid_in, grad_own_in, gain_rows = refs[8:11]
    gain_sum, resid_out, attn_out, grad_heads, branch, gate_grad, up_grad, down_grad = refs[11:19]
    arrived = grouped(refs[19:23], 2)
    hidden, down_w, out_w, tiles, staged, branch_tile, attended, work = refs[23:31]
    loads, tile_loads, stores, swap_sems, local, work_loads, work_stores = refs[31:38]
    reduce_scratch = refs[38:43]
    resid, grad_own, grad_resid, grad_attn, result_sems = refs[43:48]
    shard_sems = grouped(refs[48:], 2)

    ring, shards = Ring(count), Shards(shard_count)
    size, model = resid.shape
    heads = grad_heads.shape[1]
    others = [{"seq": (ring.index + offset) % count} for offset in range(1, count)]
    inputs = [
        pltpu.make_async_copy(source, place, loads.at[number])
        for number, (source, place) in enumerate(
            (
                (grad_gate_in, hidden.at[1]),
                (grad_up_in, hidden.at[2]),
                (act_in, hidden.at[0]),
                (down_in, down_w),
                (out_in, out_w),
                (resid_in, resid),
                (grad_own_in, grad_own),
            )
        )
    ]
    greet([*others, *shards.greeted()])
    reduce = RingReduce(ring, row_piece(partial, size), *reduce_scratch)
    reduce.start()
    gate, up = (
        ShardReduce(shards, whole, *one, work, work_loads, work_stores, *sems)
        for whole, one, sems in zip((gate_grad, up_grad), arrived, shard_sems)
    )
    count_tiles = model // TILE

    terms = (
        (normed_rows, hidden.at[1], gate_grad, inputs[0]),
        (normed_rows, hidden.at[2], up_grad, inputs[1]),
        (grad_rows, hidden.at[0], down_grad, inputs[2]),
    )
    last = len(terms) * count_tiles - 1

    def fetch(tile):
        lanes = pl.ds(tile % count_tiles * TILE, TILE)
        source = terms[tile // count_tiles][0].at[:, lanes]
        return pltpu.make_async_copy(source, tiles.at[tile % 3], tile_loads.at[tile % 3])

    def store(tile):
        place = terms[tile // count_tiles][2].at[pl.ds(tile % count_tiles * TILE, TILE)]
        return pltpu.make_async_copy(staged.at[tile % 2], place, stores.at[tile % 2, 0])

    def branch_store(tile):
        return pltpu.make_async_copy(
            branch_tile.at[tile % 2], branch.at[:, pl.ds(tile * TILE, TILE)], stores.at[tile % 2, 1]
        )

    later = {0: inputs[1:2], 1: inputs[5:], count_tiles: inputs[2:3], count_tiles + 2: inputs[3:5]}
    for copy in (inputs[0], fetch(0), fetch(1)):
        copy.start()

    def weights(tile):
        for copy in later.get(tile, ()):
            copy.start()
        slot = tile % 2
        _, right, _, ready = terms[tile // count_tiles]
        if tile % count_tiles == 0:
            ready.wait()
        if tile + 2 <= last:
            fetch(tile + 2).start()
        if tile >= 2:
            store(tile - 2).wait()
        fetch(tile).wait()
        staged[slot] = dot(tiles[tile % 3], right[...], 0, 0).astype(low)
        store(tile).start()

    def branches(tile):
        slot = tile % 2
        if tile == 0:
            store(last - 1).wait()
            store(last).wait()
            inputs[3].wait()
        if tile >= 2:
            branch_store(tile - 2).wait()
        branch_tile[slot] = dot(hidden[0], down_w[pl.ds(tile * TILE, TILE), :], 1, 1).astype(low)
        branch_store(tile).start()

    steps = reduce.steps()
    tasks = [functools.partial(weights, tile) for tile in range(last + 1)]
    early = count_tiles * 3 // 4
    weave(tasks[:early], [])
    steps[0]()
    weave(tasks[early : count_tiles + 2], [])
    gate.start()
    weave(tasks[count_tiles + 2 : 2 * count_tiles + 2], [gate.load, gate.add, gate.pass_on, lambda: None])
    up.start()
    weave(tasks[2 * count_tiles + 2 :], [*steps[1:-1], up.load, up.add])
    tasks = [functools.partial(branches, tile) for tile in range(count_tiles)]
    weave(tasks, [up.pass_on, lambda: None, steps[-1]])
    for copy in inputs[4:]:
        copy.wait()
    gain_total = jnp.zeros((1, model), full)
    swaps = []
    for part in range(PARTS):
        here = pl.ds(part * reduce.size, reduce.size)
        there = grad_heads.at[span(ring.index * size + part * reduce.size, reduce.size)]
        grad_normed, rows = reduce.total(part), resid[here, :]
        factor = lax.rsqrt(jnp.mean(rows * rows, axis=-1, keepdims=True) + EPSILON)
        weighted = grad_normed * gain_rows[1:2, :]
        inner = jnp.mean(weighted * rows, axis=-1, keepdims=True)
        grad = grad_own[here, :].astype(full) + factor * (weighted - rows * (factor * factor * inner))
        grad_resid[here, :] = grad
        grad_attn[here, :] = grad.astype(low)
        gain_total += jnp.sum(grad_normed * rows * factor, axis=0, keepdims=True)
        for number, index in enumerate([other["seq"] for other in others] + [ring.index]):
            lanes = span(index * heads, heads)
            attended[here, lanes] = dot(grad_attn[here, :], out_w[:, lanes]).astype(low)
            source = attended.at[here, lanes]
            if number < count - 1:
                sems = (swap_sems.at[0, part, number], swap_sems.at[1, part, number])
                swap = send_to(others[number], source, there, *sems)
            else:
                swap = pltpu.make_async_copy(source, there, local.at[part])
            swap.start()
            swaps.append(swap)
    gain_sum[...] = jnp.broadcast_to(gain_total, gain_sum.shape)
    results = [
        pltpu.make_async_copy(grad_resid, resid_out, result_sems.at[0]),
        pltpu.make_async_copy(grad_attn, attn_out, result_sems.at[1]),
    ]
    for copy in results:
        copy.start()
    reduce.finish()
    for tile in (count_tiles - 2, count_tiles - 1):
        branch_store(tile).wait()
    for one in (gate, up):
        one.arrive()
        one.finish()
    for copy in (*swaps, *results):
        copy.wait()


def ffn_back(partial, normed_rows, grad_rows, hidden, down_w, out_w, resid, grad_own, gain_rows, heads, collective_id):
    count, shard_count = lax.axis_size("seq"), lax.axis_size("dp")
    size, model = resid.shape
    seq_len, units = hidden[0].shape
    chips, shard_rows = shard_count // CORES, model // shard_count
    grad_w = shape_of((model, units), low)
    dma = pltpu.SemaphoreType.DMA
    return pl.pallas_call(
        functools.partial(ffn_back_kernel, count, shard_count),
        out_shape=[
            shape_of((8, model), full),
            shape_of((size, model), full),
            shape_of((size, model), low),
            shape_of((seq_len, heads), low),
            shape_of((seq_len, model), low),
            grad_w,
            grad_w,
            grad_w,
            *[shape_of((number, shard_rows, units), low) for number in (chips, chips - 1)] * 2,
        ],
        in_specs=[ANY] * 10 + [VMEM],
        out_specs=[VMEM] + [ANY] * 11,
        scratch_shapes=[
            pltpu.VMEM((3, seq_len, units), low),
            pltpu.VMEM(down_w.shape, low),
            pltpu.VMEM(out_w.shape, low),
            pltpu.VMEM((3, seq_len, TILE), low),
            pltpu.VMEM((2, TILE, units), low),
            pltpu.VMEM((2, seq_len, TILE), low),
            pltpu.VMEM((size, model), low),
            pltpu.VMEM((chips, 2, shard_rows, units), low),
            dma((7,)),
            dma((3,)),
            dma((2, 2)),
            dma((2, PARTS, count - 1)),
            dma((PARTS,)),
            dma((chips, 2)),
            dma((chips,)),
            *RingReduce.scratch(count, size, model),
            pltpu.VMEM((size, model), full),
            pltpu.VMEM((size, model), low),
            pltpu.VMEM((size, model), full),
            pltpu.VMEM((size, model), low),
            dma((2,)),
            *[dma((2, chips))] * 4,
        ],
        compiler_params=pltpu.CompilerParams(
            collective_id=collective_id, has_side_effects=True, vmem_limit_bytes=VMEM_LIMIT
        ),
        cost_estimate=pl.CostEstimate(flops=0, bytes_accessed=300_000_000, transcendentals=0),
    )(partial, normed_rows, grad_rows, *hidden, down_w, out_w, resid, grad_own, gain_rows)


def attend_back_kernel(count, shard_count, *refs):
    length, *head_refs, cos_in, sin_in, rows_in, qkv_in, branch = refs[:10]
    *own_refs, gain_rows, gain_ffn_sum, down_grad = refs[10:16]
    output_out, grad_normed, grad_out_w, gain_total, partial, qkv_grad, out_left, out_right = refs[16:24]
    arrived = grouped(refs[24:32], 2)
    cos, sin, weights, grads, sum_k, sum_v, row_tiles, staged, grad_staged, work, out_sum = refs[32:43]
    loads, tile_loads, stores, grad_stores, work_loads, work_stores, out_loads_sem, free_sems = refs[43:51]
    gain_block, gain_shards, gain_part, gain_parts, gain_sems, gain_part_sems = refs[51:57]
    slots, terms, ring_send, ring_recv, term_loads, last_send, last_recv, last_loads = refs[57:65]
    out_scratch = refs[65:70]
    grad_heads, queries, keys, values, resid, grad_attn, attended_own, output = refs[70:78]
    shard_sems = grouped(refs[78:], 2)

    ring, shards = Ring(count), Shards(shard_count)
    seq_len, width = queries.shape
    size, model = resid.shape
    blocks, tiles = seq_len // BLOCK, model // TILE
    scale = 1.0 / math.sqrt(HD)
    limit = length[0]
    others = [{"seq": (ring.index + offset) % count} for offset in range(1, count)]
    inputs = [
        pltpu.make_async_copy(source, place, loads.at[number])
        for number, (source, place) in enumerate(
            (
                (cos_in, cos),
                (sin_in, sin),
                (qkv_in, weights),
                *zip(own_refs, (resid, grad_attn, attended_own)),
                *zip(head_refs, (grad_heads, queries, keys, values)),
            )
        )
    ]
    for load in inputs[4:6]:
        load.start()
    greet([*others, *shards.others()])
    reduce = RingReduce(ring, row_piece(branch, size), slots, terms, ring_send, ring_recv, term_loads)
    last = RingReduce(ring, row_piece(partial, size), slots, terms, last_send, last_recv, last_loads)
    reduce.start()
    shard_reduces = [
        ShardReduce(shards, whole, *one, work, work_loads, work_stores, *sems)
        for whole, one, sems in zip((out_left, out_right, down_grad, qkv_grad), arrived, shard_sems)
    ]
    left, right, down, qkv = shard_reduces

    half = model // 2

    def out_store(tile):
        rows = pl.ds(tile * TILE, TILE)
        return [
            pltpu.make_async_copy(
                staged.at[tile % 2, :, pl.ds(side * half, half)], whole.at[rows], stores.at[tile % 2, side]
            )
            for side, whole in enumerate((out_left, out_right))
        ]

    def out_back(tile):
        if tile >= 2:
            for copy in out_store(tile - 2):
                copy.wait()
        staged[tile % 2] = dot(grad_attn[:, pl.ds(tile * TILE, TILE)], attended_own[...], 0, 0).astype(low)
        for copy in out_store(tile):
            copy.start()

    def out_spread():
        for tile in (tiles - 2, tiles - 1):
            for copy in out_store(tile):
                copy.wait()
        left.start()
        right.start()

    def attend_block(head, number):
        lanes = slice(head * HD, (head + 1) * HD)
        here, upto = pl.ds(number * BLOCK, BLOCK), pl.ds(0, (number + 1) * BLOCK)
        if number == 0:
            sum_k[...] = jnp.zeros_like(sum_k)
            sum_v[...] = jnp.zeros_like(sum_v)
            if head == 0:
                for load in (*inputs[:2], *inputs[6:]):
                    load.wait()
        query_part, grad_part = queries[here, lanes], grad_heads[here, lanes]
        probs = softmax_block(query_part, keys[upto, lanes], number * BLOCK, limit)
        grad_probs = dot(grad_part, values[upto, lanes], 1, 1)
        inner = jnp.sum(probs * grad_probs, axis=-1, keepdims=True)
        grad_scores = (probs * (grad_probs - inner)).astype(low)
        sum_v[upto, :] += dot(probs.astype(low), grad_part, 0, 0)
        sum_k[upto, :] += dot(grad_scores, query_part, 0, 0)
        grad_query = dot(grad_scores, keys[upto, lanes]) * scale
        grads[here, lanes] = turned_back(grad_query, cos[here, :], sin[here, :]).astype(low)
        if number == blocks - 1:
            key_lanes = slice(width + head * HD, width + (head + 1) * HD)
            value_lanes = slice(2 * width + head * HD, 2 * width + (head + 1) * HD)
            grads[:, key_lanes] = turned_back(sum_k[...] * scale, cos[...], sin[...]).astype(low)
            grads[:, value_lanes] = sum_v[...].astype(low)

    def fetch(tile):
        return pltpu.make_async_copy(
            rows_in.at[:, pl.ds(tile * TILE, TILE)], row_tiles.at[tile % 2], tile_loads.at[tile % 2]
        )

    def store(number):
        return pltpu.make_async_copy(
            staged.at[number % 2], partial.at[pl.ds(number * BLOCK, BLOCK)], stores.at[number % 2, 0]
        )

    def grad_store(tile):
        return pltpu.make_async_copy(
            grad_staged.at[tile % 2], qkv_grad.at[pl.ds(tile * TILE, TILE)], grad_stores.at[tile % 2]
        )

    def rows_back(number):
        if number == 0:
            inputs[2].wait()
            fetch(0).start()
        if number >= 2:
            store(number - 2).wait()
        staged[number % 2] = dot(grads[pl.ds(number * BLOCK, BLOCK), :], weights[...], 1, 1).astype(low)
        store(number).start()

    def weights_back(tile):
        if tile + 1 < tiles:
            fetch(tile + 1).start()
        if tile >= 2:
            grad_store(tile - 2).wait()
        fetch(tile).wait()
        grad = dot(row_tiles[tile % 2], grads[...], 0, 0)
        grad_staged[tile % 2] = grad.astype(low)
        grad_store(tile).start()
        lanes = pl.ds(tile * TILE, TILE)
        product = grad * weights[lanes, :].astype(full)
        shared = product[:, :HD]
        for first in range(HD, product.shape[1], HD):
            shared += product[:, first : first + HD]
        gain = lax.dot_general(
            jnp.ones((8, shared.shape[1]), full),
            shared,
            (((1,), (1,)), ((), ())),
            precision=lax.Precision.HIGHEST,
            preferred_element_type=full,
        )
        row = lax.broadcasted_iota(jnp.int32, gain.shape, 0)
        gain_block[:, lanes] = jnp.where(row == 0, gain / gain_rows[0:1, lanes], gain_ffn_sum[:, lanes])

    gain_width = model // shard_count
    gain_copies = [
        send_to(
            other,
            gain_block.at[:, span(other["dp"] * gain_width, gain_width)],
            gain_shards.at[shards.index],
            gain_sems.at[0, number],
            gain_sems.at[1, number],
        )
        for number, other in enumerate(shards.others())
    ]
    gain_part_copies = [
        send_to(
            other, gain_part, gain_parts.at[ring.index], gain_part_sems.at[0, number], gain_part_sems.at[1, number]
        )
        for number, other in enumerate(others)
    ]

    def gains_start():
        for copy in gain_copies:
            copy.start()

    def gains_middle():
        gain_shards[shards.index] = gain_block[:, span(shards.index * gain_width, gain_width)]
        for copy in gain_copies:
            copy.wait_recv()
        gain_part[...] = jnp.sum(gain_shards[...], axis=0)
        for copy in gain_part_copies:
            copy.start()

    def gains_end():
        gain_parts[ring.index] = gain_part[...]
        for copy in gain_part_copies:
            copy.wait_recv()
        gain_total[...] = jnp.sum(gain_parts[...], axis=0)
        for copy in (*gain_copies, *gain_part_copies):
            copy.wait_send()

    def out_loads(side):
        one = shard_reduces[side]
        lanes = pl.ds(side * half, half)
        copies = [pltpu.make_async_copy(one.beside_slots.at[0], out_sum.at[:, lanes], out_loads_sem.at[0])]
        copies += [
            pltpu.make_async_copy(
                one.across_slots.at[offset - 1], work.at[offset, 0, :, one.lanes], out_loads_sem.at[offset]
            )
            for offset in range(1, shards.chips)
        ]
        return copies

    def out_close(side):
        one = shard_reduces[side]
        lanes = pl.ds(side * half, half)
        one.arrive()
        for copy in out_loads(side):
            copy.start()
        for copy in out_loads(side):
            copy.wait()
        total = out_sum[:, lanes].astype(full)
        for offset in range(1, shards.chips):
            total += work[offset, 0, :, one.lanes].astype(full)
        out_sum[:, lanes] = total.astype(low)

    rows, out_width = grad_out_w.shape

    def out_piece(index, part):
        piece = rows // PARTS
        return out_sum.at[pl.ds(part * piece, piece), span(index * out_width, out_width)]

    out_reduce = RingReduce(ring, out_piece, *out_scratch)
    for load in (*inputs[6:], *inputs[:4]):
        load.start()
    for load in inputs[4:6]:
        load.wait()
    for tile in range(tiles):
        out_back(tile)
    out_spread()
    attention = [
        functools.partial(attend_block, head, number) for head in range(width // HD) for number in range(blocks)
    ]
    steps = reduce.steps()
    steps[0]()
    weave(attention, [left.load, left.add, left.pass_on, right.load, right.add, right.pass_on, *steps[1:-2]])
    down.start()
    projections = [functools.partial(rows_back, number) for number in range(blocks)]
    projections += [functools.partial(weights_back, tile) for tile in range(tiles)]
    weave(projections, [down.load, steps[-2], down.add, down.stored])
    for number in (blocks - 2, blocks - 1):
        store(number).wait()
    for tile in (tiles - 2, tiles - 1):
        grad_store(tile).wait()
    qkv.start()
    gains_start()
    steps[-1]()
    for event in (qkv.load, qkv.add, gains_middle, qkv.stored):
        event()
    inputs[3].wait()
    for part in range(PARTS):
        here = pl.ds(part * reduce.size, reduce.size)
        position = ring.index * size + part * reduce.size + lax.broadcasted_iota(jnp.int32, (reduce.size, model), 0)
        total = resid[here, :] + reduce.total(part)
        output[here, :] = jnp.where(position < limit, total, 0.0).astype(low)
    output_store = pltpu.make_async_copy(output, output_out, out_loads_sem.at[shards.chips])
    output_store.start()
    reduce.finish()
    reduce.free(free_sems)
    last.wait_free(free_sems)
    last.start()
    for side in range(2):
        out_close(side)
    out_reduce.start()
    down.cross()
    qkv.cross()
    for step in range(1, ring.half):
        out_reduce.advance(step)
        last.advance(step)
    gains_end()
    for part in range(PARTS):
        grad_out_w[pl.ds(part * out_reduce.size, out_reduce.size), :] = out_reduce.total(part)
    for part in range(PARTS):
        grad_normed[pl.ds(part * last.size, last.size), :] = last.total(part)
    for one in (down, qkv):
        one.arrive()
    for one in (*shard_reduces, last, out_reduce):
        one.finish()
    output_store.wait()


def attend_back(
    length, grad_heads, heads, tables, rows, qkv_w, branch, sums, gain_rows, gain_ffn_sum, down_grad, collective_id
):
    count, shard_count = lax.axis_size("seq"), lax.axis_size("dp")
    resid, grad_attn, attended_own = sums
    seq_len, width = grad_heads.shape
    size, model = resid.shape
    chips, shard_rows, units = shard_count // CORES, model // shard_count, down_grad.shape[1]
    half, gain_width = model // 2, model // shard_count
    widths = (half, half, units, 3 * width)
    dma = pltpu.SemaphoreType.DMA
    arrivals = [
        shape_of((number, shard_rows, one), low) for one in widths for number in (chips, max(chips - 1, 1))
    ]
    out_width = model // count
    return pl.pallas_call(
        functools.partial(attend_back_kernel, count, shard_count),
        out_shape=[
            shape_of((size, model), low),
            shape_of((size, model), full),
            shape_of((shard_rows, out_width), full),
            shape_of((8, gain_width), full),
            shape_of((seq_len, model), low),
            shape_of((model, 3 * width), low),
            shape_of((model, half), low),
            shape_of((model, half), low),
            *arrivals,
        ],
        in_specs=[SMEM] + [ANY] * 12 + [VMEM] * 2 + [ANY],
        out_specs=[ANY] + [VMEM] * 3 + [ANY] * (4 + len(arrivals)),
        scratch_shapes=[
            *[pltpu.VMEM((seq_len, HD), full)] * 2,
            pltpu.VMEM((model, 3 * width), low),
            pltpu.VMEM((seq_len, 3 * width), low),
            *[pltpu.VMEM((seq_len, HD), full)] * 2,
            pltpu.VMEM((2, seq_len, TILE), low),
            pltpu.VMEM((2, BLOCK, model), low),
            pltpu.VMEM((2, TILE, 3 * width), low),
            pltpu.VMEM((chips, 2, shard_rows, max(widths)), low),
            pltpu.VMEM((shard_rows, model), low),
            dma((10,)),
            dma((2,)),
            dma((2, 2)),
            dma((2,)),
            dma((chips, 2)),
            dma((chips,)),
            dma((chips + 1,)),
            pltpu.SemaphoreType.REGULAR((2,)),
            pltpu.VMEM((8, model), full),
            pltpu.VMEM((shard_count, 8, gain_width), full),
            pltpu.VMEM((8, gain_width), full),
            pltpu.VMEM((count, 8, gain_width), full),
            dma((2, shard_count - 1)),
            dma((2, count - 1)),
            *RingReduce.scratch(count, size, model),
            *RingReduce.scratch(count, size, model)[2:],
            *RingReduce.scratch(count, shard_rows, out_width),
            *[pltpu.VMEM((seq_len, width), low)] * 4,
            pltpu.VMEM((size, model), full),
            *[pltpu.VMEM((size, model), low)] * 3,
            *[dma((2, chips))] * (2 * len(widths)),
        ],
        compiler_params=pltpu.CompilerParams(
            collective_id=collective_id, has_side_effects=True, vmem_limit_bytes=VMEM_LIMIT
        ),
        cost_estimate=pl.CostEstimate(flops=0, bytes_accessed=500_000_000, transcendentals=0),
    )(length, grad_heads, *heads, *tables, rows, qkv_w, branch, *sums, gain_rows, gain_ffn_sum, down_grad)


def settle_kernel(count_weights, *refs):
    pairs = grouped(refs[: 2 * count_weights], 2)
    grad_normed, tokens, gain_rows, grad_resid, output_in, grad_out_in = refs[2 * count_weights : 2 * count_weights + 6]
    output, grad_tokens, grad_out, *owned = refs[2 * count_weights + 6 :]

    def total(pair):
        beside, across = pair
        return beside[0].astype(full) + jnp.sum(across[...].astype(full), axis=0)

    output[...] = output_in[...]
    grad_out[...] = grad_out_in[...]
    for place, pair in zip(owned, pairs[:-1]):
        place[...] = total(pair)
    qkv = total(pairs[-1])
    for number, place in enumerate(owned[-3:]):
        width = place.shape[1]
        place[...] = qkv[:, number * width : (number + 1) * width]
    values = tokens[...].astype(full)
    factor = lax.rsqrt(jnp.mean(values * values, axis=-1, keepdims=True) + EPSILON)
    weighted = grad_normed[...] * gain_rows[0:1, :]
    inner = jnp.mean(weighted * values, axis=-1, keepdims=True)
    grad_tokens[...] = grad_resid[...] + factor * (weighted - values * (factor * factor * inner))


def settle(pairs, grad_normed, tokens, gain_rows, grad_resid, output, grad_out, width):
    steps = 4
    size, model = tokens.shape
    rows = grad_out.shape[0]

    def cut(array):
        return pl.BlockSpec((array.shape[0] // steps, array.shape[1]), lambda step: (step, 0))

    def whole(array):
        return pl.BlockSpec(array.shape, lambda step: (0, 0))

    pair_specs = []
    for beside, across in pairs:
        pair_specs.append(pl.BlockSpec((1, rows // steps, beside.shape[2]), lambda step: (0, step, 0)))
        pair_specs.append(
            pl.BlockSpec((across.shape[0], rows // steps, across.shape[2]), lambda step: (0, step, 0))
        )
    outs = [
        shape_of((size, model), low),
        shape_of((size, model), full),
        shape_of(grad_out.shape, full),
        *[shape_of((rows, beside.shape[2]), full) for beside, _ in pairs[:-1]],
        *[shape_of((rows, width), full)] * 3,
    ]
    return pl.pallas_call(
        functools.partial(settle_kernel, len(pairs)),
        grid=(steps,),
        out_shape=outs,
        in_specs=[
            *pair_specs,
            cut(grad_normed),
            cut(tokens),
            whole(gain_rows),
            cut(grad_resid),
            cut(output),
            cut(grad_out),
        ],
        out_specs=[cut(out) for out in outs],
        compiler_params=pltpu.CompilerParams(vmem_limit_bytes=VMEM_LIMIT),
    )(
        *[one for pair in pairs for one in pair],
        grad_normed,
        tokens,
        gain_rows,
        grad_resid,
        output,
        grad_out,
    )


def body(
    tokens,
    lengths,
    cotangent,
    w_query,
    w_key,
    w_value,
    w_out,
    w_gate,
    w_up,
    w_down,
    gain_attn,
    gain_ffn,
):
    seq_len = tokens.shape[0] * lax.axis_size("seq")
    head_width = w_query.shape[1]
    tables = rope_tables(seq_len)
    gains = jnp.concatenate(
        [gain_attn[None], gain_ffn[None], jnp.zeros((14, gain_attn.shape[0]), gain_attn.dtype)], axis=0
    )
    (
        gain_rows,
        queries,
        keys,
        values,
        grad_ffn,
        attended_tok,
        resid,
        full1,
        grad_full,
        full2,
        qkv_w,
        out_full,
        down_w,
        activation,
        grad_gate,
        grad_up,
        partial2,
    ) = forward(
        lengths, tokens, gains, cotangent, (w_query, w_key, w_value, w_out, w_gate, w_up, w_down), tables, 1
    )
    gain_ffn_sum, grad_resid, grad_attn, grad_heads, branch, _, _, grad_w_down, *gate_up = ffn_back(
        partial2,
        full2,
        grad_full,
        (activation, grad_gate, grad_up),
        down_w,
        out_full,
        resid,
        grad_ffn,
        gain_rows,
        head_width,
        2,
    )
    output, grad_normed1, owned_out, gain_sums, _, _, _, _, *arrived = attend_back(
        lengths,
        grad_heads,
        (queries, keys, values),
        tables,
        full1,
        qkv_w,
        branch,
        (resid, grad_attn, attended_tok),
        gain_rows,
        gain_ffn_sum,
        grad_w_down,
        3,
    )
    output, grad_tokens, owned_out, owned_gate, owned_up, owned_down, owned_query, owned_key, owned_value = settle(
        grouped([*gate_up, *arrived[4:]], 2), grad_normed1, tokens, gain_rows, grad_resid, output, owned_out, head_width
    )
    piece = gain_sums.shape[1] // lax.axis_size("seq")
    owned_gains = lax.dynamic_slice_in_dim(gain_sums, lax.axis_index("seq") * piece, piece, axis=1)
    owned_gain_attn, owned_gain_ffn = owned_gains[0], owned_gains[1]
    return (
        output,
        grad_tokens,
        owned_query,
        owned_key,
        owned_value,
        owned_out,
        owned_gate,
        owned_up,
        owned_down,
        owned_gain_attn,
        owned_gain_ffn,
    )


def solution(mesh):
    rows, shard = P(("dp", "seq"), None), P("dp", "seq")
    gains = P(("dp", "seq"))
    return jax.shard_map(
        body,
        mesh=mesh,
        in_specs=(rows, P("dp"), rows, *[shard] * 7, P("dp"), P("dp")),
        out_specs=(rows, rows, *[shard] * 7, gains, gains),
        check_vma=False,
    )
```

```python
import functools
import math

import jax
import jax.numpy as jnp
import numpy as np
from jax import lax
from jax.experimental import pallas as pl
from jax.experimental.pallas import tpu as pltpu
from jax.sharding import PartitionSpec as P

HD = 128
WINDOW = 2048
EPSILON = 1e-05
NEGATIVE = -1e30
BLOCK = 256
TILE = 256
LINE = 4
CORES = 2
PARTS = 2
MESH = pl.DeviceIdType.MESH
VMEM_LIMIT = 60 * 1024 * 1024

ANY = pl.BlockSpec(memory_space=pl.ANY)
VMEM = pl.BlockSpec(memory_space=pltpu.VMEM)
SMEM = pl.BlockSpec(memory_space=pltpu.SMEM)
low = jnp.bfloat16
full = jnp.float32


def shape_of(shape, dtype):
    return jax.ShapeDtypeStruct(shape, dtype)


def span(start, size):
    if isinstance(start, int):
        return pl.ds(start, size)
    return pl.ds(pl.multiple_of(start, size), size)


def dot(left, right, left_dim=1, right_dim=0):
    return lax.dot_general(
        left, right, (((left_dim,), (right_dim,)), ((), ())), preferred_element_type=jnp.float32
    )


def greet(targets):
    barrier = pltpu.get_barrier_semaphore()
    for target in targets:
        pl.semaphore_signal(barrier, inc=1, device_id=target, device_id_type=MESH)
    pl.semaphore_wait(barrier, len(targets))


def send_to(target, source, place, send, recv):
    return pltpu.make_async_remote_copy(
        src_ref=source, dst_ref=place, send_sem=send, recv_sem=recv, device_id=target, device_id_type=MESH
    )


def weave(tasks, events):
    done = 0
    for number, task in enumerate(tasks):
        task()
        upto = (number + 1) * len(events) // len(tasks)
        for event in events[done:upto]:
            event()
        done = upto


def ring_index(place, count):
    columns = count // LINE
    column = place // LINE
    level = place % LINE
    odd = column % 2
    return (level + odd * (LINE - 1 - 2 * level)) * columns + column


def ring_place(index, count):
    columns = count // LINE
    level = index // columns
    column = index % columns
    odd = column % 2
    return column * LINE + level + odd * (LINE - 1 - 2 * level)


class Ring:
    def __init__(self, count):
        self.count = count
        self.half = count // 2
        self.index = lax.axis_index("seq")
        self.place = ring_place(self.index, count)
        self.next = ({"seq": self.shifted(1)}, {"seq": self.shifted(-1)})

    def shifted(self, offset):
        return ring_index((self.place + offset + self.count) % self.count, self.count)


def ring_semaphores(count):
    return [pltpu.SemaphoreType.DMA((2, count // 2, PARTS))] * 2


class RingGather:
    def __init__(self, ring, source, place, send, recv):
        self.ring, self.source, self.place = ring, source, place
        self.send, self.recv = send, recv

    def pieces(self, way, step):
        if step < self.ring.half - 1:
            return range(PARTS)
        return range(PARTS // 2) if way == 0 else range(PARTS // 2, PARTS)

    def copy(self, way, step, part):
        place = self.place(self.ring.shifted(step if way else -step), part)
        return send_to(
            self.ring.next[way],
            self.source(part) if step == 0 else place,
            place,
            self.send.at[way, step, part],
            self.recv.at[way, step, part],
        )

    def start(self):
        for part in range(PARTS):
            for way in range(2):
                if part in self.pieces(way, 0):
                    self.copy(way, 0, part).start()

    def advance(self, step):
        for part in range(PARTS):
            for way in range(2):
                if part in self.pieces(way, step - 1):
                    self.copy(way, step - 1, part).wait_recv()
                if step < self.ring.half and part in self.pieces(way, step):
                    self.copy(way, step, part).start()

    def finish(self):
        for step in range(self.ring.half):
            for way in range(2):
                for part in self.pieces(way, step):
                    self.copy(way, step, part).wait_send()

    def steps(self):
        return [functools.partial(self.advance, step) for step in range(1, self.ring.half + 1)]


class RingReduce:
    def __init__(self, ring, mine, slots, terms, send, recv, load):
        self.ring, self.mine, self.slots, self.terms = ring, mine, slots, terms
        self.send, self.recv, self.load = send, recv, load
        self.size = slots.shape[2] // PARTS

    @staticmethod
    def scratch(count, rows, width):
        return [
            pltpu.VMEM((2, count // 2, rows, width), low),
            pltpu.VMEM((2, 2, rows, width), low),
            *ring_semaphores(count),
            pltpu.SemaphoreType.DMA((2, 2, PARTS)),
        ]

    def pieces(self, way, step):
        if step > 0:
            return range(PARTS)
        return range(PARTS // 2) if way == 0 else range(PARTS // 2, PARTS)

    def summed(self, way, step):
        return self.pieces(way, 0) if step == 1 else range(PARTS)

    def target(self, way, step):
        left = self.ring.half - step
        return self.ring.shifted(-left if way else left)

    def slot(self, way, step, part):
        return self.slots.at[way, step, pl.ds(part * self.size, self.size)]

    def term(self, way, step, part):
        return self.terms.at[step % 2, way, pl.ds(part * self.size, self.size)]

    def fetch(self, way, step, part):
        return pltpu.make_async_copy(
            self.mine(self.target(way, step), part), self.term(way, step, part), self.load.at[step % 2, way, part]
        )

    def fetch_all(self, step):
        for part in range(PARTS):
            for way in range(2 if step < self.ring.half else 1):
                if part in self.summed(way, step):
                    self.fetch(way, step, part).start()

    def copy(self, way, step, part):
        alone = step == 0 or part not in self.summed(way, step)
        source = self.mine(self.target(way, step), part) if alone else self.slot(way, step - 1, part)
        return send_to(
            self.ring.next[way],
            source,
            self.slot(way, step, part),
            self.send.at[way, step, part],
            self.recv.at[way, step, part],
        )

    def start(self):
        for way in range(2):
            for part in self.pieces(way, 0):
                self.copy(way, 0, part).start()
        self.fetch_all(1)

    def advance(self, step):
        self.fetch_all(step + 1)
        order = [(way, part) for part in range(PARTS) for way in range(2)]
        for way, part in order:
            if part not in self.summed(way, step):
                self.copy(way, step, part).start()
        for way, part in order:
            if part in self.summed(way, step):
                self.fetch(way, step, part).wait()
                self.copy(way, step - 1, part).wait_recv()
                slot = self.slot(way, step - 1, part)
                total = slot[...].astype(full) + self.term(way, step, part)[...].astype(full)
                slot[...] = total.astype(slot.dtype)
                self.copy(way, step, part).start()

    def steps(self):
        return [functools.partial(self.advance, step) for step in range(1, self.ring.half)]

    def total(self, part):
        last = self.ring.half - 1
        self.fetch(0, last + 1, part).wait()
        for way in range(2):
            self.copy(way, last, part).wait_recv()
        return (
            self.term(0, last + 1, part)[...].astype(full)
            + self.slot(0, last, part)[...].astype(full)
            + self.slot(1, last, part)[...].astype(full)
        )

    def finish(self):
        for step in range(self.ring.half):
            for way in range(2):
                for part in self.pieces(way, step):
                    self.copy(way, step, part).wait_send()

    def free(self, sems):
        for way in range(2):
            pl.semaphore_signal(sems.at[way], inc=1, device_id=self.ring.next[way], device_id_type=MESH)

    def wait_free(self, sems):
        for way in range(2):
            pl.semaphore_wait(sems.at[way], 1)


def row_piece(ref, rows):
    size = rows // PARTS
    return lambda index, part: ref.at[span(index * rows + part * size, size)]


class Shards:
    def __init__(self, count):
        self.count = count
        self.chips = count // CORES
        self.index = lax.axis_index("dp")
        self.chip = self.index // CORES
        self.core = self.index % CORES
        self.sibling = {"dp": self.chip * CORES + 1 - self.core}

    def chip_at(self, offset):
        return (self.chip + offset) % self.chips

    def device(self, chip, core):
        return chip * CORES + core

    def others(self):
        return [{"dp": (self.index + offset) % self.count} for offset in range(1, self.count)]

    def greeted(self):
        return [self.sibling] + [
            {"dp": self.device(self.chip_at(offset), self.core)} for offset in range(1, self.chips)
        ]


class ShardGather:
    def __init__(self, shards, own, whole, send, recv, local):
        self.shards, self.own, self.whole = shards, own, whole
        self.send, self.recv, self.local = send, recv, local
        self.rows = whole.shape[0] // shards.count
        self.size = self.rows // PARTS

    @staticmethod
    def semaphores(count):
        shape = (2, count // CORES, PARTS)
        return [pltpu.SemaphoreType.DMA(shape), pltpu.SemaphoreType.DMA(shape), pltpu.SemaphoreType.DMA]

    def source(self, part):
        if self.own is None:
            return self.place(self.shards.index, part)
        return self.own.at[pl.ds(part * self.size, self.size)]

    def place(self, shard, part):
        return self.whole.at[span(shard * self.rows + part * self.size, self.size)]

    def across(self, offset, part):
        shards = self.shards
        target = {"dp": shards.device(shards.chip_at(offset), shards.core)}
        return send_to(
            target,
            self.source(part),
            self.place(shards.index, part),
            self.send.at[0, offset, part],
            self.recv.at[0, offset, part],
        )

    def beside(self, offset, part):
        shards = self.shards
        place = self.place(shards.device(shards.chip_at(shards.chips - offset), shards.core), part)
        return send_to(
            shards.sibling,
            place if offset else self.source(part),
            place,
            self.send.at[1, offset, part],
            self.recv.at[1, offset, part],
        )

    def keep(self):
        place = self.whole.at[span(self.shards.index * self.rows, self.rows)]
        return pltpu.make_async_copy(self.own, place, self.local)

    def start(self):
        for part in range(PARTS):
            for offset in range(1, self.shards.chips):
                self.across(offset, part).start()
            self.beside(0, part).start()
        if self.own is not None:
            self.keep().start()

    def pass_on(self):
        for part in range(PARTS):
            for offset in range(1, self.shards.chips):
                self.across(offset, part).wait_recv()
                self.beside(offset, part).start()

    def arrive(self):
        for part in range(PARTS):
            for offset in range(self.shards.chips):
                self.beside(offset, part).wait_recv()
        if self.own is not None:
            self.keep().wait()

    def finish(self):
        for part in range(PARTS):
            for offset in range(self.shards.chips):
                self.beside(offset, part).wait_send()
                if offset:
                    self.across(offset, part).wait_send()


class ShardReduce:
    def __init__(self, shards, whole, beside_slots, across_slots, work, loads, stores, beside_sems, across_sems):
        self.shards, self.whole = shards, whole
        self.beside_slots, self.across_slots = beside_slots, across_slots
        self.work, self.loads, self.stores = work, loads, stores
        self.beside_sems, self.across_sems = beside_sems, across_sems
        self.rows = whole.shape[0] // shards.count
        self.lanes = pl.ds(0, whole.shape[1])
        self.offsets = [*range(1, shards.chips), 0]

    def block(self, offset, core):
        shard = self.shards.device(self.shards.chip_at(offset), core)
        return self.whole.at[span(shard * self.rows, self.rows)]

    def beside(self, offset):
        return send_to(
            self.shards.sibling,
            self.block(offset, 1 - self.shards.core),
            self.beside_slots.at[offset],
            self.beside_sems.at[0, offset],
            self.beside_sems.at[1, offset],
        )

    def across(self, offset):
        return send_to(
            {"dp": self.shards.device(self.shards.chip_at(offset), self.shards.core)},
            self.beside_slots.at[offset],
            self.across_slots.at[offset - 1],
            self.across_sems.at[0, offset],
            self.across_sems.at[1, offset],
        )

    def fetches(self, offset):
        sources = (self.beside_slots.at[offset], self.block(offset, self.shards.core))
        return [
            pltpu.make_async_copy(source, self.work.at[offset, number, :, self.lanes], self.loads.at[offset, number])
            for number, source in enumerate(sources)
        ]

    def keep(self, offset):
        return pltpu.make_async_copy(
            self.work.at[offset, 0, :, self.lanes], self.beside_slots.at[offset], self.stores.at[offset]
        )

    def start(self):
        for offset in self.offsets:
            self.beside(offset).start()

    def load(self):
        for offset in self.offsets:
            self.beside(offset).wait_recv()
            for fetch in self.fetches(offset):
                fetch.start()

    def add(self):
        for offset in self.offsets:
            for fetch in self.fetches(offset):
                fetch.wait()
            total = self.work[offset, 0, :, self.lanes].astype(full) + self.work[offset, 1, :, self.lanes].astype(full)
            self.work[offset, 0, :, self.lanes] = total.astype(low)
            self.keep(offset).start()

    def stored(self):
        for offset in self.offsets:
            self.keep(offset).wait()

    def cross(self):
        for offset in self.offsets[:-1]:
            self.across(offset).start()

    def pass_on(self):
        self.stored()
        self.cross()

    def arrive(self):
        for offset in self.offsets[:-1]:
            self.across(offset).wait_recv()

    def finish(self):
        for offset in self.offsets:
            self.beside(offset).wait_send()
            if offset:
                self.across(offset).wait_send()


def grouped(refs, size):
    return [refs[number : number + size] for number in range(0, len(refs), size)]


def rope_tables(seq_len):
    half_dim = HD // 2
    steps = np.arange(half_dim, dtype=np.float32) * np.float32(2.0 / HD)
    frequency = np.exp(np.float32(-math.log(10000.0)) * steps)
    angles = np.arange(seq_len, dtype=np.float32)[:, None] * frequency[None, :]
    cos, sin = np.cos(angles), np.sin(angles)
    return (
        np.concatenate([cos, cos], axis=1).astype(np.float32),
        np.concatenate([-sin, sin], axis=1).astype(np.float32),
    )


def turned(values, cos, sin):
    return values * cos + pltpu.roll(values, HD // 2, 1) * sin


def turned_back(values, cos, sin):
    return values * cos - pltpu.roll(values, HD // 2, 1) * sin


def softmax_block(queries, keys, start, length):
    rows, count = queries.shape[0], keys.shape[0]
    scores = dot(queries, keys, 1, 1) * (1.0 / math.sqrt(HD))
    query_pos = start + lax.broadcasted_iota(jnp.int32, (rows, count), 0)
    key_pos = lax.broadcasted_iota(jnp.int32, (rows, count), 1)
    allowed = (key_pos <= query_pos) & (key_pos < length)
    if start + rows > WINDOW:
        allowed = allowed & (query_pos - key_pos < WINDOW)
    scores = jnp.where(allowed, scores, NEGATIVE)
    exponent = jnp.exp(scores - jnp.max(scores, axis=-1, keepdims=True))
    return exponent * (1.0 / jnp.sum(exponent, axis=-1, keepdims=True))


def forward_kernel(count, shard_count, *refs):
    length, tokens, both_gains, cotangent, query_in, key_in, value_in, out_in = refs[:8]
    gate_in, up_in, down_in, cos_in, sin_in = refs[8:13]
    gain_rows, *results = refs[13:20]
    (all_rows, grad_rows, normed_rows, qkv_out, out_out, down_out, act_out, grad_gate_out, grad_up_out, partial) = (
        refs[20:30]
    )
    (all_gains, qkv_w, out_w, gate_w, up_w, down_w, cos, sin, own, attended, normed, grads, hidden, back) = refs[30:44]
    (gain_sems, local, row_loads, stores, weight_stores, swap_sems) = refs[44:50]
    queries, keys, values, grad_own, attended_own, resid, result_sems = refs[50:57]
    gains, acts = refs[57:59]
    result_copies = [
        pltpu.make_async_copy(source, place, result_sems.at[number])
        for number, (source, place) in enumerate(
            zip((queries, keys, values, grad_own, attended_own, resid), results)
        )
    ]
    sems = refs[59:]
    out_sems, row_sems, grad_sems, normed_sems = grouped(sems[:8], 2)
    shard_sems = grouped(sems[8:], 3)

    ring, shards = Ring(count), Shards(shard_count)
    size, model = tokens.shape
    seq_len, width = queries.shape
    units = gate_w.shape[1]
    limit = length[0]
    others = [{"seq": (ring.index + offset) % count} for offset in range(1, count)]
    tables = [pltpu.make_async_copy(cos_in, cos, local.at[0]), pltpu.make_async_copy(sin_in, sin, local.at[1])]
    for table in tables:
        table.start()
    row = lax.broadcasted_iota(jnp.int32, gains.shape, 0)
    both = jnp.where(row == 0, both_gains[0:1, :], both_gains[1:2, :])
    gains[...] = jnp.where(row < 2, both, 0.0).astype(low)
    greet([*others, *shards.others()])

    out_rows, out_width = out_in.shape
    out_mine = out_w.at[span(shards.index * out_rows, out_rows)]
    out_piece = out_rows // PARTS
    out_gather = RingGather(
        ring,
        lambda part: out_in.at[pl.ds(part * out_piece, out_piece)],
        lambda index, part: out_w.at[
            span(shards.index * out_rows + part * out_piece, out_piece), span(index * out_width, out_width)
        ],
        *out_sems,
    )
    out_kept = pltpu.make_async_copy(out_in, out_mine.at[:, span(ring.index * out_width, out_width)], local.at[2])
    out_gather.start()
    out_kept.start()
    gain_copies = [
        send_to(target, gains, all_gains.at[shards.index], gain_sems.at[0, number], gain_sems.at[1, number])
        for number, target in enumerate(shards.others())
    ]
    for copy in gain_copies:
        copy.start()
    qkv_gathers = [
        ShardGather(shards, source, qkv_w.at[:, pl.ds(number * width, width)], *shard_sems[number])
        for number, source in enumerate((query_in, key_in, value_in))
    ]
    out_shards = ShardGather(shards, None, out_w, *shard_sems[3])
    gate_gather, up_gather, down_gather = (
        ShardGather(shards, source, whole, *shard_sems[4 + number])
        for number, (source, whole) in enumerate(((gate_in, gate_w), (up_in, up_w), (down_in, down_w)))
    )
    for gather in qkv_gathers:
        gather.start()

    piece = size // PARTS
    rows = tokens[...].astype(full)
    rows = rows * lax.rsqrt(jnp.mean(rows * rows, axis=-1, keepdims=True) + EPSILON)
    all_gains[shards.index] = gains[...]
    for copy in gain_copies:
        copy.wait_recv()
    gain_width = gains.shape[1]
    for shard in range(shard_count):
        gain_rows[:, shard * gain_width : (shard + 1) * gain_width] = all_gains[shard, :8, :].astype(full)
    own[0] = (rows * gain_rows[0:1, :]).astype(low)

    def own_gather(source, whole, pair):
        return RingGather(ring, lambda part: source.at[pl.ds(part * piece, piece)], row_piece(whole, size), *pair)

    def own_kept(source, whole, number):
        return pltpu.make_async_copy(source, whole.at[span(ring.index * size, size)], local.at[number])

    row_gather = own_gather(own.at[0], all_rows, row_sems)
    row_gather.start()
    row_kept = own_kept(own.at[0], all_rows, 3)
    row_kept.start()
    gate_gather.start()
    position = ring.index * size + lax.broadcasted_iota(jnp.int32, (size, model), 0)
    grad_own[...] = jnp.where(position < limit, cotangent[...].astype(full), 0.0).astype(low)
    grad_gather = own_gather(grad_own, grad_rows, grad_sems)
    grad_kept = own_kept(grad_own, grad_rows, 4)
    grad_kept.start()

    def owners(step):
        if step in (0, ring.half):
            return [ring.shifted(step)]
        return [ring.shifted(-step), ring.shifted(step)]

    def normed_loads(step, mine, whole):
        return [
            pltpu.make_async_copy(
                mine if step == 0 else whole.at[span(owner * size, size)],
                normed.at[pl.ds(side * size, size)],
                row_loads.at[2, side],
            )
            for side, owner in enumerate(owners(step))
        ]

    def project(step):
        loads = normed_loads(step, own.at[0], all_rows)
        for load in loads:
            load.start()
        for load in loads:
            load.wait()
        linear = dot(normed[pl.ds(0, size * len(loads)), :], qkv_w[...])
        for side, owner in enumerate(owners(step)):
            here = span(owner * size, size)
            side_cos, side_sin = cos[here, :], sin[here, :]
            for number, place in enumerate((queries, keys, values)):
                for head in range(width // HD):
                    lanes = slice(head * HD, (head + 1) * HD)
                    first = number * width + head * HD
                    one = linear[side * size : (side + 1) * size, first : first + HD]
                    if number < 2:
                        one = turned(one, side_cos, side_sin)
                    place[here, lanes] = one.astype(low)

    for step in out_gather.steps():
        step()
    out_kept.wait()
    for gather in qkv_gathers:
        gather.pass_on()
    out_shards.start()
    row_gather.advance(1)
    up_gather.start()
    for table in tables:
        table.wait()
    for gather in qkv_gathers:
        gather.arrive()
    qkv_store = pltpu.make_async_copy(qkv_w, qkv_out, weight_stores.at[0])
    qkv_store.start()
    project(0)
    project(1)
    for step in range(2, ring.half + 1):
        row_gather.advance(step)
        if step == 2:
            gate_gather.pass_on()
        if step == ring.half:
            grad_gather.start()
            down_gather.start()
        project(step)

    for copy in result_copies[:4]:
        copy.start()

    blocks = seq_len // BLOCK

    def swap(head, number):
        other = others[number]
        lanes = pl.ds(head * HD, HD)
        return send_to(
            other,
            attended.at[span(other["seq"] * size, size), lanes],
            attended_own.at[:, span(ring.index * width + head * HD, HD)],
            swap_sems.at[0, head, number],
            swap_sems.at[1, head, number],
        )

    swap_kept = pltpu.make_async_copy(
        attended.at[span(ring.index * size, size)],
        attended_own.at[:, span(ring.index * width, width)],
        local.at[5],
    )
    for head in range(width // HD):
        lanes = slice(head * HD, (head + 1) * HD)
        for number in range(blocks):
            here, upto = pl.ds(number * BLOCK, BLOCK), pl.ds(0, (number + 1) * BLOCK)
            probs = softmax_block(queries[here, lanes], keys[upto, lanes], number * BLOCK, limit)
            attended[here, lanes] = dot(probs.astype(low), values[upto, lanes]).astype(low)
        for number in range(count - 1):
            swap(head, number).start()
    swap_kept.start()
    up_gather.pass_on()
    grad_gather.advance(1)
    out_shards.pass_on()
    out_shards.arrive()
    out_store = pltpu.make_async_copy(out_w, out_out, weight_stores.at[1])
    out_store.start()
    swap_kept.wait()
    for head in range(width // HD):
        for number in range(count - 1):
            swap(head, number).wait_recv()

    def out_project(tile, carry):
        lanes = span(tile * TILE, TILE)
        resid[:, lanes] = tokens[:, lanes].astype(full) + dot(attended_own[...], out_w[lanes, :], 1, 1)
        return carry

    lax.fori_loop(0, model // TILE, out_project, 0)
    rows = resid[...]
    factor = lax.rsqrt(jnp.mean(rows * rows, axis=-1, keepdims=True) + EPSILON)
    own[1] = (rows * factor * gain_rows[1:2, :]).astype(low)
    for copy in result_copies[4:]:
        copy.start()
    normed_gather = own_gather(own.at[1], normed_rows, normed_sems)
    normed_gather.start()
    normed_kept = own_kept(own.at[1], normed_rows, 6)
    normed_kept.start()

    def grad_loads(step):
        return [
            pltpu.make_async_copy(
                grad_own if step == 0 else grad_rows.at[span(owner * size, size)],
                grads.at[step % 2, pl.ds(side * size, size)],
                row_loads.at[step % 2, side],
            )
            for side, owner in enumerate(owners(step))
        ]

    def result_stores(step):
        results = []
        for side, owner in enumerate(owners(step)):
            here, there = pl.ds(side * size, size), span(owner * size, size)
            for number, place in enumerate((act_out, grad_gate_out, grad_up_out)):
                results.append(
                    pltpu.make_async_copy(hidden.at[number, here], place.at[there], stores.at[side, number])
                )
            results.append(pltpu.make_async_copy(back.at[here], partial.at[there], stores.at[side, 3]))
        return results

    def ahead(step):
        return step >= ring.half - 1

    def ahead_rows(step):
        return pl.ds(0 if step < ring.half else 2 * size, size * len(owners(step)))

    def grad_acts(step):
        for load in grad_loads(step):
            load.start()
        for load in grad_loads(step):
            load.wait()
        rows, there = pl.ds(0, size * len(owners(step))), ahead_rows(step)

        def one(tile, carry):
            lanes = span(tile * TILE, TILE)
            acts[there, lanes] = dot(grads[step % 2, rows, :], down_w[:, lanes])
            return carry

        lax.fori_loop(0, units // TILE, one, 0)

    def feed(step):
        loads = normed_loads(step, own.at[1], normed_rows)
        if not ahead(step):
            loads += grad_loads(step)
        for load in loads:
            load.start()
        if step > 0:
            for store in result_stores(step - 1):
                store.wait()
        for load in loads:
            load.wait()
        rows = pl.ds(0, size * len(owners(step)))

        def forward(tile, carry):
            lanes = span(tile * TILE, TILE)
            gate = dot(normed[rows, :], gate_w[:, lanes])
            up = dot(normed[rows, :], up_w[:, lanes])
            if ahead(step):
                grad_act = acts[ahead_rows(step), lanes]
            else:
                grad_act = dot(grads[step % 2, rows, :], down_w[:, lanes])
            sigmoid = 1.0 / (1.0 + jnp.exp(-gate))
            silu = gate * sigmoid
            hidden[0, rows, lanes] = (silu * up).astype(low)
            hidden[1, rows, lanes] = (grad_act * up * sigmoid * (1.0 + gate * (1.0 - sigmoid))).astype(low)
            hidden[2, rows, lanes] = (grad_act * silu).astype(low)
            return carry

        lax.fori_loop(0, units // TILE, forward, 0)

        def backward(tile, carry):
            lanes = span(tile * TILE, TILE)
            total = dot(hidden[1, rows, :], gate_w[lanes, :], 1, 1) + dot(hidden[2, rows, :], up_w[lanes, :], 1, 1)
            back[rows, lanes] = total.astype(low)
            return carry

        lax.fori_loop(0, model // TILE, backward, 0)
        for store in result_stores(step):
            store.start()

    grad_gather.advance(2)
    down_gather.pass_on()
    gate_gather.arrive()
    up_gather.arrive()
    down_gather.arrive()
    down_store = pltpu.make_async_copy(down_w, down_out, weight_stores.at[2])
    down_store.start()
    feed(0)
    for step in range(1, ring.half + 1):
        normed_gather.advance(step)
        if step + 2 <= ring.half:
            grad_gather.advance(step + 2)
        feed(step)
        if step == ring.half - 2:
            grad_acts(step + 1)
            grad_acts(step + 2)
    for store in result_stores(ring.half):
        store.wait()
    for gather in (out_gather, row_gather, grad_gather, normed_gather):
        gather.finish()
    for gather in (*qkv_gathers, out_shards, gate_gather, up_gather, down_gather):
        gather.finish()
    for copy in (row_kept, grad_kept, normed_kept, qkv_store, out_store, down_store, *result_copies):
        copy.wait()
    for copy in gain_copies:
        copy.wait_send()
    for head in range(width // HD):
        for number in range(count - 1):
            swap(head, number).wait_send()


def forward(length, tokens, both_gains, cotangent, weights, tables, collective_id):
    count, shard_count = lax.axis_size("seq"), lax.axis_size("dp")
    size, model = tokens.shape
    seq_len, width, units = size * count, weights[0].shape[1], weights[4].shape[1]
    heads, hidden, rows = shape_of((seq_len, width), low), shape_of((seq_len, units), low), shape_of((size, model), low)
    all_rows = shape_of((seq_len, model), low)
    dma = pltpu.SemaphoreType.DMA
    return pl.pallas_call(
        functools.partial(forward_kernel, count, shard_count),
        out_shape=[
            shape_of((8, model), full),
            heads,
            heads,
            heads,
            rows,
            rows,
            shape_of((size, model), full),
            all_rows,
            all_rows,
            all_rows,
            shape_of((model, 3 * width), low),
            shape_of((model, model), low),
            shape_of((model, units), low),
            hidden,
            hidden,
            hidden,
            all_rows,
        ],
        in_specs=[SMEM] + [VMEM] * 3 + [ANY] * 9,
        out_specs=[VMEM] + [ANY] * 16,
        scratch_shapes=[
            pltpu.VMEM((shard_count, 16, both_gains.shape[1]), low),
            pltpu.VMEM((model, 3 * width), low),
            pltpu.VMEM((model, model), low),
            *[pltpu.VMEM((model, units), low)] * 3,
            *[pltpu.VMEM((seq_len, HD), full)] * 2,
            pltpu.VMEM((2, size, model), low),
            pltpu.VMEM((seq_len, width), low),
            pltpu.VMEM((2 * size, model), low),
            pltpu.VMEM((2, 2 * size, model), low),
            pltpu.VMEM((3, 2 * size, units), low),
            pltpu.VMEM((2 * size, model), low),
            dma((2, shard_count - 1)),
            dma((7,)),
            dma((3, 2)),
            dma((2, 4)),
            dma((3,)),
            dma((2, width // HD, count - 1)),
            *[pltpu.VMEM((seq_len, width), low)] * 3,
            *[pltpu.VMEM((size, model), low)] * 2,
            pltpu.VMEM((size, model), full),
            dma((6,)),
            pltpu.VMEM((16, both_gains.shape[1]), low),
            pltpu.VMEM((3 * size, units), full),
            *ring_semaphores(count) * 4,
            *ShardGather.semaphores(shard_count) * 7,
        ],
        compiler_params=pltpu.CompilerParams(
            collective_id=collective_id, has_side_effects=True, vmem_limit_bytes=VMEM_LIMIT
        ),
        cost_estimate=pl.CostEstimate(flops=0, bytes_accessed=600_000_000, transcendentals=0),
    )(length, tokens, both_gains, cotangent, *weights, *tables)


def ffn_back_kernel(count, shard_count, *refs):
    (partial, normed_rows, grad_rows, act_in, grad_gate_in, grad_up_in, down_in, out_in) = refs[:8]
    resid_in, grad_own_in, gain_rows = refs[8:11]
    gain_sum, resid_out, attn_out, grad_heads, branch, gate_grad, up_grad, down_grad = refs[11:19]
    arrived = grouped(refs[19:23], 2)
    hidden, down_w, out_w, tiles, staged, branch_tile, attended, work = refs[23:31]
    loads, tile_loads, stores, swap_sems, local, work_loads, work_stores = refs[31:38]
    reduce_scratch = refs[38:43]
    resid, grad_own, grad_resid, grad_attn, result_sems = refs[43:48]
    shard_sems = grouped(refs[48:], 2)

    ring, shards = Ring(count), Shards(shard_count)
    size, model = resid.shape
    heads = grad_heads.shape[1]
    others = [{"seq": (ring.index + offset) % count} for offset in range(1, count)]
    inputs = [
        pltpu.make_async_copy(source, place, loads.at[number])
        for number, (source, place) in enumerate(
            (
                (grad_gate_in, hidden.at[1]),
                (grad_up_in, hidden.at[2]),
                (act_in, hidden.at[0]),
                (down_in, down_w),
                (out_in, out_w),
                (resid_in, resid),
                (grad_own_in, grad_own),
            )
        )
    ]
    greet([*others, *shards.greeted()])
    reduce = RingReduce(ring, row_piece(partial, size), *reduce_scratch)
    reduce.start()
    gate, up = (
        ShardReduce(shards, whole, *one, work, work_loads, work_stores, *sems)
        for whole, one, sems in zip((gate_grad, up_grad), arrived, shard_sems)
    )
    count_tiles = model // TILE

    terms = (
        (normed_rows, hidden.at[1], gate_grad, inputs[0]),
        (normed_rows, hidden.at[2], up_grad, inputs[1]),
        (grad_rows, hidden.at[0], down_grad, inputs[2]),
    )
    last = len(terms) * count_tiles - 1

    def fetch(tile):
        lanes = pl.ds(tile % count_tiles * TILE, TILE)
        source = terms[tile // count_tiles][0].at[:, lanes]
        return pltpu.make_async_copy(source, tiles.at[tile % 3], tile_loads.at[tile % 3])

    def store(tile):
        place = terms[tile // count_tiles][2].at[pl.ds(tile % count_tiles * TILE, TILE)]
        return pltpu.make_async_copy(staged.at[tile % 2], place, stores.at[tile % 2, 0])

    def branch_store(tile):
        return pltpu.make_async_copy(
            branch_tile.at[tile % 2], branch.at[:, pl.ds(tile * TILE, TILE)], stores.at[tile % 2, 1]
        )

    later = {0: inputs[1:2], 1: inputs[5:], count_tiles: inputs[2:3], count_tiles + 2: inputs[3:5]}
    for copy in (inputs[0], fetch(0), fetch(1)):
        copy.start()

    def weights(tile):
        for copy in later.get(tile, ()):
            copy.start()
        slot = tile % 2
        _, right, _, ready = terms[tile // count_tiles]
        if tile % count_tiles == 0:
            ready.wait()
        if tile + 2 <= last:
            fetch(tile + 2).start()
        if tile >= 2:
            store(tile - 2).wait()
        fetch(tile).wait()
        staged[slot] = dot(tiles[tile % 3], right[...], 0, 0).astype(low)
        store(tile).start()

    def branches(tile):
        slot = tile % 2
        if tile == 0:
            store(last - 1).wait()
            store(last).wait()
            inputs[3].wait()
        if tile >= 2:
            branch_store(tile - 2).wait()
        branch_tile[slot] = dot(hidden[0], down_w[pl.ds(tile * TILE, TILE), :], 1, 1).astype(low)
        branch_store(tile).start()

    steps = reduce.steps()
    tasks = [functools.partial(weights, tile) for tile in range(last + 1)]
    early = count_tiles // 2
    weave(tasks[:early], [])
    steps[0]()
    weave(tasks[early : count_tiles + 2], [])
    gate.start()
    weave(tasks[count_tiles + 2 : 2 * count_tiles + 2], [gate.load, gate.add, gate.pass_on, lambda: None])
    up.start()
    for step in steps[1:-1]:
        step()
    weave(tasks[2 * count_tiles + 2 :], [up.load, up.add])
    tasks = [functools.partial(branches, tile) for tile in range(count_tiles)]
    weave(tasks, [up.pass_on, steps[-1], lambda: None])
    for copy in inputs[4:]:
        copy.wait()
    gain_total = jnp.zeros((1, model), full)
    swaps = []
    for part in range(PARTS):
        here = pl.ds(part * reduce.size, reduce.size)
        there = grad_heads.at[span(ring.index * size + part * reduce.size, reduce.size)]
        grad_normed, rows = reduce.total(part), resid[here, :]
        factor = lax.rsqrt(jnp.mean(rows * rows, axis=-1, keepdims=True) + EPSILON)
        weighted = grad_normed * gain_rows[1:2, :]
        inner = jnp.mean(weighted * rows, axis=-1, keepdims=True)
        grad = grad_own[here, :].astype(full) + factor * (weighted - rows * (factor * factor * inner))
        grad_resid[here, :] = grad
        grad_attn[here, :] = grad.astype(low)
        gain_total += jnp.sum(grad_normed * rows * factor, axis=0, keepdims=True)
        for number, index in enumerate([other["seq"] for other in others] + [ring.index]):
            lanes = span(index * heads, heads)
            attended[here, lanes] = dot(grad_attn[here, :], out_w[:, lanes]).astype(low)
            source = attended.at[here, lanes]
            if number < count - 1:
                sems = (swap_sems.at[0, part, number], swap_sems.at[1, part, number])
                swap = send_to(others[number], source, there, *sems)
            else:
                swap = pltpu.make_async_copy(source, there, local.at[part])
            swap.start()
            swaps.append(swap)
    gain_sum[...] = jnp.broadcast_to(gain_total, gain_sum.shape)
    results = [
        pltpu.make_async_copy(grad_resid, resid_out, result_sems.at[0]),
        pltpu.make_async_copy(grad_attn, attn_out, result_sems.at[1]),
    ]
    for copy in results:
        copy.start()
    reduce.finish()
    for tile in (count_tiles - 2, count_tiles - 1):
        branch_store(tile).wait()
    for one in (gate, up):
        one.arrive()
        one.finish()
    for copy in (*swaps, *results):
        copy.wait()


def ffn_back(partial, normed_rows, grad_rows, hidden, down_w, out_w, resid, grad_own, gain_rows, heads, collective_id):
    count, shard_count = lax.axis_size("seq"), lax.axis_size("dp")
    size, model = resid.shape
    seq_len, units = hidden[0].shape
    chips, shard_rows = shard_count // CORES, model // shard_count
    grad_w = shape_of((model, units), low)
    dma = pltpu.SemaphoreType.DMA
    return pl.pallas_call(
        functools.partial(ffn_back_kernel, count, shard_count),
        out_shape=[
            shape_of((8, model), full),
            shape_of((size, model), full),
            shape_of((size, model), low),
            shape_of((seq_len, heads), low),
            shape_of((seq_len, model), low),
            grad_w,
            grad_w,
            grad_w,
            *[shape_of((number, shard_rows, units), low) for number in (chips, chips - 1)] * 2,
        ],
        in_specs=[ANY] * 10 + [VMEM],
        out_specs=[VMEM] + [ANY] * 11,
        scratch_shapes=[
            pltpu.VMEM((3, seq_len, units), low),
            pltpu.VMEM(down_w.shape, low),
            pltpu.VMEM(out_w.shape, low),
            pltpu.VMEM((3, seq_len, TILE), low),
            pltpu.VMEM((2, TILE, units), low),
            pltpu.VMEM((2, seq_len, TILE), low),
            pltpu.VMEM((size, model), low),
            pltpu.VMEM((chips, 2, shard_rows, units), low),
            dma((7,)),
            dma((3,)),
            dma((2, 2)),
            dma((2, PARTS, count - 1)),
            dma((PARTS,)),
            dma((chips, 2)),
            dma((chips,)),
            *RingReduce.scratch(count, size, model),
            pltpu.VMEM((size, model), full),
            pltpu.VMEM((size, model), low),
            pltpu.VMEM((size, model), full),
            pltpu.VMEM((size, model), low),
            dma((2,)),
            *[dma((2, chips))] * 4,
        ],
        compiler_params=pltpu.CompilerParams(
            collective_id=collective_id, has_side_effects=True, vmem_limit_bytes=VMEM_LIMIT
        ),
        cost_estimate=pl.CostEstimate(flops=0, bytes_accessed=300_000_000, transcendentals=0),
    )(partial, normed_rows, grad_rows, *hidden, down_w, out_w, resid, grad_own, gain_rows)


def attend_back_kernel(count, shard_count, *refs):
    length, *head_refs, cos_in, sin_in, rows_in, qkv_in, branch = refs[:10]
    *own_refs, gain_rows, gain_ffn_sum, down_grad = refs[10:16]
    output_out, grad_normed, grad_out_w, gain_total, partial, qkv_grad, out_left, out_right = refs[16:24]
    arrived = grouped(refs[24:32], 2)
    cos, sin, weights, grads, sum_k, sum_v, row_tiles, staged, grad_staged, work, out_sum = refs[32:43]
    loads, tile_loads, stores, grad_stores, work_loads, work_stores, out_loads_sem, free_sems = refs[43:51]
    gain_block, gain_shards, gain_part, gain_parts, gain_sems, gain_part_sems = refs[51:57]
    slots, terms, ring_send, ring_recv, term_loads, last_send, last_recv, last_loads = refs[57:65]
    out_scratch = refs[65:70]
    grad_heads, queries, keys, values, resid, grad_attn, attended_own, output = refs[70:78]
    shard_sems = grouped(refs[78:], 2)

    ring, shards = Ring(count), Shards(shard_count)
    seq_len, width = queries.shape
    size, model = resid.shape
    blocks, tiles = seq_len // BLOCK, model // TILE
    scale = 1.0 / math.sqrt(HD)
    limit = length[0]
    others = [{"seq": (ring.index + offset) % count} for offset in range(1, count)]
    inputs = [
        pltpu.make_async_copy(source, place, loads.at[number])
        for number, (source, place) in enumerate(
            (
                (cos_in, cos),
                (sin_in, sin),
                (qkv_in, weights),
                *zip(own_refs, (resid, grad_attn, attended_own)),
                *zip(head_refs, (grad_heads, queries, keys, values)),
            )
        )
    ]
    for load in inputs[4:6]:
        load.start()
    greet([*others, *shards.others()])
    reduce = RingReduce(ring, row_piece(branch, size), slots, terms, ring_send, ring_recv, term_loads)
    last = RingReduce(ring, row_piece(partial, size), slots, terms, last_send, last_recv, last_loads)
    reduce.start()
    shard_reduces = [
        ShardReduce(shards, whole, *one, work, work_loads, work_stores, *sems)
        for whole, one, sems in zip((out_left, out_right, down_grad, qkv_grad), arrived, shard_sems)
    ]
    left, right, down, qkv = shard_reduces

    half = model // 2

    def out_store(tile):
        rows = pl.ds(tile * TILE, TILE)
        return [
            pltpu.make_async_copy(
                staged.at[tile % 2, :, pl.ds(side * half, half)], whole.at[rows], stores.at[tile % 2, side]
            )
            for side, whole in enumerate((out_left, out_right))
        ]

    def out_back(tile):
        if tile >= 2:
            for copy in out_store(tile - 2):
                copy.wait()
        staged[tile % 2] = dot(grad_attn[:, pl.ds(tile * TILE, TILE)], attended_own[...], 0, 0).astype(low)
        for copy in out_store(tile):
            copy.start()

    def out_spread():
        for tile in (tiles - 2, tiles - 1):
            for copy in out_store(tile):
                copy.wait()
        left.start()
        right.start()

    def attend_block(head, number):
        lanes = slice(head * HD, (head + 1) * HD)
        here, upto = pl.ds(number * BLOCK, BLOCK), pl.ds(0, (number + 1) * BLOCK)
        if number == 0:
            sum_k[...] = jnp.zeros_like(sum_k)
            sum_v[...] = jnp.zeros_like(sum_v)
            if head == 0:
                for load in (*inputs[:2], *inputs[6:]):
                    load.wait()
        query_part, grad_part = queries[here, lanes], grad_heads[here, lanes]
        probs = softmax_block(query_part, keys[upto, lanes], number * BLOCK, limit)
        grad_probs = dot(grad_part, values[upto, lanes], 1, 1)
        inner = jnp.sum(probs * grad_probs, axis=-1, keepdims=True)
        grad_scores = (probs * (grad_probs - inner)).astype(low)
        sum_v[upto, :] += dot(probs.astype(low), grad_part, 0, 0)
        sum_k[upto, :] += dot(grad_scores, query_part, 0, 0)
        grad_query = dot(grad_scores, keys[upto, lanes]) * scale
        grads[here, lanes] = turned_back(grad_query, cos[here, :], sin[here, :]).astype(low)
        if number == blocks - 1:
            key_lanes = slice(width + head * HD, width + (head + 1) * HD)
            value_lanes = slice(2 * width + head * HD, 2 * width + (head + 1) * HD)
            grads[:, key_lanes] = turned_back(sum_k[...] * scale, cos[...], sin[...]).astype(low)
            grads[:, value_lanes] = sum_v[...].astype(low)

    def fetch(tile):
        return pltpu.make_async_copy(
            rows_in.at[:, pl.ds(tile * TILE, TILE)], row_tiles.at[tile % 2], tile_loads.at[tile % 2]
        )

    def store(number):
        return pltpu.make_async_copy(
            staged.at[number % 2], partial.at[pl.ds(number * BLOCK, BLOCK)], stores.at[number % 2, 0]
        )

    def grad_store(tile):
        return pltpu.make_async_copy(
            grad_staged.at[tile % 2], qkv_grad.at[pl.ds(tile * TILE, TILE)], grad_stores.at[tile % 2]
        )

    def rows_back(number):
        if number == 0:
            inputs[2].wait()
            fetch(0).start()
        if number >= 2:
            store(number - 2).wait()
        staged[number % 2] = dot(grads[pl.ds(number * BLOCK, BLOCK), :], weights[...], 1, 1).astype(low)
        store(number).start()

    def weights_back(tile):
        if tile + 1 < tiles:
            fetch(tile + 1).start()
        if tile >= 2:
            grad_store(tile - 2).wait()
        fetch(tile).wait()
        grad = dot(row_tiles[tile % 2], grads[...], 0, 0)
        grad_staged[tile % 2] = grad.astype(low)
        grad_store(tile).start()
        lanes = pl.ds(tile * TILE, TILE)
        product = grad * weights[lanes, :].astype(full)
        shared = product[:, :HD]
        for first in range(HD, product.shape[1], HD):
            shared += product[:, first : first + HD]
        gain = lax.dot_general(
            jnp.ones((8, shared.shape[1]), full),
            shared,
            (((1,), (1,)), ((), ())),
            precision=lax.Precision.HIGHEST,
            preferred_element_type=full,
        )
        row = lax.broadcasted_iota(jnp.int32, gain.shape, 0)
        gain_block[:, lanes] = jnp.where(row == 0, gain / gain_rows[0:1, lanes], gain_ffn_sum[:, lanes])

    gain_width = model // shard_count
    gain_copies = [
        send_to(
            other,
            gain_block.at[:, span(other["dp"] * gain_width, gain_width)],
            gain_shards.at[shards.index],
            gain_sems.at[0, number],
            gain_sems.at[1, number],
        )
        for number, other in enumerate(shards.others())
    ]
    gain_part_copies = [
        send_to(
            other, gain_part, gain_parts.at[ring.index], gain_part_sems.at[0, number], gain_part_sems.at[1, number]
        )
        for number, other in enumerate(others)
    ]

    def gains_start():
        for copy in gain_copies:
            copy.start()

    def gains_middle():
        gain_shards[shards.index] = gain_block[:, span(shards.index * gain_width, gain_width)]
        for copy in gain_copies:
            copy.wait_recv()
        gain_part[...] = jnp.sum(gain_shards[...], axis=0)
        for copy in gain_part_copies:
            copy.start()

    def gains_end():
        gain_parts[ring.index] = gain_part[...]
        for copy in gain_part_copies:
            copy.wait_recv()
        gain_total[...] = jnp.sum(gain_parts[...], axis=0)
        for copy in (*gain_copies, *gain_part_copies):
            copy.wait_send()

    def out_loads(side):
        one = shard_reduces[side]
        lanes = pl.ds(side * half, half)
        copies = [pltpu.make_async_copy(one.beside_slots.at[0], out_sum.at[:, lanes], out_loads_sem.at[0])]
        copies += [
            pltpu.make_async_copy(
                one.across_slots.at[offset - 1], work.at[offset, 0, :, one.lanes], out_loads_sem.at[offset]
            )
            for offset in range(1, shards.chips)
        ]
        return copies

    def out_close(side):
        one = shard_reduces[side]
        lanes = pl.ds(side * half, half)
        one.arrive()
        for copy in out_loads(side):
            copy.start()
        for copy in out_loads(side):
            copy.wait()
        total = out_sum[:, lanes].astype(full)
        for offset in range(1, shards.chips):
            total += work[offset, 0, :, one.lanes].astype(full)
        out_sum[:, lanes] = total.astype(low)

    rows, out_width = grad_out_w.shape

    def out_piece(index, part):
        piece = rows // PARTS
        return out_sum.at[pl.ds(part * piece, piece), span(index * out_width, out_width)]

    out_reduce = RingReduce(ring, out_piece, *out_scratch)
    for load in (*inputs[6:], *inputs[:4]):
        load.start()
    for load in inputs[4:6]:
        load.wait()
    steps = reduce.steps()
    for tile in range(tiles):
        out_back(tile)
        if tile == tiles // 2:
            steps[0]()
    out_spread()
    attention = [
        functools.partial(attend_block, head, number) for head in range(width // HD) for number in range(blocks)
    ]
    weave(attention, [left.load, left.add, left.pass_on, right.load, right.add, right.pass_on, *steps[1:-1]])
    down.start()
    projections = [functools.partial(rows_back, number) for number in range(blocks)]
    projections += [functools.partial(weights_back, tile) for tile in range(tiles)]
    weave(projections, [down.load, down.add, down.stored, steps[-1], lambda: None])
    for number in (blocks - 2, blocks - 1):
        store(number).wait()
    for tile in (tiles - 2, tiles - 1):
        grad_store(tile).wait()
    qkv.start()
    gains_start()
    inputs[3].wait()
    for part in range(PARTS):
        here = pl.ds(part * reduce.size, reduce.size)
        position = ring.index * size + part * reduce.size + lax.broadcasted_iota(jnp.int32, (reduce.size, model), 0)
        total = resid[here, :] + reduce.total(part)
        output[here, :] = jnp.where(position < limit, total, 0.0).astype(low)
    output_store = pltpu.make_async_copy(output, output_out, out_loads_sem.at[shards.chips])
    output_store.start()
    reduce.finish()
    reduce.free(free_sems)
    last.wait_free(free_sems)
    last.start()
    for side in range(2):
        out_close(side)
    out_reduce.start()
    down.cross()
    last.advance(1)
    qkv.load()
    qkv.add()
    out_reduce.advance(1)
    qkv.pass_on()
    gains_middle()
    for step in range(2, ring.half):
        last.advance(step)
        out_reduce.advance(step)
    gains_end()
    for part in range(PARTS):
        grad_out_w[pl.ds(part * out_reduce.size, out_reduce.size), :] = out_reduce.total(part)
    for part in range(PARTS):
        grad_normed[pl.ds(part * last.size, last.size), :] = last.total(part)
    for one in (down, qkv):
        one.arrive()
    for one in (*shard_reduces, last, out_reduce):
        one.finish()
    output_store.wait()


def attend_back(
    length, grad_heads, heads, tables, rows, qkv_w, branch, sums, gain_rows, gain_ffn_sum, down_grad, collective_id
):
    count, shard_count = lax.axis_size("seq"), lax.axis_size("dp")
    resid, grad_attn, attended_own = sums
    seq_len, width = grad_heads.shape
    size, model = resid.shape
    chips, shard_rows, units = shard_count // CORES, model // shard_count, down_grad.shape[1]
    half, gain_width = model // 2, model // shard_count
    widths = (half, half, units, 3 * width)
    dma = pltpu.SemaphoreType.DMA
    arrivals = [
        shape_of((number, shard_rows, one), low) for one in widths for number in (chips, max(chips - 1, 1))
    ]
    out_width = model // count
    return pl.pallas_call(
        functools.partial(attend_back_kernel, count, shard_count),
        out_shape=[
            shape_of((size, model), low),
            shape_of((size, model), full),
            shape_of((shard_rows, out_width), full),
            shape_of((8, gain_width), full),
            shape_of((seq_len, model), low),
            shape_of((model, 3 * width), low),
            shape_of((model, half), low),
            shape_of((model, half), low),
            *arrivals,
        ],
        in_specs=[SMEM] + [ANY] * 12 + [VMEM] * 2 + [ANY],
        out_specs=[ANY] + [VMEM] * 3 + [ANY] * (4 + len(arrivals)),
        scratch_shapes=[
            *[pltpu.VMEM((seq_len, HD), full)] * 2,
            pltpu.VMEM((model, 3 * width), low),
            pltpu.VMEM((seq_len, 3 * width), low),
            *[pltpu.VMEM((seq_len, HD), full)] * 2,
            pltpu.VMEM((2, seq_len, TILE), low),
            pltpu.VMEM((2, BLOCK, model), low),
            pltpu.VMEM((2, TILE, 3 * width), low),
            pltpu.VMEM((chips, 2, shard_rows, max(widths)), low),
            pltpu.VMEM((shard_rows, model), low),
            dma((10,)),
            dma((2,)),
            dma((2, 2)),
            dma((2,)),
            dma((chips, 2)),
            dma((chips,)),
            dma((chips + 1,)),
            pltpu.SemaphoreType.REGULAR((2,)),
            pltpu.VMEM((8, model), full),
            pltpu.VMEM((shard_count, 8, gain_width), full),
            pltpu.VMEM((8, gain_width), full),
            pltpu.VMEM((count, 8, gain_width), full),
            dma((2, shard_count - 1)),
            dma((2, count - 1)),
            *RingReduce.scratch(count, size, model),
            *RingReduce.scratch(count, size, model)[2:],
            *RingReduce.scratch(count, shard_rows, out_width),
            *[pltpu.VMEM((seq_len, width), low)] * 4,
            pltpu.VMEM((size, model), full),
            *[pltpu.VMEM((size, model), low)] * 3,
            *[dma((2, chips))] * (2 * len(widths)),
        ],
        compiler_params=pltpu.CompilerParams(
            collective_id=collective_id, has_side_effects=True, vmem_limit_bytes=VMEM_LIMIT
        ),
        cost_estimate=pl.CostEstimate(flops=0, bytes_accessed=500_000_000, transcendentals=0),
    )(length, grad_heads, *heads, *tables, rows, qkv_w, branch, *sums, gain_rows, gain_ffn_sum, down_grad)


def settle_kernel(count_weights, *refs):
    pairs = grouped(refs[: 2 * count_weights], 2)
    grad_normed, tokens, gain_rows, grad_resid, output_in, grad_out_in = refs[2 * count_weights : 2 * count_weights + 6]
    output, grad_tokens, grad_out, *owned = refs[2 * count_weights + 6 :]

    def total(pair):
        beside, across = pair
        return beside[0].astype(full) + jnp.sum(across[...].astype(full), axis=0)

    output[...] = output_in[...]
    grad_out[...] = grad_out_in[...]
    for place, pair in zip(owned, pairs[:-1]):
        place[...] = total(pair)
    qkv = total(pairs[-1])
    for number, place in enumerate(owned[-3:]):
        width = place.shape[1]
        place[...] = qkv[:, number * width : (number + 1) * width]
    values = tokens[...].astype(full)
    factor = lax.rsqrt(jnp.mean(values * values, axis=-1, keepdims=True) + EPSILON)
    weighted = grad_normed[...] * gain_rows[0:1, :]
    inner = jnp.mean(weighted * values, axis=-1, keepdims=True)
    grad_tokens[...] = grad_resid[...] + factor * (weighted - values * (factor * factor * inner))


def settle(pairs, grad_normed, tokens, gain_rows, grad_resid, output, grad_out, width):
    steps = 4
    size, model = tokens.shape
    rows = grad_out.shape[0]

    def cut(array):
        return pl.BlockSpec((array.shape[0] // steps, array.shape[1]), lambda step: (step, 0))

    def whole(array):
        return pl.BlockSpec(array.shape, lambda step: (0, 0))

    pair_specs = []
    for beside, across in pairs:
        pair_specs.append(pl.BlockSpec((1, rows // steps, beside.shape[2]), lambda step: (0, step, 0)))
        pair_specs.append(
            pl.BlockSpec((across.shape[0], rows // steps, across.shape[2]), lambda step: (0, step, 0))
        )
    outs = [
        shape_of((size, model), low),
        shape_of((size, model), full),
        shape_of(grad_out.shape, full),
        *[shape_of((rows, beside.shape[2]), full) for beside, _ in pairs[:-1]],
        *[shape_of((rows, width), full)] * 3,
    ]
    return pl.pallas_call(
        functools.partial(settle_kernel, len(pairs)),
        grid=(steps,),
        out_shape=outs,
        in_specs=[
            *pair_specs,
            cut(grad_normed),
            cut(tokens),
            whole(gain_rows),
            cut(grad_resid),
            cut(output),
            cut(grad_out),
        ],
        out_specs=[cut(out) for out in outs],
        compiler_params=pltpu.CompilerParams(vmem_limit_bytes=VMEM_LIMIT),
    )(
        *[one for pair in pairs for one in pair],
        grad_normed,
        tokens,
        gain_rows,
        grad_resid,
        output,
        grad_out,
    )


def body(
    tokens,
    lengths,
    cotangent,
    w_query,
    w_key,
    w_value,
    w_out,
    w_gate,
    w_up,
    w_down,
    gain_attn,
    gain_ffn,
):
    seq_len = tokens.shape[0] * lax.axis_size("seq")
    head_width = w_query.shape[1]
    tables = rope_tables(seq_len)
    both_gains = jnp.stack([gain_attn, gain_ffn]).astype(jnp.float32)
    (
        gain_rows,
        queries,
        keys,
        values,
        grad_ffn,
        attended_tok,
        resid,
        full1,
        grad_full,
        full2,
        qkv_w,
        out_full,
        down_w,
        activation,
        grad_gate,
        grad_up,
        partial2,
    ) = forward(
        lengths, tokens, both_gains, cotangent, (w_query, w_key, w_value, w_out, w_gate, w_up, w_down), tables, 1
    )
    gain_ffn_sum, grad_resid, grad_attn, grad_heads, branch, _, _, grad_w_down, *gate_up = ffn_back(
        partial2,
        full2,
        grad_full,
        (activation, grad_gate, grad_up),
        down_w,
        out_full,
        resid,
        grad_ffn,
        gain_rows,
        head_width,
        2,
    )
    output, grad_normed1, owned_out, gain_sums, _, _, _, _, *arrived = attend_back(
        lengths,
        grad_heads,
        (queries, keys, values),
        tables,
        full1,
        qkv_w,
        branch,
        (resid, grad_attn, attended_tok),
        gain_rows,
        gain_ffn_sum,
        grad_w_down,
        3,
    )
    output, grad_tokens, owned_out, owned_gate, owned_up, owned_down, owned_query, owned_key, owned_value = settle(
        grouped([*gate_up, *arrived[4:]], 2), grad_normed1, tokens, gain_rows, grad_resid, output, owned_out, head_width
    )
    piece = gain_sums.shape[1] // lax.axis_size("seq")
    owned_gains = lax.dynamic_slice_in_dim(gain_sums, lax.axis_index("seq") * piece, piece, axis=1)
    owned_gain_attn, owned_gain_ffn = owned_gains[0], owned_gains[1]
    return (
        output,
        grad_tokens,
        owned_query,
        owned_key,
        owned_value,
        owned_out,
        owned_gate,
        owned_up,
        owned_down,
        owned_gain_attn,
        owned_gain_ffn,
    )


def solution(mesh):
    rows, shard = P(("dp", "seq"), None), P("dp", "seq")
    gains = P(("dp", "seq"))
    return jax.shard_map(
        body,
        mesh=mesh,
        in_specs=(rows, P("dp"), rows, *[shard] * 7, P("dp"), P("dp")),
        out_specs=(rows, rows, *[shard] * 7, gains, gains),
        check_vma=False,
    )
```

```python
import functools
import math

import jax
import jax.numpy as jnp
import numpy as np
from jax import lax
from jax.experimental import pallas as pl
from jax.experimental.pallas import tpu as pltpu
from jax.sharding import PartitionSpec as P

HD = 128
WINDOW = 2048
EPSILON = 1e-05
NEGATIVE = -1e30
BLOCK = 256
TILE = 256
LINE = 4
CORES = 2
PARTS = 2
MESH = pl.DeviceIdType.MESH
VMEM_LIMIT = 60 * 1024 * 1024

ANY = pl.BlockSpec(memory_space=pl.ANY)
VMEM = pl.BlockSpec(memory_space=pltpu.VMEM)
SMEM = pl.BlockSpec(memory_space=pltpu.SMEM)
low = jnp.bfloat16
full = jnp.float32


def shape_of(shape, dtype):
    return jax.ShapeDtypeStruct(shape, dtype)


def span(start, size):
    if isinstance(start, int):
        return pl.ds(start, size)
    return pl.ds(pl.multiple_of(start, size), size)


def dot(left, right, left_dim=1, right_dim=0):
    return lax.dot_general(
        left, right, (((left_dim,), (right_dim,)), ((), ())), preferred_element_type=jnp.float32
    )


def greet(targets):
    barrier = pltpu.get_barrier_semaphore()
    for target in targets:
        pl.semaphore_signal(barrier, inc=1, device_id=target, device_id_type=MESH)
    pl.semaphore_wait(barrier, len(targets))


def send_to(target, source, place, send, recv):
    return pltpu.make_async_remote_copy(
        src_ref=source, dst_ref=place, send_sem=send, recv_sem=recv, device_id=target, device_id_type=MESH
    )


def weave(tasks, events):
    done = 0
    for number, task in enumerate(tasks):
        task()
        upto = (number + 1) * len(events) // len(tasks)
        for event in events[done:upto]:
            event()
        done = upto


def ring_index(place, count):
    columns = count // LINE
    column = place // LINE
    level = place % LINE
    odd = column % 2
    return (level + odd * (LINE - 1 - 2 * level)) * columns + column


def ring_place(index, count):
    columns = count // LINE
    level = index // columns
    column = index % columns
    odd = column % 2
    return column * LINE + level + odd * (LINE - 1 - 2 * level)


class Ring:
    def __init__(self, count):
        self.count = count
        self.half = count // 2
        self.index = lax.axis_index("seq")
        self.place = ring_place(self.index, count)
        self.next = ({"seq": self.shifted(1)}, {"seq": self.shifted(-1)})

    def shifted(self, offset):
        return ring_index((self.place + offset + self.count) % self.count, self.count)


def ring_semaphores(count):
    return [pltpu.SemaphoreType.DMA((2, count // 2, PARTS))] * 2


class RingGather:
    def __init__(self, ring, source, place, send, recv):
        self.ring, self.source, self.place = ring, source, place
        self.send, self.recv = send, recv

    def pieces(self, way, step):
        if step < self.ring.half - 1:
            return range(PARTS)
        return range(PARTS // 2) if way == 0 else range(PARTS // 2, PARTS)

    def copy(self, way, step, part):
        place = self.place(self.ring.shifted(step if way else -step), part)
        return send_to(
            self.ring.next[way],
            self.source(part) if step == 0 else place,
            place,
            self.send.at[way, step, part],
            self.recv.at[way, step, part],
        )

    def start(self):
        for part in range(PARTS):
            for way in range(2):
                if part in self.pieces(way, 0):
                    self.copy(way, 0, part).start()

    def advance(self, step):
        for part in range(PARTS):
            for way in range(2):
                if part in self.pieces(way, step - 1):
                    self.copy(way, step - 1, part).wait_recv()
                if step < self.ring.half and part in self.pieces(way, step):
                    self.copy(way, step, part).start()

    def finish(self):
        for step in range(self.ring.half):
            for way in range(2):
                for part in self.pieces(way, step):
                    self.copy(way, step, part).wait_send()

    def steps(self):
        return [functools.partial(self.advance, step) for step in range(1, self.ring.half + 1)]


class RingReduce:
    def __init__(self, ring, mine, slots, terms, send, recv, load):
        self.ring, self.mine, self.slots, self.terms = ring, mine, slots, terms
        self.send, self.recv, self.load = send, recv, load
        self.size = slots.shape[2] // PARTS

    @staticmethod
    def scratch(count, rows, width):
        return [
            pltpu.VMEM((2, count // 2, rows, width), low),
            pltpu.VMEM((2, 2, rows, width), low),
            *ring_semaphores(count),
            pltpu.SemaphoreType.DMA((2, 2, PARTS)),
        ]

    def pieces(self, way, step):
        if step > 0:
            return range(PARTS)
        return range(PARTS // 2) if way == 0 else range(PARTS // 2, PARTS)

    def summed(self, way, step):
        return self.pieces(way, 0) if step == 1 else range(PARTS)

    def target(self, way, step):
        left = self.ring.half - step
        return self.ring.shifted(-left if way else left)

    def slot(self, way, step, part):
        return self.slots.at[way, step, pl.ds(part * self.size, self.size)]

    def term(self, way, step, part):
        return self.terms.at[step % 2, way, pl.ds(part * self.size, self.size)]

    def fetch(self, way, step, part):
        return pltpu.make_async_copy(
            self.mine(self.target(way, step), part), self.term(way, step, part), self.load.at[step % 2, way, part]
        )

    def fetch_all(self, step):
        for part in range(PARTS):
            for way in range(2 if step < self.ring.half else 1):
                if part in self.summed(way, step):
                    self.fetch(way, step, part).start()

    def copy(self, way, step, part):
        alone = step == 0 or part not in self.summed(way, step)
        source = self.mine(self.target(way, step), part) if alone else self.slot(way, step - 1, part)
        return send_to(
            self.ring.next[way],
            source,
            self.slot(way, step, part),
            self.send.at[way, step, part],
            self.recv.at[way, step, part],
        )

    def start(self):
        for way in range(2):
            for part in self.pieces(way, 0):
                self.copy(way, 0, part).start()
        self.fetch_all(1)

    def advance(self, step):
        self.fetch_all(step + 1)
        order = [(way, part) for part in range(PARTS) for way in range(2)]
        for way, part in order:
            if part not in self.summed(way, step):
                self.copy(way, step, part).start()
        for way, part in order:
            if part in self.summed(way, step):
                self.fetch(way, step, part).wait()
                self.copy(way, step - 1, part).wait_recv()
                slot = self.slot(way, step - 1, part)
                total = slot[...].astype(full) + self.term(way, step, part)[...].astype(full)
                slot[...] = total.astype(slot.dtype)
                self.copy(way, step, part).start()

    def steps(self):
        return [functools.partial(self.advance, step) for step in range(1, self.ring.half)]

    def total(self, part):
        last = self.ring.half - 1
        self.fetch(0, last + 1, part).wait()
        for way in range(2):
            self.copy(way, last, part).wait_recv()
        return (
            self.term(0, last + 1, part)[...].astype(full)
            + self.slot(0, last, part)[...].astype(full)
            + self.slot(1, last, part)[...].astype(full)
        )

    def finish(self):
        for step in range(self.ring.half):
            for way in range(2):
                for part in self.pieces(way, step):
                    self.copy(way, step, part).wait_send()

    def free(self, sems):
        for way in range(2):
            pl.semaphore_signal(sems.at[way], inc=1, device_id=self.ring.next[way], device_id_type=MESH)

    def wait_free(self, sems):
        for way in range(2):
            pl.semaphore_wait(sems.at[way], 1)


def row_piece(ref, rows):
    size = rows // PARTS
    return lambda index, part: ref.at[span(index * rows + part * size, size)]


class Shards:
    def __init__(self, count):
        self.count = count
        self.chips = count // CORES
        self.index = lax.axis_index("dp")
        self.chip = self.index // CORES
        self.core = self.index % CORES
        self.sibling = {"dp": self.chip * CORES + 1 - self.core}

    def chip_at(self, offset):
        return (self.chip + offset) % self.chips

    def device(self, chip, core):
        return chip * CORES + core

    def others(self):
        return [{"dp": (self.index + offset) % self.count} for offset in range(1, self.count)]

    def greeted(self):
        return [self.sibling] + [
            {"dp": self.device(self.chip_at(offset), self.core)} for offset in range(1, self.chips)
        ]


class ShardGather:
    def __init__(self, shards, own, whole, send, recv, local):
        self.shards, self.own, self.whole = shards, own, whole
        self.send, self.recv, self.local = send, recv, local
        self.rows = whole.shape[0] // shards.count
        self.size = self.rows // PARTS

    @staticmethod
    def semaphores(count):
        shape = (2, count // CORES, PARTS)
        return [pltpu.SemaphoreType.DMA(shape), pltpu.SemaphoreType.DMA(shape), pltpu.SemaphoreType.DMA]

    def source(self, part):
        if self.own is None:
            return self.place(self.shards.index, part)
        return self.own.at[pl.ds(part * self.size, self.size)]

    def place(self, shard, part):
        return self.whole.at[span(shard * self.rows + part * self.size, self.size)]

    def across(self, offset, part):
        shards = self.shards
        target = {"dp": shards.device(shards.chip_at(offset), shards.core)}
        return send_to(
            target,
            self.source(part),
            self.place(shards.index, part),
            self.send.at[0, offset, part],
            self.recv.at[0, offset, part],
        )

    def beside(self, offset, part):
        shards = self.shards
        place = self.place(shards.device(shards.chip_at(shards.chips - offset), shards.core), part)
        return send_to(
            shards.sibling,
            place if offset else self.source(part),
            place,
            self.send.at[1, offset, part],
            self.recv.at[1, offset, part],
        )

    def keep(self):
        place = self.whole.at[span(self.shards.index * self.rows, self.rows)]
        return pltpu.make_async_copy(self.own, place, self.local)

    def start(self):
        for part in range(PARTS):
            for offset in range(1, self.shards.chips):
                self.across(offset, part).start()
            self.beside(0, part).start()
        if self.own is not None:
            self.keep().start()

    def pass_on(self):
        for part in range(PARTS):
            for offset in range(1, self.shards.chips):
                self.across(offset, part).wait_recv()
                self.beside(offset, part).start()

    def arrive(self):
        for part in range(PARTS):
            for offset in range(self.shards.chips):
                self.beside(offset, part).wait_recv()
        if self.own is not None:
            self.keep().wait()

    def finish(self):
        for part in range(PARTS):
            for offset in range(self.shards.chips):
                self.beside(offset, part).wait_send()
                if offset:
                    self.across(offset, part).wait_send()


class ShardReduce:
    def __init__(self, shards, whole, beside_slots, across_slots, work, loads, stores, beside_sems, across_sems):
        self.shards, self.whole = shards, whole
        self.beside_slots, self.across_slots = beside_slots, across_slots
        self.work, self.loads, self.stores = work, loads, stores
        self.beside_sems, self.across_sems = beside_sems, across_sems
        self.rows = whole.shape[0] // shards.count
        self.lanes = pl.ds(0, whole.shape[1])
        self.offsets = [*range(1, shards.chips), 0]

    def block(self, offset, core):
        shard = self.shards.device(self.shards.chip_at(offset), core)
        return self.whole.at[span(shard * self.rows, self.rows)]

    def beside(self, offset):
        return send_to(
            self.shards.sibling,
            self.block(offset, 1 - self.shards.core),
            self.beside_slots.at[offset],
            self.beside_sems.at[0, offset],
            self.beside_sems.at[1, offset],
        )

    def across(self, offset):
        return send_to(
            {"dp": self.shards.device(self.shards.chip_at(offset), self.shards.core)},
            self.beside_slots.at[offset],
            self.across_slots.at[offset - 1],
            self.across_sems.at[0, offset],
            self.across_sems.at[1, offset],
        )

    def fetches(self, offset):
        sources = (self.beside_slots.at[offset], self.block(offset, self.shards.core))
        return [
            pltpu.make_async_copy(source, self.work.at[offset, number, :, self.lanes], self.loads.at[offset, number])
            for number, source in enumerate(sources)
        ]

    def keep(self, offset):
        return pltpu.make_async_copy(
            self.work.at[offset, 0, :, self.lanes], self.beside_slots.at[offset], self.stores.at[offset]
        )

    def start(self):
        for offset in self.offsets:
            self.beside(offset).start()

    def load(self):
        for offset in self.offsets:
            self.beside(offset).wait_recv()
            for fetch in self.fetches(offset):
                fetch.start()

    def add(self):
        for offset in self.offsets:
            for fetch in self.fetches(offset):
                fetch.wait()
            total = self.work[offset, 0, :, self.lanes].astype(full) + self.work[offset, 1, :, self.lanes].astype(full)
            self.work[offset, 0, :, self.lanes] = total.astype(low)
            self.keep(offset).start()

    def stored(self):
        for offset in self.offsets:
            self.keep(offset).wait()

    def cross(self):
        for offset in self.offsets[:-1]:
            self.across(offset).start()

    def pass_on(self):
        self.stored()
        self.cross()

    def arrive(self):
        for offset in self.offsets[:-1]:
            self.across(offset).wait_recv()

    def finish(self):
        for offset in self.offsets:
            self.beside(offset).wait_send()
            if offset:
                self.across(offset).wait_send()


def grouped(refs, size):
    return [refs[number : number + size] for number in range(0, len(refs), size)]


def rope_tables(seq_len):
    half_dim = HD // 2
    steps = np.arange(half_dim, dtype=np.float32) * np.float32(2.0 / HD)
    frequency = np.exp(np.float32(-math.log(10000.0)) * steps)
    angles = np.arange(seq_len, dtype=np.float32)[:, None] * frequency[None, :]
    cos, sin = np.cos(angles), np.sin(angles)
    return (
        np.concatenate([cos, cos], axis=1).astype(np.float32),
        np.concatenate([-sin, sin], axis=1).astype(np.float32),
    )


def turned(values, cos, sin):
    return values * cos + pltpu.roll(values, HD // 2, 1) * sin


def turned_back(values, cos, sin):
    return values * cos - pltpu.roll(values, HD // 2, 1) * sin


def softmax_block(queries, keys, start, length):
    rows, count = queries.shape[0], keys.shape[0]
    scores = dot(queries, keys, 1, 1) * (1.0 / math.sqrt(HD))
    query_pos = start + lax.broadcasted_iota(jnp.int32, (rows, count), 0)
    key_pos = lax.broadcasted_iota(jnp.int32, (rows, count), 1)
    allowed = (key_pos <= query_pos) & (key_pos < length)
    if start + rows > WINDOW:
        allowed = allowed & (query_pos - key_pos < WINDOW)
    scores = jnp.where(allowed, scores, NEGATIVE)
    exponent = jnp.exp(scores - jnp.max(scores, axis=-1, keepdims=True))
    return exponent * (1.0 / jnp.sum(exponent, axis=-1, keepdims=True))


def forward_kernel(count, shard_count, *refs):
    length, tokens, both_gains, cotangent, query_in, key_in, value_in, out_in = refs[:8]
    gate_in, up_in, down_in, cos_in, sin_in = refs[8:13]
    gain_rows, *results = refs[13:20]
    (all_rows, grad_rows, normed_rows, qkv_out, out_out, down_out, act_out, grad_gate_out, grad_up_out, partial) = (
        refs[20:30]
    )
    (all_gains, qkv_w, out_w, gate_w, up_w, down_w, cos, sin, own, attended, normed, grads, hidden, back) = refs[30:44]
    (gain_sems, local, row_loads, stores, weight_stores, swap_sems) = refs[44:50]
    queries, keys, values, grad_own, attended_own, resid, result_sems = refs[50:57]
    gains, acts = refs[57:59]
    result_copies = [
        pltpu.make_async_copy(source, place, result_sems.at[number])
        for number, (source, place) in enumerate(
            zip((queries, keys, values, grad_own, attended_own, resid), results)
        )
    ]
    sems = refs[59:]
    out_sems, row_sems, grad_sems, normed_sems = grouped(sems[:8], 2)
    shard_sems = grouped(sems[8:], 3)

    ring, shards = Ring(count), Shards(shard_count)
    size, model = tokens.shape
    seq_len, width = queries.shape
    units = gate_w.shape[1]
    limit = length[0]
    others = [{"seq": (ring.index + offset) % count} for offset in range(1, count)]
    tables = [pltpu.make_async_copy(cos_in, cos, local.at[0]), pltpu.make_async_copy(sin_in, sin, local.at[1])]
    for table in tables:
        table.start()
    row = lax.broadcasted_iota(jnp.int32, gains.shape, 0)
    both = jnp.where(row == 0, both_gains[0:1, :], both_gains[1:2, :])
    gains[...] = jnp.where(row < 2, both, 0.0).astype(low)
    greet([*others, *shards.others()])

    out_rows, out_width = out_in.shape
    out_mine = out_w.at[span(shards.index * out_rows, out_rows)]
    out_piece = out_rows // PARTS
    out_gather = RingGather(
        ring,
        lambda part: out_in.at[pl.ds(part * out_piece, out_piece)],
        lambda index, part: out_w.at[
            span(shards.index * out_rows + part * out_piece, out_piece), span(index * out_width, out_width)
        ],
        *out_sems,
    )
    out_kept = pltpu.make_async_copy(out_in, out_mine.at[:, span(ring.index * out_width, out_width)], local.at[2])
    out_gather.start()
    out_kept.start()
    gain_copies = [
        send_to(target, gains, all_gains.at[shards.index], gain_sems.at[0, number], gain_sems.at[1, number])
        for number, target in enumerate(shards.others())
    ]
    for copy in gain_copies:
        copy.start()
    qkv_gathers = [
        ShardGather(shards, source, qkv_w.at[:, pl.ds(number * width, width)], *shard_sems[number])
        for number, source in enumerate((query_in, key_in, value_in))
    ]
    out_shards = ShardGather(shards, None, out_w, *shard_sems[3])
    gate_gather, up_gather, down_gather = (
        ShardGather(shards, source, whole, *shard_sems[4 + number])
        for number, (source, whole) in enumerate(((gate_in, gate_w), (up_in, up_w), (down_in, down_w)))
    )
    for gather in qkv_gathers:
        gather.start()

    piece = size // PARTS

    def own_gather(source, whole, pair):
        return RingGather(ring, lambda part: source.at[pl.ds(part * piece, piece)], row_piece(whole, size), *pair)

    def own_kept(source, whole, number):
        return pltpu.make_async_copy(source, whole.at[span(ring.index * size, size)], local.at[number])

    position = ring.index * size + lax.broadcasted_iota(jnp.int32, (size, model), 0)
    grad_own[...] = jnp.where(position < limit, cotangent[...].astype(full), 0.0).astype(low)
    grad_gather = own_gather(grad_own, grad_rows, grad_sems)
    grad_kept = own_kept(grad_own, grad_rows, 4)
    grad_kept.start()
    grad_gather.start()

    rows = tokens[...].astype(full)
    rows = rows * lax.rsqrt(jnp.mean(rows * rows, axis=-1, keepdims=True) + EPSILON)
    all_gains[shards.index] = gains[...]
    for copy in gain_copies:
        copy.wait_recv()
    gain_width = gains.shape[1]
    for shard in range(shard_count):
        gain_rows[:, shard * gain_width : (shard + 1) * gain_width] = all_gains[shard, :8, :].astype(full)
    own[0] = (rows * gain_rows[0:1, :]).astype(low)

    row_gather = own_gather(own.at[0], all_rows, row_sems)
    row_gather.start()
    row_kept = own_kept(own.at[0], all_rows, 3)
    row_kept.start()
    gate_gather.start()

    def owners(step):
        if step in (0, ring.half):
            return [ring.shifted(step)]
        return [ring.shifted(-step), ring.shifted(step)]

    def normed_loads(step, mine, whole):
        return [
            pltpu.make_async_copy(
                mine if step == 0 else whole.at[span(owner * size, size)],
                normed.at[pl.ds(side * size, size)],
                row_loads.at[2, side],
            )
            for side, owner in enumerate(owners(step))
        ]

    def project(step):
        loads = normed_loads(step, own.at[0], all_rows)
        for load in loads:
            load.start()
        for load in loads:
            load.wait()
        linear = dot(normed[pl.ds(0, size * len(loads)), :], qkv_w[...])
        for side, owner in enumerate(owners(step)):
            here = span(owner * size, size)
            side_cos, side_sin = cos[here, :], sin[here, :]
            for number, place in enumerate((queries, keys, values)):
                for head in range(width // HD):
                    lanes = slice(head * HD, (head + 1) * HD)
                    first = number * width + head * HD
                    one = linear[side * size : (side + 1) * size, first : first + HD]
                    if number < 2:
                        one = turned(one, side_cos, side_sin)
                    place[here, lanes] = one.astype(low)

    for step in out_gather.steps():
        step()
    out_kept.wait()
    for gather in qkv_gathers:
        gather.pass_on()
    out_shards.start()
    row_gather.advance(1)
    up_gather.start()
    for table in tables:
        table.wait()
    for gather in qkv_gathers:
        gather.arrive()
    qkv_store = pltpu.make_async_copy(qkv_w, qkv_out, weight_stores.at[0])
    qkv_store.start()
    project(0)
    project(1)
    for step in range(2, ring.half + 1):
        row_gather.advance(step)
        if step == 2:
            gate_gather.pass_on()
        if step == ring.half:
            grad_gather.advance(1)
            down_gather.start()
        project(step)

    for copy in result_copies[:4]:
        copy.start()

    blocks = seq_len // BLOCK

    def swap(head, number):
        other = others[number]
        lanes = pl.ds(head * HD, HD)
        return send_to(
            other,
            attended.at[span(other["seq"] * size, size), lanes],
            attended_own.at[:, span(ring.index * width + head * HD, HD)],
            swap_sems.at[0, head, number],
            swap_sems.at[1, head, number],
        )

    swap_kept = pltpu.make_async_copy(
        attended.at[span(ring.index * size, size)],
        attended_own.at[:, span(ring.index * width, width)],
        local.at[5],
    )
    for head in range(width // HD):
        lanes = slice(head * HD, (head + 1) * HD)
        for number in range(blocks):
            here, upto = pl.ds(number * BLOCK, BLOCK), pl.ds(0, (number + 1) * BLOCK)
            probs = softmax_block(queries[here, lanes], keys[upto, lanes], number * BLOCK, limit)
            attended[here, lanes] = dot(probs.astype(low), values[upto, lanes]).astype(low)
        for number in range(count - 1):
            swap(head, number).start()
    swap_kept.start()
    up_gather.pass_on()
    grad_gather.advance(2)
    out_shards.pass_on()
    out_shards.arrive()
    out_store = pltpu.make_async_copy(out_w, out_out, weight_stores.at[1])
    out_store.start()
    swap_kept.wait()
    for head in range(width // HD):
        for number in range(count - 1):
            swap(head, number).wait_recv()

    def out_project(tile, carry):
        lanes = span(tile * TILE, TILE)
        resid[:, lanes] = tokens[:, lanes].astype(full) + dot(attended_own[...], out_w[lanes, :], 1, 1)
        return carry

    lax.fori_loop(0, model // TILE, out_project, 0)
    rows = resid[...]
    factor = lax.rsqrt(jnp.mean(rows * rows, axis=-1, keepdims=True) + EPSILON)
    own[1] = (rows * factor * gain_rows[1:2, :]).astype(low)
    for copy in result_copies[4:]:
        copy.start()
    normed_gather = own_gather(own.at[1], normed_rows, normed_sems)
    normed_gather.start()
    normed_kept = own_kept(own.at[1], normed_rows, 6)
    normed_kept.start()

    def grad_loads(step):
        return [
            pltpu.make_async_copy(
                grad_own if step == 0 else grad_rows.at[span(owner * size, size)],
                grads.at[step % 2, pl.ds(side * size, size)],
                row_loads.at[step % 2, side],
            )
            for side, owner in enumerate(owners(step))
        ]

    def result_stores(step):
        results = []
        for side, owner in enumerate(owners(step)):
            here, there = pl.ds(side * size, size), span(owner * size, size)
            for number, place in enumerate((act_out, grad_gate_out, grad_up_out)):
                results.append(
                    pltpu.make_async_copy(hidden.at[number, here], place.at[there], stores.at[side, number])
                )
            results.append(pltpu.make_async_copy(back.at[here], partial.at[there], stores.at[side, 3]))
        return results

    def ahead(step):
        return step >= ring.half - 1

    def ahead_rows(step):
        return pl.ds(0 if step < ring.half else 2 * size, size * len(owners(step)))

    def grad_acts(step):
        for load in grad_loads(step):
            load.start()
        for load in grad_loads(step):
            load.wait()
        rows, there = pl.ds(0, size * len(owners(step))), ahead_rows(step)

        def one(tile, carry):
            lanes = span(tile * TILE, TILE)
            acts[there, lanes] = dot(grads[step % 2, rows, :], down_w[:, lanes])
            return carry

        lax.fori_loop(0, units // TILE, one, 0)

    def feed(step):
        loads = normed_loads(step, own.at[1], normed_rows)
        if not ahead(step):
            loads += grad_loads(step)
        for load in loads:
            load.start()
        if step > 0:
            for store in result_stores(step - 1):
                store.wait()
        for load in loads:
            load.wait()
        rows = pl.ds(0, size * len(owners(step)))

        def forward(tile, carry):
            lanes = span(tile * TILE, TILE)
            gate = dot(normed[rows, :], gate_w[:, lanes])
            up = dot(normed[rows, :], up_w[:, lanes])
            if ahead(step):
                grad_act = acts[ahead_rows(step), lanes]
            else:
                grad_act = dot(grads[step % 2, rows, :], down_w[:, lanes])
            sigmoid = 1.0 / (1.0 + jnp.exp(-gate))
            silu = gate * sigmoid
            hidden[0, rows, lanes] = (silu * up).astype(low)
            hidden[1, rows, lanes] = (grad_act * up * sigmoid * (1.0 + gate * (1.0 - sigmoid))).astype(low)
            hidden[2, rows, lanes] = (grad_act * silu).astype(low)
            return carry

        lax.fori_loop(0, units // TILE, forward, 0)

        def backward(tile, carry):
            lanes = span(tile * TILE, TILE)
            total = dot(hidden[1, rows, :], gate_w[lanes, :], 1, 1) + dot(hidden[2, rows, :], up_w[lanes, :], 1, 1)
            back[rows, lanes] = total.astype(low)
            return carry

        lax.fori_loop(0, model // TILE, backward, 0)
        for store in result_stores(step):
            store.start()

    grad_gather.advance(3)
    down_gather.pass_on()
    gate_gather.arrive()
    up_gather.arrive()
    down_gather.arrive()
    down_store = pltpu.make_async_copy(down_w, down_out, weight_stores.at[2])
    down_store.start()
    feed(0)
    for step in range(1, ring.half + 1):
        normed_gather.advance(step)
        if step + 3 <= ring.half:
            grad_gather.advance(step + 3)
        feed(step)
        if step == ring.half - 2:
            grad_acts(step + 1)
            grad_acts(step + 2)
    for store in result_stores(ring.half):
        store.wait()
    for gather in (out_gather, row_gather, grad_gather, normed_gather):
        gather.finish()
    for gather in (*qkv_gathers, out_shards, gate_gather, up_gather, down_gather):
        gather.finish()
    for copy in (row_kept, grad_kept, normed_kept, qkv_store, out_store, down_store, *result_copies):
        copy.wait()
    for copy in gain_copies:
        copy.wait_send()
    for head in range(width // HD):
        for number in range(count - 1):
            swap(head, number).wait_send()


def forward(length, tokens, both_gains, cotangent, weights, tables, collective_id):
    count, shard_count = lax.axis_size("seq"), lax.axis_size("dp")
    size, model = tokens.shape
    seq_len, width, units = size * count, weights[0].shape[1], weights[4].shape[1]
    heads, hidden, rows = shape_of((seq_len, width), low), shape_of((seq_len, units), low), shape_of((size, model), low)
    all_rows = shape_of((seq_len, model), low)
    dma = pltpu.SemaphoreType.DMA
    return pl.pallas_call(
        functools.partial(forward_kernel, count, shard_count),
        out_shape=[
            shape_of((8, model), full),
            heads,
            heads,
            heads,
            rows,
            rows,
            shape_of((size, model), full),
            all_rows,
            all_rows,
            all_rows,
            shape_of((model, 3 * width), low),
            shape_of((model, model), low),
            shape_of((model, units), low),
            hidden,
            hidden,
            hidden,
            all_rows,
        ],
        in_specs=[SMEM] + [VMEM] * 3 + [ANY] * 9,
        out_specs=[VMEM] + [ANY] * 16,
        scratch_shapes=[
            pltpu.VMEM((shard_count, 16, both_gains.shape[1]), low),
            pltpu.VMEM((model, 3 * width), low),
            pltpu.VMEM((model, model), low),
            *[pltpu.VMEM((model, units), low)] * 3,
            *[pltpu.VMEM((seq_len, HD), full)] * 2,
            pltpu.VMEM((2, size, model), low),
            pltpu.VMEM((seq_len, width), low),
            pltpu.VMEM((2 * size, model), low),
            pltpu.VMEM((2, 2 * size, model), low),
            pltpu.VMEM((3, 2 * size, units), low),
            pltpu.VMEM((2 * size, model), low),
            dma((2, shard_count - 1)),
            dma((7,)),
            dma((3, 2)),
            dma((2, 4)),
            dma((3,)),
            dma((2, width // HD, count - 1)),
            *[pltpu.VMEM((seq_len, width), low)] * 3,
            *[pltpu.VMEM((size, model), low)] * 2,
            pltpu.VMEM((size, model), full),
            dma((6,)),
            pltpu.VMEM((16, both_gains.shape[1]), low),
            pltpu.VMEM((3 * size, units), full),
            *ring_semaphores(count) * 4,
            *ShardGather.semaphores(shard_count) * 7,
        ],
        compiler_params=pltpu.CompilerParams(
            collective_id=collective_id, has_side_effects=True, vmem_limit_bytes=VMEM_LIMIT
        ),
        cost_estimate=pl.CostEstimate(flops=0, bytes_accessed=600_000_000, transcendentals=0),
    )(length, tokens, both_gains, cotangent, *weights, *tables)


def ffn_back_kernel(count, shard_count, *refs):
    (partial, normed_rows, grad_rows, act_in, grad_gate_in, grad_up_in, down_in, out_in) = refs[:8]
    resid_in, grad_own_in, gain_rows = refs[8:11]
    gain_sum, resid_out, attn_out, grad_heads, branch, gate_grad, up_grad, down_grad = refs[11:19]
    arrived = grouped(refs[19:23], 2)
    hidden, down_w, out_w, tiles, staged, branch_tile, attended, work = refs[23:31]
    loads, tile_loads, stores, swap_sems, local, work_loads, work_stores = refs[31:38]
    reduce_scratch = refs[38:43]
    resid, grad_own, grad_resid, grad_attn, result_sems = refs[43:48]
    shard_sems = grouped(refs[48:], 2)

    ring, shards = Ring(count), Shards(shard_count)
    size, model = resid.shape
    heads = grad_heads.shape[1]
    others = [{"seq": (ring.index + offset) % count} for offset in range(1, count)]
    inputs = [
        pltpu.make_async_copy(source, place, loads.at[number])
        for number, (source, place) in enumerate(
            (
                (grad_gate_in, hidden.at[1]),
                (grad_up_in, hidden.at[2]),
                (act_in, hidden.at[0]),
                (down_in, down_w),
                (out_in, out_w),
                (resid_in, resid),
                (grad_own_in, grad_own),
            )
        )
    ]
    greet([*others, *shards.greeted()])
    reduce = RingReduce(ring, row_piece(partial, size), *reduce_scratch)
    reduce.start()
    gate, up = (
        ShardReduce(shards, whole, *one, work, work_loads, work_stores, *sems)
        for whole, one, sems in zip((gate_grad, up_grad), arrived, shard_sems)
    )
    count_tiles = model // TILE

    terms = (
        (normed_rows, hidden.at[1], gate_grad, inputs[0]),
        (normed_rows, hidden.at[2], up_grad, inputs[1]),
        (grad_rows, hidden.at[0], down_grad, inputs[2]),
    )
    last = len(terms) * count_tiles - 1

    def fetch(tile):
        lanes = pl.ds(tile % count_tiles * TILE, TILE)
        source = terms[tile // count_tiles][0].at[:, lanes]
        return pltpu.make_async_copy(source, tiles.at[tile % 3], tile_loads.at[tile % 3])

    def store(tile):
        place = terms[tile // count_tiles][2].at[pl.ds(tile % count_tiles * TILE, TILE)]
        return pltpu.make_async_copy(staged.at[tile % 2], place, stores.at[tile % 2, 0])

    def branch_store(tile):
        return pltpu.make_async_copy(
            branch_tile.at[tile % 2], branch.at[:, pl.ds(tile * TILE, TILE)], stores.at[tile % 2, 1]
        )

    later = {0: inputs[1:2], 1: inputs[5:], count_tiles: inputs[2:3], count_tiles + 2: inputs[3:5]}
    for copy in (inputs[0], fetch(0), fetch(1)):
        copy.start()

    def weights(tile):
        for copy in later.get(tile, ()):
            copy.start()
        slot = tile % 2
        _, right, _, ready = terms[tile // count_tiles]
        if tile % count_tiles == 0:
            ready.wait()
        if tile + 2 <= last:
            fetch(tile + 2).start()
        if tile >= 2:
            store(tile - 2).wait()
        fetch(tile).wait()
        staged[slot] = dot(tiles[tile % 3], right[...], 0, 0).astype(low)
        store(tile).start()

    def branches(tile):
        slot = tile % 2
        if tile == 0:
            store(last - 1).wait()
            store(last).wait()
            inputs[3].wait()
        if tile >= 2:
            branch_store(tile - 2).wait()
        branch_tile[slot] = dot(hidden[0], down_w[pl.ds(tile * TILE, TILE), :], 1, 1).astype(low)
        branch_store(tile).start()

    steps = reduce.steps()
    tasks = [functools.partial(weights, tile) for tile in range(last + 1)]
    early = count_tiles // 2
    weave(tasks[:early], [])
    steps[0]()
    weave(tasks[early : count_tiles + 2], [])
    gate.start()
    weave(tasks[count_tiles + 2 : 2 * count_tiles + 2], [gate.load, gate.add, gate.pass_on, lambda: None])
    up.start()
    for step in steps[1:-1]:
        step()
    weave(tasks[2 * count_tiles + 2 :], [up.load, up.add])
    tasks = [functools.partial(branches, tile) for tile in range(count_tiles)]
    weave(tasks, [up.pass_on, steps[-1], lambda: None])
    for copy in inputs[4:]:
        copy.wait()
    gain_total = jnp.zeros((1, model), full)
    swaps = []
    for part in range(PARTS):
        here = pl.ds(part * reduce.size, reduce.size)
        there = grad_heads.at[span(ring.index * size + part * reduce.size, reduce.size)]
        grad_normed, rows = reduce.total(part), resid[here, :]
        factor = lax.rsqrt(jnp.mean(rows * rows, axis=-1, keepdims=True) + EPSILON)
        weighted = grad_normed * gain_rows[1:2, :]
        inner = jnp.mean(weighted * rows, axis=-1, keepdims=True)
        grad = grad_own[here, :].astype(full) + factor * (weighted - rows * (factor * factor * inner))
        grad_resid[here, :] = grad
        grad_attn[here, :] = grad.astype(low)
        gain_total += jnp.sum(grad_normed * rows * factor, axis=0, keepdims=True)
        for number, index in enumerate([other["seq"] for other in others] + [ring.index]):
            lanes = span(index * heads, heads)
            attended[here, lanes] = dot(grad_attn[here, :], out_w[:, lanes]).astype(low)
            source = attended.at[here, lanes]
            if number < count - 1:
                sems = (swap_sems.at[0, part, number], swap_sems.at[1, part, number])
                swap = send_to(others[number], source, there, *sems)
            else:
                swap = pltpu.make_async_copy(source, there, local.at[part])
            swap.start()
            swaps.append(swap)
    gain_sum[...] = jnp.broadcast_to(gain_total, gain_sum.shape)
    results = [
        pltpu.make_async_copy(grad_resid, resid_out, result_sems.at[0]),
        pltpu.make_async_copy(grad_attn, attn_out, result_sems.at[1]),
    ]
    for copy in results:
        copy.start()
    reduce.finish()
    for tile in (count_tiles - 2, count_tiles - 1):
        branch_store(tile).wait()
    for one in (gate, up):
        one.arrive()
        one.finish()
    for copy in (*swaps, *results):
        copy.wait()


def ffn_back(partial, normed_rows, grad_rows, hidden, down_w, out_w, resid, grad_own, gain_rows, heads, collective_id):
    count, shard_count = lax.axis_size("seq"), lax.axis_size("dp")
    size, model = resid.shape
    seq_len, units = hidden[0].shape
    chips, shard_rows = shard_count // CORES, model // shard_count
    grad_w = shape_of((model, units), low)
    dma = pltpu.SemaphoreType.DMA
    return pl.pallas_call(
        functools.partial(ffn_back_kernel, count, shard_count),
        out_shape=[
            shape_of((8, model), full),
            shape_of((size, model), full),
            shape_of((size, model), low),
            shape_of((seq_len, heads), low),
            shape_of((seq_len, model), low),
            grad_w,
            grad_w,
            grad_w,
            *[shape_of((number, shard_rows, units), low) for number in (chips, chips - 1)] * 2,
        ],
        in_specs=[ANY] * 10 + [VMEM],
        out_specs=[VMEM] + [ANY] * 11,
        scratch_shapes=[
            pltpu.VMEM((3, seq_len, units), low),
            pltpu.VMEM(down_w.shape, low),
            pltpu.VMEM(out_w.shape, low),
            pltpu.VMEM((3, seq_len, TILE), low),
            pltpu.VMEM((2, TILE, units), low),
            pltpu.VMEM((2, seq_len, TILE), low),
            pltpu.VMEM((size, model), low),
            pltpu.VMEM((chips, 2, shard_rows, units), low),
            dma((7,)),
            dma((3,)),
            dma((2, 2)),
            dma((2, PARTS, count - 1)),
            dma((PARTS,)),
            dma((chips, 2)),
            dma((chips,)),
            *RingReduce.scratch(count, size, model),
            pltpu.VMEM((size, model), full),
            pltpu.VMEM((size, model), low),
            pltpu.VMEM((size, model), full),
            pltpu.VMEM((size, model), low),
            dma((2,)),
            *[dma((2, chips))] * 4,
        ],
        compiler_params=pltpu.CompilerParams(
            collective_id=collective_id, has_side_effects=True, vmem_limit_bytes=VMEM_LIMIT
        ),
        cost_estimate=pl.CostEstimate(flops=0, bytes_accessed=300_000_000, transcendentals=0),
    )(partial, normed_rows, grad_rows, *hidden, down_w, out_w, resid, grad_own, gain_rows)


def attend_back_kernel(count, shard_count, *refs):
    length, *head_refs, cos_in, sin_in, rows_in, qkv_in, branch = refs[:10]
    *own_refs, gain_rows, gain_ffn_sum, down_grad = refs[10:16]
    output_out, grad_normed, grad_out_w, gain_total, partial, qkv_grad, out_left, out_right = refs[16:24]
    arrived = grouped(refs[24:32], 2)
    cos, sin, weights, grads, sum_k, sum_v, row_tiles, staged, grad_staged, work, out_sum = refs[32:43]
    loads, tile_loads, stores, grad_stores, work_loads, work_stores, out_loads_sem, free_sems = refs[43:51]
    gain_block, gain_shards, gain_part, gain_parts, gain_sems, gain_part_sems = refs[51:57]
    slots, terms, ring_send, ring_recv, term_loads, last_send, last_recv, last_loads = refs[57:65]
    out_scratch = refs[65:70]
    grad_heads, queries, keys, values, resid, grad_attn, attended_own, output = refs[70:78]
    shard_sems = grouped(refs[78:], 2)

    ring, shards = Ring(count), Shards(shard_count)
    seq_len, width = queries.shape
    size, model = resid.shape
    blocks, tiles = seq_len // BLOCK, model // TILE
    scale = 1.0 / math.sqrt(HD)
    limit = length[0]
    others = [{"seq": (ring.index + offset) % count} for offset in range(1, count)]
    inputs = [
        pltpu.make_async_copy(source, place, loads.at[number])
        for number, (source, place) in enumerate(
            (
                (cos_in, cos),
                (sin_in, sin),
                (qkv_in, weights),
                *zip(own_refs, (resid, grad_attn, attended_own)),
                *zip(head_refs, (grad_heads, queries, keys, values)),
            )
        )
    ]
    for load in inputs[4:6]:
        load.start()
    greet([*others, *shards.others()])
    reduce = RingReduce(ring, row_piece(branch, size), slots, terms, ring_send, ring_recv, term_loads)
    last = RingReduce(ring, row_piece(partial, size), slots, terms, last_send, last_recv, last_loads)
    reduce.start()
    shard_reduces = [
        ShardReduce(shards, whole, *one, work, work_loads, work_stores, *sems)
        for whole, one, sems in zip((out_left, out_right, down_grad, qkv_grad), arrived, shard_sems)
    ]
    left, right, down, qkv = shard_reduces

    half = model // 2

    def out_store(tile):
        rows = pl.ds(tile * TILE, TILE)
        return [
            pltpu.make_async_copy(
                staged.at[tile % 2, :, pl.ds(side * half, half)], whole.at[rows], stores.at[tile % 2, side]
            )
            for side, whole in enumerate((out_left, out_right))
        ]

    def out_back(tile):
        if tile >= 2:
            for copy in out_store(tile - 2):
                copy.wait()
        staged[tile % 2] = dot(grad_attn[:, pl.ds(tile * TILE, TILE)], attended_own[...], 0, 0).astype(low)
        for copy in out_store(tile):
            copy.start()

    def out_spread():
        for tile in (tiles - 2, tiles - 1):
            for copy in out_store(tile):
                copy.wait()
        left.start()
        right.start()

    def attend_block(head, number):
        lanes = slice(head * HD, (head + 1) * HD)
        here, upto = pl.ds(number * BLOCK, BLOCK), pl.ds(0, (number + 1) * BLOCK)
        if number == 0:
            sum_k[...] = jnp.zeros_like(sum_k)
            sum_v[...] = jnp.zeros_like(sum_v)
            if head == 0:
                for load in (*inputs[:2], *inputs[6:]):
                    load.wait()
        query_part, grad_part = queries[here, lanes], grad_heads[here, lanes]
        probs = softmax_block(query_part, keys[upto, lanes], number * BLOCK, limit)
        grad_probs = dot(grad_part, values[upto, lanes], 1, 1)
        inner = jnp.sum(probs * grad_probs, axis=-1, keepdims=True)
        grad_scores = (probs * (grad_probs - inner)).astype(low)
        sum_v[upto, :] += dot(probs.astype(low), grad_part, 0, 0)
        sum_k[upto, :] += dot(grad_scores, query_part, 0, 0)
        grad_query = dot(grad_scores, keys[upto, lanes]) * scale
        grads[here, lanes] = turned_back(grad_query, cos[here, :], sin[here, :]).astype(low)
        if number == blocks - 1:
            key_lanes = slice(width + head * HD, width + (head + 1) * HD)
            value_lanes = slice(2 * width + head * HD, 2 * width + (head + 1) * HD)
            grads[:, key_lanes] = turned_back(sum_k[...] * scale, cos[...], sin[...]).astype(low)
            grads[:, value_lanes] = sum_v[...].astype(low)

    def fetch(tile):
        return pltpu.make_async_copy(
            rows_in.at[:, pl.ds(tile * TILE, TILE)], row_tiles.at[tile % 2], tile_loads.at[tile % 2]
        )

    def store(number):
        return pltpu.make_async_copy(
            staged.at[number % 2], partial.at[pl.ds(number * BLOCK, BLOCK)], stores.at[number % 2, 0]
        )

    def grad_store(tile):
        return pltpu.make_async_copy(
            grad_staged.at[tile % 2], qkv_grad.at[pl.ds(tile * TILE, TILE)], grad_stores.at[tile % 2]
        )

    def rows_back(number):
        if number == 0:
            inputs[2].wait()
            fetch(0).start()
        if number >= 2:
            store(number - 2).wait()
        staged[number % 2] = dot(grads[pl.ds(number * BLOCK, BLOCK), :], weights[...], 1, 1).astype(low)
        store(number).start()

    def weights_back(tile):
        if tile + 1 < tiles:
            fetch(tile + 1).start()
        if tile >= 2:
            grad_store(tile - 2).wait()
        fetch(tile).wait()
        grad = dot(row_tiles[tile % 2], grads[...], 0, 0)
        grad_staged[tile % 2] = grad.astype(low)
        grad_store(tile).start()
        lanes = pl.ds(tile * TILE, TILE)
        product = grad * weights[lanes, :].astype(full)
        shared = product[:, :HD]
        for first in range(HD, product.shape[1], HD):
            shared += product[:, first : first + HD]
        gain = lax.dot_general(
            jnp.ones((8, shared.shape[1]), full),
            shared,
            (((1,), (1,)), ((), ())),
            precision=lax.Precision.HIGHEST,
            preferred_element_type=full,
        )
        row = lax.broadcasted_iota(jnp.int32, gain.shape, 0)
        gain_block[:, lanes] = jnp.where(row == 0, gain / gain_rows[0:1, lanes], gain_ffn_sum[:, lanes])

    gain_width = model // shard_count
    gain_copies = [
        send_to(
            other,
            gain_block.at[:, span(other["dp"] * gain_width, gain_width)],
            gain_shards.at[shards.index],
            gain_sems.at[0, number],
            gain_sems.at[1, number],
        )
        for number, other in enumerate(shards.others())
    ]
    gain_part_copies = [
        send_to(
            other, gain_part, gain_parts.at[ring.index], gain_part_sems.at[0, number], gain_part_sems.at[1, number]
        )
        for number, other in enumerate(others)
    ]

    def gains_start():
        for copy in gain_copies:
            copy.start()

    def gains_middle():
        gain_shards[shards.index] = gain_block[:, span(shards.index * gain_width, gain_width)]
        for copy in gain_copies:
            copy.wait_recv()
        gain_part[...] = jnp.sum(gain_shards[...], axis=0)
        for copy in gain_part_copies:
            copy.start()

    def gains_end():
        gain_parts[ring.index] = gain_part[...]
        for copy in gain_part_copies:
            copy.wait_recv()
        gain_total[...] = jnp.sum(gain_parts[...], axis=0)
        for copy in (*gain_copies, *gain_part_copies):
            copy.wait_send()

    def out_loads(side):
        one = shard_reduces[side]
        lanes = pl.ds(side * half, half)
        copies = [pltpu.make_async_copy(one.beside_slots.at[0], out_sum.at[:, lanes], out_loads_sem.at[0])]
        copies += [
            pltpu.make_async_copy(
                one.across_slots.at[offset - 1], work.at[offset, 0, :, one.lanes], out_loads_sem.at[offset]
            )
            for offset in range(1, shards.chips)
        ]
        return copies

    def out_close(side):
        one = shard_reduces[side]
        lanes = pl.ds(side * half, half)
        one.arrive()
        for copy in out_loads(side):
            copy.start()
        for copy in out_loads(side):
            copy.wait()
        total = out_sum[:, lanes].astype(full)
        for offset in range(1, shards.chips):
            total += work[offset, 0, :, one.lanes].astype(full)
        out_sum[:, lanes] = total.astype(low)

    rows, out_width = grad_out_w.shape

    def out_piece(index, part):
        piece = rows // PARTS
        return out_sum.at[pl.ds(part * piece, piece), span(index * out_width, out_width)]

    out_reduce = RingReduce(ring, out_piece, *out_scratch)
    for load in (*inputs[6:], *inputs[:4]):
        load.start()
    for load in inputs[4:6]:
        load.wait()
    steps = reduce.steps()
    for tile in range(tiles):
        out_back(tile)
        if tile == tiles // 2:
            steps[0]()
    out_spread()
    attention = [
        functools.partial(attend_block, head, number) for head in range(width // HD) for number in range(blocks)
    ]
    weave(attention, [left.load, left.add, left.pass_on, right.load, right.add, right.pass_on, *steps[1:-1]])
    down.start()
    projections = [functools.partial(rows_back, number) for number in range(blocks)]
    projections += [functools.partial(weights_back, tile) for tile in range(tiles)]
    weave(projections, [down.load, down.add, down.stored, steps[-1], lambda: None])
    for number in (blocks - 2, blocks - 1):
        store(number).wait()
    for tile in (tiles - 2, tiles - 1):
        grad_store(tile).wait()
    qkv.start()
    gains_start()
    inputs[3].wait()
    for part in range(PARTS):
        here = pl.ds(part * reduce.size, reduce.size)
        position = ring.index * size + part * reduce.size + lax.broadcasted_iota(jnp.int32, (reduce.size, model), 0)
        total = resid[here, :] + reduce.total(part)
        output[here, :] = jnp.where(position < limit, total, 0.0).astype(low)
    output_store = pltpu.make_async_copy(output, output_out, out_loads_sem.at[shards.chips])
    output_store.start()
    reduce.finish()
    reduce.free(free_sems)
    last.wait_free(free_sems)
    last.start()
    for side in range(2):
        out_close(side)
    out_reduce.start()
    down.cross()
    last.advance(1)
    qkv.load()
    qkv.add()
    out_reduce.advance(1)
    qkv.pass_on()
    gains_middle()
    for step in range(2, ring.half):
        last.advance(step)
        out_reduce.advance(step)
    gains_end()
    for part in range(PARTS):
        grad_out_w[pl.ds(part * out_reduce.size, out_reduce.size), :] = out_reduce.total(part)
    for part in range(PARTS):
        grad_normed[pl.ds(part * last.size, last.size), :] = last.total(part)
    for one in (down, qkv):
        one.arrive()
    for one in (*shard_reduces, last, out_reduce):
        one.finish()
    output_store.wait()


def attend_back(
    length, grad_heads, heads, tables, rows, qkv_w, branch, sums, gain_rows, gain_ffn_sum, down_grad, collective_id
):
    count, shard_count = lax.axis_size("seq"), lax.axis_size("dp")
    resid, grad_attn, attended_own = sums
    seq_len, width = grad_heads.shape
    size, model = resid.shape
    chips, shard_rows, units = shard_count // CORES, model // shard_count, down_grad.shape[1]
    half, gain_width = model // 2, model // shard_count
    widths = (half, half, units, 3 * width)
    dma = pltpu.SemaphoreType.DMA
    arrivals = [
        shape_of((number, shard_rows, one), low) for one in widths for number in (chips, max(chips - 1, 1))
    ]
    out_width = model // count
    return pl.pallas_call(
        functools.partial(attend_back_kernel, count, shard_count),
        out_shape=[
            shape_of((size, model), low),
            shape_of((size, model), full),
            shape_of((shard_rows, out_width), full),
            shape_of((8, gain_width), full),
            shape_of((seq_len, model), low),
            shape_of((model, 3 * width), low),
            shape_of((model, half), low),
            shape_of((model, half), low),
            *arrivals,
        ],
        in_specs=[SMEM] + [ANY] * 12 + [VMEM] * 2 + [ANY],
        out_specs=[ANY] + [VMEM] * 3 + [ANY] * (4 + len(arrivals)),
        scratch_shapes=[
            *[pltpu.VMEM((seq_len, HD), full)] * 2,
            pltpu.VMEM((model, 3 * width), low),
            pltpu.VMEM((seq_len, 3 * width), low),
            *[pltpu.VMEM((seq_len, HD), full)] * 2,
            pltpu.VMEM((2, seq_len, TILE), low),
            pltpu.VMEM((2, BLOCK, model), low),
            pltpu.VMEM((2, TILE, 3 * width), low),
            pltpu.VMEM((chips, 2, shard_rows, max(widths)), low),
            pltpu.VMEM((shard_rows, model), low),
            dma((10,)),
            dma((2,)),
            dma((2, 2)),
            dma((2,)),
            dma((chips, 2)),
            dma((chips,)),
            dma((chips + 1,)),
            pltpu.SemaphoreType.REGULAR((2,)),
            pltpu.VMEM((8, model), full),
            pltpu.VMEM((shard_count, 8, gain_width), full),
            pltpu.VMEM((8, gain_width), full),
            pltpu.VMEM((count, 8, gain_width), full),
            dma((2, shard_count - 1)),
            dma((2, count - 1)),
            *RingReduce.scratch(count, size, model),
            *RingReduce.scratch(count, size, model)[2:],
            *RingReduce.scratch(count, shard_rows, out_width),
            *[pltpu.VMEM((seq_len, width), low)] * 4,
            pltpu.VMEM((size, model), full),
            *[pltpu.VMEM((size, model), low)] * 3,
            *[dma((2, chips))] * (2 * len(widths)),
        ],
        compiler_params=pltpu.CompilerParams(
            collective_id=collective_id, has_side_effects=True, vmem_limit_bytes=VMEM_LIMIT
        ),
        cost_estimate=pl.CostEstimate(flops=0, bytes_accessed=500_000_000, transcendentals=0),
    )(length, grad_heads, *heads, *tables, rows, qkv_w, branch, *sums, gain_rows, gain_ffn_sum, down_grad)


def settle_kernel(count_weights, *refs):
    pairs = grouped(refs[: 2 * count_weights], 2)
    grad_normed, tokens, gain_rows, grad_resid, output_in, grad_out_in = refs[2 * count_weights : 2 * count_weights + 6]
    output, grad_tokens, grad_out, *owned = refs[2 * count_weights + 6 :]

    def total(pair):
        beside, across = pair
        return beside[0].astype(full) + jnp.sum(across[...].astype(full), axis=0)

    output[...] = output_in[...]
    grad_out[...] = grad_out_in[...]
    for place, pair in zip(owned, pairs[:-1]):
        place[...] = total(pair)
    qkv = total(pairs[-1])
    for number, place in enumerate(owned[-3:]):
        width = place.shape[1]
        place[...] = qkv[:, number * width : (number + 1) * width]
    values = tokens[...].astype(full)
    factor = lax.rsqrt(jnp.mean(values * values, axis=-1, keepdims=True) + EPSILON)
    weighted = grad_normed[...] * gain_rows[0:1, :]
    inner = jnp.mean(weighted * values, axis=-1, keepdims=True)
    grad_tokens[...] = grad_resid[...] + factor * (weighted - values * (factor * factor * inner))


def settle(pairs, grad_normed, tokens, gain_rows, grad_resid, output, grad_out, width):
    steps = 4
    size, model = tokens.shape
    rows = grad_out.shape[0]

    def cut(array):
        return pl.BlockSpec((array.shape[0] // steps, array.shape[1]), lambda step: (step, 0))

    def whole(array):
        return pl.BlockSpec(array.shape, lambda step: (0, 0))

    pair_specs = []
    for beside, across in pairs:
        pair_specs.append(pl.BlockSpec((1, rows // steps, beside.shape[2]), lambda step: (0, step, 0)))
        pair_specs.append(
            pl.BlockSpec((across.shape[0], rows // steps, across.shape[2]), lambda step: (0, step, 0))
        )
    outs = [
        shape_of((size, model), low),
        shape_of((size, model), full),
        shape_of(grad_out.shape, full),
        *[shape_of((rows, beside.shape[2]), full) for beside, _ in pairs[:-1]],
        *[shape_of((rows, width), full)] * 3,
    ]
    return pl.pallas_call(
        functools.partial(settle_kernel, len(pairs)),
        grid=(steps,),
        out_shape=outs,
        in_specs=[
            *pair_specs,
            cut(grad_normed),
            cut(tokens),
            whole(gain_rows),
            cut(grad_resid),
            cut(output),
            cut(grad_out),
        ],
        out_specs=[cut(out) for out in outs],
        compiler_params=pltpu.CompilerParams(vmem_limit_bytes=VMEM_LIMIT),
    )(
        *[one for pair in pairs for one in pair],
        grad_normed,
        tokens,
        gain_rows,
        grad_resid,
        output,
        grad_out,
    )


def body(
    tokens,
    lengths,
    cotangent,
    w_query,
    w_key,
    w_value,
    w_out,
    w_gate,
    w_up,
    w_down,
    gain_attn,
    gain_ffn,
):
    seq_len = tokens.shape[0] * lax.axis_size("seq")
    head_width = w_query.shape[1]
    tables = rope_tables(seq_len)
    both_gains = jnp.stack([gain_attn, gain_ffn]).astype(jnp.float32)
    (
        gain_rows,
        queries,
        keys,
        values,
        grad_ffn,
        attended_tok,
        resid,
        full1,
        grad_full,
        full2,
        qkv_w,
        out_full,
        down_w,
        activation,
        grad_gate,
        grad_up,
        partial2,
    ) = forward(
        lengths, tokens, both_gains, cotangent, (w_query, w_key, w_value, w_out, w_gate, w_up, w_down), tables, 1
    )
    gain_ffn_sum, grad_resid, grad_attn, grad_heads, branch, _, _, grad_w_down, *gate_up = ffn_back(
        partial2,
        full2,
        grad_full,
        (activation, grad_gate, grad_up),
        down_w,
        out_full,
        resid,
        grad_ffn,
        gain_rows,
        head_width,
        2,
    )
    output, grad_normed1, owned_out, gain_sums, _, _, _, _, *arrived = attend_back(
        lengths,
        grad_heads,
        (queries, keys, values),
        tables,
        full1,
        qkv_w,
        branch,
        (resid, grad_attn, attended_tok),
        gain_rows,
        gain_ffn_sum,
        grad_w_down,
        3,
    )
    output, grad_tokens, owned_out, owned_gate, owned_up, owned_down, owned_query, owned_key, owned_value = settle(
        grouped([*gate_up, *arrived[4:]], 2), grad_normed1, tokens, gain_rows, grad_resid, output, owned_out, head_width
    )
    piece = gain_sums.shape[1] // lax.axis_size("seq")
    owned_gains = lax.dynamic_slice_in_dim(gain_sums, lax.axis_index("seq") * piece, piece, axis=1)
    owned_gain_attn, owned_gain_ffn = owned_gains[0], owned_gains[1]
    return (
        output,
        grad_tokens,
        owned_query,
        owned_key,
        owned_value,
        owned_out,
        owned_gate,
        owned_up,
        owned_down,
        owned_gain_attn,
        owned_gain_ffn,
    )


def solution(mesh):
    rows, shard = P(("dp", "seq"), None), P("dp", "seq")
    gains = P(("dp", "seq"))
    return jax.shard_map(
        body,
        mesh=mesh,
        in_specs=(rows, P("dp"), rows, *[shard] * 7, P("dp"), P("dp")),
        out_specs=(rows, rows, *[shard] * 7, gains, gains),
        check_vma=False,
    )
```
